32 devices in a mesh: dp: 8 (over y, x, core), mp: 4 (over z).
Axes of the slice: x: 2, y: 2, z: 4, core: 2. Of those that a mesh axis runs over, the one named last changes fastest.
Arguments:
- tokens: bfloat16 [32, 1024, 512], P('dp', 'mp'), may hold values from -6 to 6
- segment_ids: int32 [32, 1024], P('dp', 'mp'), may hold values from 0 to 3, as said below
- block_mask: int32 [32, 16, 16], P('dp'), may hold values from 0 to 1, as said below
- gain_one: float32 [512], replicated, may hold values from 0.1 to 1.9
- shift_one: float32 [512], replicated, may hold values from -3 to 3
- w_qkv: bfloat16 [512, 1536], replicated, may hold values from -0.25 to 0.25
- w_out: bfloat16 [512, 512], replicated, may hold values from -0.75 to 0.75
- out_bias: float32 [512], replicated, may hold values from -3 to 3
- sort_query: bfloat16 [512, 512], replicated, may hold values from -2 to 2
- sort_key: bfloat16 [512, 512], replicated, may hold values from -2 to 2
- gain_two: float32 [512], replicated, may hold values from 0.1 to 1.9
- shift_two: float32 [512], replicated, may hold values from -3 to 3
- input_weight: bfloat16 [512, 2048], P(None, 'mp'), may hold values from -0.25 to 0.25
- in_bias: bfloat16 [2048], P('mp'), may hold values from -3 to 3
- output_weight: bfloat16 [2048, 512], P('mp'), may hold values from -0.25 to 0.25
- back_bias: float32 [512], replicated, may hold values from -3 to 3
- cotangent: bfloat16 [32, 1024, 512], P('dp', 'mp'), may hold values from -6 to 6
Outputs:
- layer_out: float32 [32, 1024, 512], P('dp', 'mp')
- grad_tokens: float32 [32, 1024, 512], P('dp', 'mp')
- grad_gain_one: float32 [512], replicated
- grad_shift_one: float32 [512], replicated
- grad_qkv: float32 [512, 1536], replicated
- grad_w_out: float32 [512, 512], replicated
- grad_out_bias: float32 [512], replicated
- grad_sort_query: float32 [512, 512], replicated
- grad_sort_key: float32 [512, 512], replicated
- grad_gain_two: float32 [512], replicated
- grad_shift_two: float32 [512], replicated
- grad_w_in: float32 [512, 2048], P(None, 'mp')
- grad_in_bias: float32 [2048], P('mp')
- grad_w_back: float32 [2048, 512], P('mp')
- grad_back_bias: float32 [512], replicated
The draws below stay inside these ranges and needn't reach their ends.
Inputs may be any that keep to these rules, and one draw needn't show every extreme that they name: `segment_ids`: ids of one sequence start at 0, never fall and rise by at most one from position to position; each sequence holds 4 documents of 1 to 512 positions, one of exactly 512. `block_mask`: 1 exactly where blocks i and j of the sequence hold a common document id.
All inputs are finite; a program needn't handle non-finite values.
Results may differ from the reference program's by a relative error of at most 0.015.
The reference program's roundings to bfloat16 on the way count: a program that leaves them out, or rounds other values in their place, can miss the bound.
Values may be sent and summed in bfloat16 or wider, within the bound.
A program may use at most 640 MiB of HBM per device.

```python
import jax
import jax.numpy as jnp
from jax import lax

D = 512
HEADS = 8
FF = 2048
HEAD = 64
BLOCK = 64
ITERS = 8
LENGTH = 1024
NB = 16
DOCS = 4
LARGEST_DOC = 512
SEQ_ROWS = 32


def layout_row(row_key):
    doc_count = DOCS
    largest = LARGEST_DOC
    remain = LENGTH - largest
    place_key, cut_key = jax.random.split(row_key)
    big_index = jax.random.randint(place_key, (), 0, doc_count)
    order = jax.random.permutation(cut_key, remain - 1) + 1
    cuts = jnp.sort(order[:doc_count - 2])
    edges = jnp.concatenate([jnp.zeros((1,), jnp.int32), cuts.astype(jnp.int32), jnp.full((1,), remain, jnp.int32)])
    smaller = edges[1:] - edges[:-1]
    index = jnp.arange(doc_count)
    after_pad = jnp.concatenate([smaller, jnp.zeros((1,), jnp.int32)])
    before_pad = jnp.concatenate([jnp.zeros((1,), jnp.int32), smaller])
    sizes_all = jnp.where(index < big_index, after_pad, jnp.where(index == big_index, largest, before_pad))
    starts = jnp.cumsum(sizes_all) - sizes_all
    positions = jnp.arange(LENGTH)
    return jnp.sum((positions[:, None] >= starts[None, 1:]).astype(jnp.int32), axis=1).astype(jnp.int32)


def segment_layout(key):
    row_keys = jax.random.split(key, SEQ_ROWS)
    return jax.vmap(layout_row)(row_keys)


def draw_segment_ids(key, part):
    return segment_layout(key)


def draw_block_mask(key, part):
    doc_ids = segment_layout(key).reshape(SEQ_ROWS, NB, BLOCK)
    first_id = doc_ids[:, :, 0]
    last_id = doc_ids[:, :, BLOCK - 1]
    common = (first_id[:, :, None] <= last_id[:, None, :]) & (first_id[:, None, :] <= last_id[:, :, None])
    return common.astype(jnp.int32)


def steps_of(own_key, extent, shards, low, high):
    loudness = 1.0
    for axis_at, blocks in shards:
        heights = jax.random.uniform(jax.random.fold_in(jax.random.fold_in(own_key, 6), axis_at), (blocks,), jnp.float32, low / len(shards), high / len(shards))
        loudness = loudness * jnp.repeat(jnp.exp(heights), extent[axis_at] // blocks).reshape((-1,) + (1,) * (len(extent) - 1 - axis_at))
    return loudness


def gaussian(own_key, shape, scale, reach, cuts=(), held_as=jnp.bfloat16):
    array = jax.random.normal(own_key, shape, jnp.float32) * scale
    if len(cuts) > 0:
        array = steps_of(own_key, shape, cuts, -0.22, 0.18) * array
    return jnp.clip(array, min=-reach, max=reach).astype(held_as)


def setup_inputs(seed: int = 0) -> dict:
    keys = jax.random.split(jax.random.key(seed), 18)
    return {
        "tokens": gaussian(keys[0], (SEQ_ROWS, LENGTH, D), 1.0, 6.0, ((0, 8), (1, 4))),
        "segment_ids": draw_segment_ids(jax.random.fold_in(keys[17], 71), 0),
        "block_mask": draw_block_mask(jax.random.fold_in(keys[17], 71), 0),
        "gain_one": jnp.clip(1.0 + 0.18 * jax.random.normal(keys[3], (D,), jnp.float32), 0.1, 1.9),
        "shift_one": gaussian(keys[4], (D,), 0.5, 3.0, (), jnp.float32),
        "w_qkv": gaussian(keys[5], (D, 3 * D), D ** -0.5, 0.25),
        "w_out": gaussian(keys[6], (D, D), (D // 8) ** -0.5, 0.75),
        "out_bias": gaussian(keys[7], (D,), 0.5, 3.0, (), jnp.float32),
        "sort_query": gaussian(keys[8], (D, D), (D // BLOCK) ** -0.5, 2.0),
        "sort_key": gaussian(keys[9], (D, D), (D // BLOCK) ** -0.5, 2.0),
        "gain_two": jnp.clip(1.0 + 0.18 * jax.random.normal(keys[10], (D,), jnp.float32), 0.1, 1.9),
        "shift_two": gaussian(keys[11], (D,), 0.5, 3.0, (), jnp.float32),
        "input_weight": gaussian(keys[12], (D, FF), D ** -0.5, 0.25, ((1, 4),)),
        "in_bias": gaussian(keys[13], (FF,), 0.5, 3.0, ((0, 4),)),
        "output_weight": gaussian(keys[14], (FF, D), (FF // 4) ** -0.5, 0.25, ((0, 4),)),
        "back_bias": gaussian(keys[15], (D,), 0.5, 3.0, (), jnp.float32),
        "cotangent": gaussian(keys[16], (SEQ_ROWS, LENGTH, D), 1.0, 6.0, ((0, 8), (1, 4))),
    }


TEMPER = 0.75
EPSILON = 1e-05
HIGH = lax.Precision.HIGHEST

@jax.custom_vjp
def low(v):
    return lax.optimization_barrier(v.astype(jnp.bfloat16)).astype(jnp.float32)

@jax.custom_vjp
def low_back(v):
    return v

def low_keep(v):
    return (low(v), None)

def low_pass(kept, grad):
    return (grad,)

def back_keep(v):
    return (v, None)

def back_low(kept, grad):
    return (low(grad),)
low.defvjp(low_keep, low_pass)
low_back.defvjp(back_keep, back_low)

def round_both(value_in):
    return low(low_back(value_in))

def layer_norm(source, gain_vec, shift_vec):
    centred = source - lax.optimization_barrier(jnp.mean(source, axis=-1, keepdims=True))
    inverse = lax.rsqrt(lax.optimization_barrier(jnp.mean(centred * centred, axis=-1, keepdims=True)) + EPSILON)
    return centred * inverse * gain_vec + shift_vec

def transport(sort_q, sort_k, allowed):
    logits = jnp.einsum('ihe,jhe->hij', sort_q, sort_k, precision=HIGH) * HEAD ** (-0.5)
    log_plan = jnp.where(allowed[None], logits / TEMPER, -1000000000.0)
    for sweep_index in range(ITERS):
        log_plan = log_plan - jax.nn.logsumexp(log_plan, axis=-1, keepdims=True)
        log_plan = log_plan - jax.nn.logsumexp(log_plan, axis=-2, keepdims=True)
    return jnp.exp(log_plan)

def forward(source, params, segment, allowed):
    gain_one, shift_one, w_qkv, w_out, out_bias, sort_query, sort_key, gain_two, shift_two, input_weight, in_bias, output_weight, back_bias = params
    blocks = LENGTH // BLOCK
    scale_factor = HEAD ** (-0.5)
    normed_one = layer_norm(source, gain_one, shift_one)
    mixed_rows = round_both(jnp.dot(low(normed_one), w_qkv, precision=HIGH))
    mixed_rows = mixed_rows.reshape(blocks, BLOCK, 3, HEADS, HEAD)
    queries = mixed_rows[:, :, 0]
    key_rows = mixed_rows[:, :, 1]
    value_rows = mixed_rows[:, :, 2]
    summary = low(lax.optimization_barrier(jnp.mean(normed_one.reshape(blocks, BLOCK, D), axis=1)))
    sort_q = jnp.dot(summary, sort_query, precision=HIGH).reshape(blocks, HEADS, HEAD)
    sort_k = jnp.dot(summary, sort_key, precision=HIGH).reshape(blocks, HEADS, HEAD)
    plan = low(transport(sort_q, sort_k, allowed))
    sorted_keys = round_both(jnp.einsum('hij,jbhe->ibhe', plan, key_rows, precision=HIGH))
    sorted_values = round_both(jnp.einsum('hij,jbhe->ibhe', plan, value_rows, precision=HIGH))
    key_cat = jnp.concatenate([sorted_keys, key_rows], axis=1)
    value_cat = jnp.concatenate([sorted_values, value_rows], axis=1)
    scores = low_back(jnp.einsum('ibhe,ikhe->ihbk', queries, key_cat, precision=HIGH) * scale_factor)
    segment_blocks = segment.reshape(blocks, BLOCK)
    same_doc = segment_blocks[:, :, None] == segment_blocks[:, None, :]
    keep_mask = jnp.concatenate([jnp.ones_like(same_doc), same_doc], axis=-1)[:, None]
    scores = jnp.where(keep_mask, scores, -1000000000.0)
    weights_soft = jax.nn.softmax(scores, axis=-1)
    attended = jnp.einsum('ihbk,ikhe->ibhe', low(weights_soft), value_cat, precision=HIGH)
    attended = round_both(attended.reshape(LENGTH, D))
    hidden = source + low_back(jnp.dot(attended, w_out, precision=HIGH)) + out_bias
    normed_two = low(layer_norm(hidden, gain_two, shift_two))
    pre_act = low_back(jnp.dot(normed_two, input_weight, precision=HIGH)) + in_bias
    activated_hidden = low(jax.nn.gelu(pre_act, approximate=False))
    return hidden + low_back(jnp.dot(activated_hidden, output_weight, precision=HIGH)) + back_bias

def reference(tokens, segment_ids, block_mask, gain_one, shift_one, w_qkv, w_out, out_bias, sort_query, sort_key, gain_two, shift_two, input_weight, in_bias, output_weight, back_bias, cotangent):
    params = tuple((weight_item.astype(jnp.float32) for weight_item in (gain_one, shift_one, w_qkv, w_out, out_bias, sort_query, sort_key, gain_two, shift_two, input_weight, in_bias, output_weight, back_bias)))
    blocks = LENGTH // BLOCK
    diagonal = jnp.arange(blocks)[:, None] == jnp.arange(blocks)[None, :]

    def per_sequence(totals, inputs):
        row_tokens, row_segment, row_mask, row_cot = inputs
        allowed = (row_mask == 1) | diagonal

        def apply_layer(source, weights):
            return forward(source, weights, row_segment, allowed)
        result, pullback = jax.vjp(apply_layer, row_tokens.astype(jnp.float32), params)
        grad_source, grad_params = pullback(row_cot.astype(jnp.float32))
        totals = jax.tree.map(lambda running, update: running + update, totals, grad_params)
        return (totals, (result, grad_source))
    zeros = jax.tree.map(jnp.zeros_like, params)
    totals, (outputs, grad_tokens) = lax.scan(per_sequence, zeros, (tokens, segment_ids, block_mask, cotangent))
    return (outputs, grad_tokens) + tuple(totals)
```

```python
from functools import partial

import jax
import jax.numpy as jnp
from jax import lax
from jax.sharding import PartitionSpec as P

HEADS = 8
BLOCK = 64
ITERS = 8


TEMPER = 0.75
EPSILON = 1e-05
HIGH = lax.Precision.HIGHEST


def norm_stats(source):
    centred = source - jnp.mean(source, axis=-1, keepdims=True)
    inverse = lax.rsqrt(jnp.mean(centred * centred, axis=-1, keepdims=True) + EPSILON)
    return (centred * inverse, inverse)


def norm_back(grad_out, unit_rows, inverse, gain_vec):
    scaled = grad_out * gain_vec
    first_mean = jnp.mean(scaled, axis=-1, keepdims=True)
    second_mean = jnp.mean(scaled * unit_rows, axis=-1, keepdims=True)
    return inverse * (scaled - first_mean - unit_rows * second_mean)


def exact_gelu(pre_act):
    return jax.nn.gelu(pre_act, approximate=False)


def transport_plan(sort_q, sort_k, allowed):
    seq_count, blocks, model_width = sort_q.shape
    head_size = model_width // HEADS
    query_heads = sort_q.reshape(seq_count, blocks, HEADS, head_size)
    key_heads = sort_k.reshape(seq_count, blocks, HEADS, head_size)
    logits = jnp.einsum("sihe,sjhe->shij", query_heads, key_heads, precision=HIGH) * head_size ** (
        -0.5
    )
    log_plan = jnp.where(allowed[:, None], logits / TEMPER, -1000000000.0)
    for sweep_index in range(ITERS):
        log_plan = log_plan - jax.nn.logsumexp(log_plan, axis=-1, keepdims=True)
        log_plan = log_plan - jax.nn.logsumexp(log_plan, axis=-2, keepdims=True)
    return jnp.exp(log_plan)


def per_device(
    tokens,
    segment_ids,
    block_mask,
    gain_one,
    shift_one,
    w_qkv,
    w_out,
    out_bias,
    sort_query,
    sort_key,
    gain_two,
    shift_two,
    input_weight,
    in_bias,
    output_weight,
    back_bias,
    cotangent,
):
    seq_count, shard_len, model_width = tokens.shape
    head_size = model_width // HEADS
    local_blocks = shard_len // BLOCK
    all_blocks = block_mask.shape[1]
    first_block = lax.axis_index("mp") * local_blocks
    scale_factor = head_size ** (-0.5)
    token_rows = seq_count * shard_len
    pair_shape = (seq_count, local_blocks, BLOCK, 2, HEADS, head_size)
    source = tokens.astype(jnp.float32)
    unit_one, inverse_one = norm_stats(source)
    normed_one = unit_one * gain_one + shift_one
    normed_low = normed_one.astype(jnp.bfloat16).reshape(token_rows, model_width)
    mixed_rows = jnp.dot(normed_low, w_qkv, preferred_element_type=jnp.float32).astype(jnp.bfloat16)
    mixed_rows = mixed_rows.reshape(seq_count, local_blocks, BLOCK, 3, HEADS, head_size)
    queries = mixed_rows[:, :, :, 0]
    key_value = mixed_rows[:, :, :, 1:]
    pair_flat = key_value.reshape(seq_count, local_blocks, BLOCK, 2 * model_width)
    summary_low = jnp.mean(
        normed_one.reshape(seq_count, local_blocks, BLOCK, model_width), axis=2
    ).astype(jnp.bfloat16)
    summary_all = lax.all_gather(summary_low, "mp", axis=1, tiled=True)
    sort_q = jnp.dot(summary_all, sort_query, preferred_element_type=jnp.float32)
    sort_k = jnp.dot(summary_all, sort_key, preferred_element_type=jnp.float32)
    diagonal = jnp.arange(all_blocks)[:, None] == jnp.arange(all_blocks)[None, :]
    allowed = (block_mask == 1) | diagonal[None]
    plan_full, plan_back = jax.vjp(partial(transport_plan, allowed=allowed), sort_q, sort_k)
    plan_local = lax.dynamic_slice_in_dim(plan_full, first_block, local_blocks, 2).astype(
        jnp.bfloat16
    )
    pair_all = lax.all_gather(pair_flat, "mp", axis=1, tiled=True).reshape(
        seq_count, all_blocks, BLOCK, 2, HEADS, head_size
    )
    sorted_pair = jnp.einsum(
        "shij,sjbchd->sibchd", plan_local, pair_all, preferred_element_type=jnp.float32
    )
    sorted_low = sorted_pair.astype(jnp.bfloat16)
    key_cat = jnp.concatenate([sorted_low[:, :, :, 0], key_value[:, :, :, 0]], axis=2)
    value_cat = jnp.concatenate([sorted_low[:, :, :, 1], key_value[:, :, :, 1]], axis=2)
    segment_blocks = segment_ids.reshape(seq_count, local_blocks, BLOCK)
    same_doc = segment_blocks[:, :, :, None] == segment_blocks[:, :, None, :]
    keep_mask = jnp.concatenate([jnp.ones_like(same_doc), same_doc], axis=-1)[:, :, None]
    raw_scores = (
        jnp.einsum("sibhd,sikhd->sihbk", queries, key_cat, preferred_element_type=jnp.float32)
        * scale_factor
    )
    scores = jnp.where(keep_mask, raw_scores, -1000000000.0)
    weights_soft = jax.nn.softmax(scores, axis=-1)
    weights_low = weights_soft.astype(jnp.bfloat16)
    attended = jnp.einsum(
        "sihbk,sikhd->sibhd", weights_low, value_cat, preferred_element_type=jnp.float32
    )
    attended_low = attended.astype(jnp.bfloat16).reshape(token_rows, model_width)
    projected = jnp.dot(attended_low, w_out, preferred_element_type=jnp.float32) + out_bias
    hidden = source + projected.reshape(seq_count, shard_len, model_width)
    unit_two, inverse_two = norm_stats(hidden)
    normed_two = (unit_two * gain_two + shift_two).astype(jnp.bfloat16)
    cot_float = cotangent.astype(jnp.float32)
    gathered_rows = lax.all_gather(normed_two, "mp", axis=1, tiled=True)
    pre_act = jnp.dot(
        gathered_rows, input_weight, preferred_element_type=jnp.float32
    ) + in_bias.astype(jnp.float32)
    active_float, gelu_back = jax.vjp(exact_gelu, pre_act)
    activated_hidden = active_float.astype(jnp.bfloat16)
    partial_out = jnp.dot(activated_hidden, output_weight, preferred_element_type=jnp.float32)
    ffn_out = lax.psum_scatter(
        partial_out.astype(jnp.bfloat16), "mp", scatter_dimension=1, tiled=True
    ).astype(jnp.float32)
    cotangent_gathered = lax.all_gather(cotangent, "mp", axis=1, tiled=True)
    grad_activated_hidden = jnp.einsum(
        "mci,ni->mcn", cotangent_gathered, output_weight, preferred_element_type=jnp.float32
    )
    grad_pre = gelu_back(grad_activated_hidden)[0]
    grad_preactivation_rounded = grad_pre.astype(jnp.bfloat16)
    local_w_in = jnp.einsum(
        "rjy,rjq->yq", gathered_rows, grad_preactivation_rounded, preferred_element_type=jnp.float32
    )
    local_in_bias = jnp.sum(grad_pre, axis=(0, 1))
    local_output_weight = jnp.einsum(
        "wko,wkp->op", activated_hidden, cotangent_gathered, preferred_element_type=jnp.float32
    )
    grad_normed_two = lax.psum_scatter(
        jnp.einsum(
            "giv,cv->gic",
            grad_preactivation_rounded,
            input_weight,
            preferred_element_type=jnp.float32,
        ),
        "mp",
        scatter_dimension=1,
        tiled=True,
    )
    grad_w_in, grad_in_bias, grad_w_back = (
        lax.psum(local_w_in.astype(jnp.bfloat16), "dp").astype(jnp.float32),
        lax.psum(local_in_bias.astype(jnp.bfloat16), "dp").astype(jnp.float32),
        lax.psum(local_output_weight.astype(jnp.bfloat16), "dp").astype(jnp.float32),
    )
    layer_out = hidden + ffn_out + back_bias
    grad_hidden = cot_float + norm_back(grad_normed_two, unit_two, inverse_two, gain_two)
    grad_gain_two = jnp.sum(grad_normed_two * unit_two, axis=(0, 1))
    grad_shift_two = jnp.sum(grad_normed_two, axis=(0, 1))
    grad_back_bias = jnp.sum(cot_float, axis=(0, 1))
    grad_out_bias = jnp.sum(grad_hidden, axis=(0, 1))
    grad_proj_low = grad_hidden.astype(jnp.bfloat16).reshape(token_rows, model_width)
    grad_w_out = jnp.einsum(
        "td,te->de", attended_low, grad_proj_low, preferred_element_type=jnp.float32
    )
    grad_attended = jnp.einsum(
        "te,de->td", grad_proj_low, w_out, preferred_element_type=jnp.float32
    )
    grad_attended = grad_attended.astype(jnp.bfloat16).reshape(
        seq_count, local_blocks, BLOCK, HEADS, head_size
    )
    grad_weights = jnp.einsum(
        "sibhd,sikhd->sihbk", grad_attended, value_cat, preferred_element_type=jnp.float32
    )
    grad_value_cat = jnp.einsum(
        "sihbk,sibhd->sikhd", weights_low, grad_attended, preferred_element_type=jnp.float32
    )
    grad_scores = weights_soft * (
        grad_weights - jnp.sum(grad_weights * weights_soft, axis=-1, keepdims=True)
    )
    grad_scores_low = grad_scores.astype(jnp.bfloat16)
    grad_queries = (
        jnp.einsum(
            "sihbk,sikhd->sibhd", grad_scores_low, key_cat, preferred_element_type=jnp.float32
        )
        * scale_factor
    )
    grad_key_cat = (
        jnp.einsum(
            "sihbk,sibhd->sikhd", grad_scores_low, queries, preferred_element_type=jnp.float32
        )
        * scale_factor
    )
    grad_sorted = jnp.stack(
        [grad_key_cat[:, :, :BLOCK], grad_value_cat[:, :, :BLOCK]], axis=3
    ).astype(jnp.bfloat16)
    grad_pair_own = jnp.stack([grad_key_cat[:, :, BLOCK:], grad_value_cat[:, :, BLOCK:]], axis=3)
    grad_plan = jnp.einsum(
        "sibchd,sjbchd->shij", grad_sorted, pair_all, preferred_element_type=jnp.float32
    )
    term = jnp.einsum(
        "shij,sibchd->jsbchd", plan_local, grad_sorted, preferred_element_type=jnp.float32
    )
    from_sorted = lax.psum_scatter(
        term.reshape(local_blocks * lax.axis_size("mp"), seq_count, BLOCK, 2 * model_width).astype(
            jnp.bfloat16
        ),
        "mp",
        scatter_dimension=0,
        tiled=True,
    ).astype(jnp.float32)
    from_sorted = jnp.moveaxis(from_sorted, 0, 1).reshape(pair_shape)
    grad_pair = grad_pair_own + from_sorted
    grad_mixed = jnp.concatenate([grad_queries[:, :, :, None], grad_pair], axis=3)
    grad_mixed_low = grad_mixed.astype(jnp.bfloat16).reshape(token_rows, 3 * model_width)
    grad_qkv = jnp.einsum(
        "td,te->de", normed_low, grad_mixed_low, preferred_element_type=jnp.float32
    )
    grad_plan_all = lax.all_gather(grad_plan.astype(jnp.bfloat16), "mp", axis=2, tiled=True).astype(
        grad_plan.dtype
    )
    grad_sq_all, grad_sk_all = plan_back(grad_plan_all)
    grad_sq = lax.dynamic_slice_in_dim(grad_sq_all, first_block, local_blocks, 1)
    grad_sk = lax.dynamic_slice_in_dim(grad_sk_all, first_block, local_blocks, 1)
    summary_float = summary_low.astype(jnp.float32)
    grad_sort_query = jnp.einsum("sid,sie->de", summary_float, grad_sq, precision=HIGH)
    grad_sort_key = jnp.einsum("sid,sie->de", summary_float, grad_sk, precision=HIGH)
    grad_summary = jnp.einsum(
        "sie,de->sid", grad_sq, sort_query.astype(jnp.float32), precision=HIGH
    ) + jnp.einsum("sie,de->sid", grad_sk, sort_key.astype(jnp.float32), precision=HIGH)
    spread_summary = jnp.broadcast_to(
        (grad_summary / BLOCK)[:, :, None, :], (seq_count, local_blocks, BLOCK, model_width)
    ).reshape(seq_count, shard_len, model_width)
    grad_normed_one = jnp.einsum(
        "te,de->td", grad_mixed_low, w_qkv, preferred_element_type=jnp.float32
    )
    grad_normed_one = grad_normed_one.reshape(seq_count, shard_len, model_width) + spread_summary
    grad_gain_one = jnp.sum(grad_normed_one * unit_one, axis=(0, 1))
    grad_shift_one = jnp.sum(grad_normed_one, axis=(0, 1))
    grad_tokens = grad_hidden + norm_back(grad_normed_one, unit_one, inverse_one, gain_one)
    (
        grad_gain_one,
        grad_shift_one,
        grad_qkv,
        grad_w_out,
        grad_out_bias,
        grad_sort_query,
        grad_sort_key,
        grad_gain_two,
        grad_shift_two,
        grad_back_bias,
    ) = lax.psum(
        (
            grad_gain_one,
            grad_shift_one,
            grad_qkv,
            grad_w_out,
            grad_out_bias,
            grad_sort_query,
            grad_sort_key,
            grad_gain_two,
            grad_shift_two,
            grad_back_bias,
        ),
        ("dp", "mp"),
    )
    return (
        layer_out,
        grad_tokens,
        grad_gain_one,
        grad_shift_one,
        grad_qkv,
        grad_w_out,
        grad_out_bias,
        grad_sort_query,
        grad_sort_key,
        grad_gain_two,
        grad_shift_two,
        grad_w_in,
        grad_in_bias,
        grad_w_back,
        grad_back_bias,
    )


def to_sequences(array):
    return lax.all_to_all(array, "mp", split_axis=0, concat_axis=1, tiled=True)


def to_positions(array):
    return lax.all_to_all(
        array.astype(jnp.bfloat16), "mp", split_axis=1, concat_axis=0, tiled=True
    ).astype(jnp.float32)


def per_sequence(
    tokens,
    segment_ids,
    block_mask,
    gain_one,
    shift_one,
    w_qkv,
    w_out,
    out_bias,
    sort_query,
    sort_key,
    gain_two,
    shift_two,
    input_weight,
    in_bias,
    output_weight,
    back_bias,
    cotangent,
):
    mp_size = lax.axis_size("mp")
    kept_rows = tokens.shape[0] // mp_size
    block_mask = lax.dynamic_slice_in_dim(
        block_mask, lax.axis_index("mp") * kept_rows, kept_rows, 0
    )
    tokens = to_sequences(tokens)
    segment_ids = to_sequences(segment_ids)
    cotangent = to_sequences(cotangent)
    input_weight = lax.all_gather(input_weight, "mp", axis=1, tiled=True)
    output_weight = lax.all_gather(output_weight, "mp", axis=0, tiled=True)
    in_bias = lax.all_gather(in_bias, "mp", axis=0, tiled=True)
    seq_count, shard_len, model_width = tokens.shape
    head_size = model_width // HEADS
    local_blocks = shard_len // BLOCK
    all_blocks = block_mask.shape[1]
    scale_factor = head_size ** (-0.5)
    token_rows = seq_count * shard_len
    pair_shape = (seq_count, local_blocks, BLOCK, 2, HEADS, head_size)
    source = tokens.astype(jnp.float32)
    unit_one, inverse_one = norm_stats(source)
    normed_one = unit_one * gain_one + shift_one
    normed_low = normed_one.astype(jnp.bfloat16).reshape(token_rows, model_width)
    mixed_rows = jnp.dot(normed_low, w_qkv, preferred_element_type=jnp.float32).astype(jnp.bfloat16)
    mixed_rows = mixed_rows.reshape(seq_count, local_blocks, BLOCK, 3, HEADS, head_size)
    queries = mixed_rows[:, :, :, 0]
    key_value = mixed_rows[:, :, :, 1:]
    pair_flat = key_value.reshape(seq_count, local_blocks, BLOCK, 2 * model_width)
    summary_low = jnp.mean(
        normed_one.reshape(seq_count, local_blocks, BLOCK, model_width), axis=2
    ).astype(jnp.bfloat16)
    summary_all = summary_low
    sort_q = jnp.dot(summary_all, sort_query, preferred_element_type=jnp.float32)
    sort_k = jnp.dot(summary_all, sort_key, preferred_element_type=jnp.float32)
    diagonal = jnp.arange(all_blocks)[:, None] == jnp.arange(all_blocks)[None, :]
    allowed = (block_mask == 1) | diagonal[None]
    plan_full, plan_back = jax.vjp(partial(transport_plan, allowed=allowed), sort_q, sort_k)
    plan_local = plan_full.astype(jnp.bfloat16)
    pair_all = key_value
    sorted_pair = jnp.einsum(
        "shij,sjbchd->sibchd", plan_local, pair_all, preferred_element_type=jnp.float32
    )
    sorted_low = sorted_pair.astype(jnp.bfloat16)
    key_cat = jnp.concatenate([sorted_low[:, :, :, 0], key_value[:, :, :, 0]], axis=2)
    value_cat = jnp.concatenate([sorted_low[:, :, :, 1], key_value[:, :, :, 1]], axis=2)
    segment_blocks = segment_ids.reshape(seq_count, local_blocks, BLOCK)
    same_doc = segment_blocks[:, :, :, None] == segment_blocks[:, :, None, :]
    keep_mask = jnp.concatenate([jnp.ones_like(same_doc), same_doc], axis=-1)[:, :, None]
    raw_scores = (
        jnp.einsum("sibhd,sikhd->sihbk", queries, key_cat, preferred_element_type=jnp.float32)
        * scale_factor
    )
    scores = jnp.where(keep_mask, raw_scores, -1000000000.0)
    weights_soft = jax.nn.softmax(scores, axis=-1)
    weights_low = weights_soft.astype(jnp.bfloat16)
    attended = jnp.einsum(
        "sihbk,sikhd->sibhd", weights_low, value_cat, preferred_element_type=jnp.float32
    )
    attended_low = attended.astype(jnp.bfloat16).reshape(token_rows, model_width)
    projected = jnp.dot(attended_low, w_out, preferred_element_type=jnp.float32) + out_bias
    hidden = source + projected.reshape(seq_count, shard_len, model_width)
    unit_two, inverse_two = norm_stats(hidden)
    normed_two = (unit_two * gain_two + shift_two).astype(jnp.bfloat16)
    cot_float = cotangent.astype(jnp.float32)
    gathered_rows = normed_two
    pre_act = jnp.dot(
        gathered_rows, input_weight, preferred_element_type=jnp.float32
    ) + in_bias.astype(jnp.float32)
    active_float, gelu_back = jax.vjp(exact_gelu, pre_act)
    activated_hidden = active_float.astype(jnp.bfloat16)
    partial_out = jnp.dot(activated_hidden, output_weight, preferred_element_type=jnp.float32)
    ffn_out = partial_out
    cotangent_gathered = cotangent
    grad_activated_hidden = jnp.einsum(
        "mci,ni->mcn", cotangent_gathered, output_weight, preferred_element_type=jnp.float32
    )
    grad_pre = gelu_back(grad_activated_hidden)[0]
    grad_preactivation_rounded = grad_pre.astype(jnp.bfloat16)
    local_w_in = jnp.einsum(
        "rjy,rjq->yq", gathered_rows, grad_preactivation_rounded, preferred_element_type=jnp.float32
    )
    local_in_bias = jnp.sum(grad_pre, axis=(0, 1))
    local_output_weight = jnp.einsum(
        "wko,wkp->op", activated_hidden, cotangent_gathered, preferred_element_type=jnp.float32
    )
    grad_normed_two = jnp.einsum(
        "giv,cv->gic",
        grad_preactivation_rounded,
        input_weight,
        preferred_element_type=jnp.float32,
    )
    local_w_in, local_in_bias, local_output_weight = (
        lax.psum_scatter(local_w_in.astype(jnp.bfloat16), "mp", scatter_dimension=1, tiled=True),
        lax.psum_scatter(local_in_bias, "mp", scatter_dimension=0, tiled=True),
        lax.psum_scatter(
            local_output_weight.astype(jnp.bfloat16), "mp", scatter_dimension=0, tiled=True
        ),
    )
    grad_w_in, grad_in_bias, grad_w_back = (
        lax.psum(local_w_in, "dp").astype(jnp.float32),
        lax.psum(local_in_bias, "dp").astype(jnp.float32),
        lax.psum(local_output_weight, "dp").astype(jnp.float32),
    )
    layer_out = hidden + ffn_out + back_bias
    grad_hidden = cot_float + norm_back(grad_normed_two, unit_two, inverse_two, gain_two)
    grad_gain_two = jnp.sum(grad_normed_two * unit_two, axis=(0, 1))
    grad_shift_two = jnp.sum(grad_normed_two, axis=(0, 1))
    grad_back_bias = jnp.sum(cot_float, axis=(0, 1))
    grad_out_bias = jnp.sum(grad_hidden, axis=(0, 1))
    grad_proj_low = grad_hidden.astype(jnp.bfloat16).reshape(token_rows, model_width)
    grad_w_out = jnp.einsum(
        "td,te->de", attended_low, grad_proj_low, preferred_element_type=jnp.float32
    )
    grad_attended = jnp.einsum(
        "te,de->td", grad_proj_low, w_out, preferred_element_type=jnp.float32
    )
    grad_attended = grad_attended.astype(jnp.bfloat16).reshape(
        seq_count, local_blocks, BLOCK, HEADS, head_size
    )
    grad_weights = jnp.einsum(
        "sibhd,sikhd->sihbk", grad_attended, value_cat, preferred_element_type=jnp.float32
    )
    grad_value_cat = jnp.einsum(
        "sihbk,sibhd->sikhd", weights_low, grad_attended, preferred_element_type=jnp.float32
    )
    grad_scores = weights_soft * (
        grad_weights - jnp.sum(grad_weights * weights_soft, axis=-1, keepdims=True)
    )
    grad_scores_low = grad_scores.astype(jnp.bfloat16)
    grad_queries = (
        jnp.einsum(
            "sihbk,sikhd->sibhd", grad_scores_low, key_cat, preferred_element_type=jnp.float32
        )
        * scale_factor
    )
    grad_key_cat = (
        jnp.einsum(
            "sihbk,sibhd->sikhd", grad_scores_low, queries, preferred_element_type=jnp.float32
        )
        * scale_factor
    )
    grad_sorted = jnp.stack(
        [grad_key_cat[:, :, :BLOCK], grad_value_cat[:, :, :BLOCK]], axis=3
    ).astype(jnp.bfloat16)
    grad_pair_own = jnp.stack([grad_key_cat[:, :, BLOCK:], grad_value_cat[:, :, BLOCK:]], axis=3)
    grad_plan = jnp.einsum(
        "sibchd,sjbchd->shij", grad_sorted, pair_all, preferred_element_type=jnp.float32
    )
    term = jnp.einsum(
        "shij,sibchd->jsbchd", plan_local, grad_sorted, preferred_element_type=jnp.float32
    )
    from_sorted = jnp.moveaxis(term, 0, 1)
    grad_pair = grad_pair_own + from_sorted
    grad_mixed = jnp.concatenate([grad_queries[:, :, :, None], grad_pair], axis=3)
    grad_mixed_low = grad_mixed.astype(jnp.bfloat16).reshape(token_rows, 3 * model_width)
    grad_qkv = jnp.einsum(
        "td,te->de", normed_low, grad_mixed_low, preferred_element_type=jnp.float32
    )
    grad_sq, grad_sk = plan_back(grad_plan)
    summary_float = summary_low.astype(jnp.float32)
    grad_sort_query = jnp.einsum("sid,sie->de", summary_float, grad_sq, precision=HIGH)
    grad_sort_key = jnp.einsum("sid,sie->de", summary_float, grad_sk, precision=HIGH)
    grad_summary = jnp.einsum(
        "sie,de->sid", grad_sq, sort_query.astype(jnp.float32), precision=HIGH
    ) + jnp.einsum("sie,de->sid", grad_sk, sort_key.astype(jnp.float32), precision=HIGH)
    spread_summary = jnp.broadcast_to(
        (grad_summary / BLOCK)[:, :, None, :], (seq_count, local_blocks, BLOCK, model_width)
    ).reshape(seq_count, shard_len, model_width)
    grad_normed_one = jnp.einsum(
        "te,de->td", grad_mixed_low, w_qkv, preferred_element_type=jnp.float32
    )
    grad_normed_one = grad_normed_one.reshape(seq_count, shard_len, model_width) + spread_summary
    grad_gain_one = jnp.sum(grad_normed_one * unit_one, axis=(0, 1))
    grad_shift_one = jnp.sum(grad_normed_one, axis=(0, 1))
    grad_tokens = grad_hidden + norm_back(grad_normed_one, unit_one, inverse_one, gain_one)
    (
        grad_gain_one,
        grad_shift_one,
        grad_qkv,
        grad_w_out,
        grad_out_bias,
        grad_sort_query,
        grad_sort_key,
        grad_gain_two,
        grad_shift_two,
        grad_back_bias,
    ) = lax.psum(
        (
            grad_gain_one,
            grad_shift_one,
            grad_qkv,
            grad_w_out,
            grad_out_bias,
            grad_sort_query,
            grad_sort_key,
            grad_gain_two,
            grad_shift_two,
            grad_back_bias,
        ),
        ("dp", "mp"),
    )
    return (
        to_positions(layer_out),
        to_positions(grad_tokens),
        grad_gain_one,
        grad_shift_one,
        grad_qkv,
        grad_w_out,
        grad_out_bias,
        grad_sort_query,
        grad_sort_key,
        grad_gain_two,
        grad_shift_two,
        grad_w_in,
        grad_in_bias,
        grad_w_back,
        grad_back_bias,
    )


def solution(mesh):
    in_specs = (
        P("dp", "mp", None),
        P("dp", "mp"),
        P("dp", None, None),
        P(),
        P(),
        P(),
        P(),
        P(),
        P(),
        P(),
        P(),
        P(),
        P(None, "mp"),
        P("mp"),
        P("mp", None),
        P(),
        P("dp", "mp", None),
    )
    out_specs = (
        P("dp", "mp", None),
        P("dp", "mp", None),
        P(),
        P(),
        P(),
        P(),
        P(),
        P(),
        P(),
        P(),
        P(),
        P(None, "mp"),
        P("mp"),
        P("mp", None),
        P(),
    )

    def per_shard(tokens, *others):
        whole = tokens.shape[0] % lax.axis_size("mp") == 0
        return (per_sequence if whole else per_device)(tokens, *others)

    return jax.shard_map(
        per_shard, mesh=mesh, in_specs=in_specs, out_specs=out_specs, check_vma=False
    )
```

```python
from functools import partial
from types import SimpleNamespace

import jax
import jax.numpy as jnp
from jax import lax
from jax.experimental import pallas as pl
from jax.experimental.pallas import tpu as pltpu
from jax.sharding import PartitionSpec as P

HEADS = 8
BLOCK = 64
ITERS = 8
VMEM_BYTES = 60 * 2**20
COPIES = 128
LOCAL_COPIES = 16
TEMPER = 0.75
EPSILON = 1e-05
HIGH = lax.Precision.HIGHEST


def norm_stats(source):
    centred = source - jnp.mean(source, axis=-1, keepdims=True)
    inverse = lax.rsqrt(jnp.mean(centred * centred, axis=-1, keepdims=True) + EPSILON)
    return (centred * inverse, inverse)


def norm_back(grad_out, unit_rows, inverse, gain_vec):
    scaled = grad_out * gain_vec
    first_mean = jnp.mean(scaled, axis=-1, keepdims=True)
    second_mean = jnp.mean(scaled * unit_rows, axis=-1, keepdims=True)
    return inverse * (scaled - first_mean - unit_rows * second_mean)


def exact_gelu(pre_act):
    return jax.nn.gelu(pre_act, approximate=False)


def transport_plan(sort_q, sort_k, allowed):
    seq_count, blocks, model_width = sort_q.shape
    head_size = model_width // HEADS
    query_heads = sort_q.reshape(seq_count, blocks, HEADS, head_size)
    key_heads = sort_k.reshape(seq_count, blocks, HEADS, head_size)
    logits = jnp.einsum("sihe,sjhe->shij", query_heads, key_heads, precision=HIGH) * head_size ** (
        -0.5
    )
    log_plan = jnp.where(allowed[:, None], logits / TEMPER, -1000000000.0)
    for sweep_index in range(ITERS):
        log_plan = log_plan - jax.nn.logsumexp(log_plan, axis=-1, keepdims=True)
        log_plan = log_plan - jax.nn.logsumexp(log_plan, axis=-2, keepdims=True)
    return jnp.exp(log_plan)


def per_device(
    tokens,
    segment_ids,
    block_mask,
    gain_one,
    shift_one,
    w_qkv,
    w_out,
    out_bias,
    sort_query,
    sort_key,
    gain_two,
    shift_two,
    input_weight,
    in_bias,
    output_weight,
    back_bias,
    cotangent,
):
    seq_count, shard_len, model_width = tokens.shape
    head_size = model_width // HEADS
    local_blocks = shard_len // BLOCK
    all_blocks = block_mask.shape[1]
    first_block = lax.axis_index("mp") * local_blocks
    scale_factor = head_size ** (-0.5)
    token_rows = seq_count * shard_len
    pair_shape = (seq_count, local_blocks, BLOCK, 2, HEADS, head_size)
    source = tokens.astype(jnp.float32)
    unit_one, inverse_one = norm_stats(source)
    normed_one = unit_one * gain_one + shift_one
    normed_low = normed_one.astype(jnp.bfloat16).reshape(token_rows, model_width)
    mixed_rows = jnp.dot(normed_low, w_qkv, preferred_element_type=jnp.float32).astype(jnp.bfloat16)
    mixed_rows = mixed_rows.reshape(seq_count, local_blocks, BLOCK, 3, HEADS, head_size)
    queries = mixed_rows[:, :, :, 0]
    key_value = mixed_rows[:, :, :, 1:]
    pair_flat = key_value.reshape(seq_count, local_blocks, BLOCK, 2 * model_width)
    summary_low = jnp.mean(
        normed_one.reshape(seq_count, local_blocks, BLOCK, model_width), axis=2
    ).astype(jnp.bfloat16)
    summary_all = lax.all_gather(summary_low, "mp", axis=1, tiled=True)
    sort_q = jnp.dot(summary_all, sort_query, preferred_element_type=jnp.float32)
    sort_k = jnp.dot(summary_all, sort_key, preferred_element_type=jnp.float32)
    diagonal = jnp.arange(all_blocks)[:, None] == jnp.arange(all_blocks)[None, :]
    allowed = (block_mask == 1) | diagonal[None]
    plan_full, plan_back = jax.vjp(partial(transport_plan, allowed=allowed), sort_q, sort_k)
    plan_local = lax.dynamic_slice_in_dim(plan_full, first_block, local_blocks, 2).astype(
        jnp.bfloat16
    )
    pair_all = lax.all_gather(pair_flat, "mp", axis=1, tiled=True).reshape(
        seq_count, all_blocks, BLOCK, 2, HEADS, head_size
    )
    sorted_pair = jnp.einsum(
        "shij,sjbchd->sibchd", plan_local, pair_all, preferred_element_type=jnp.float32
    )
    sorted_low = sorted_pair.astype(jnp.bfloat16)
    key_cat = jnp.concatenate([sorted_low[:, :, :, 0], key_value[:, :, :, 0]], axis=2)
    value_cat = jnp.concatenate([sorted_low[:, :, :, 1], key_value[:, :, :, 1]], axis=2)
    segment_blocks = segment_ids.reshape(seq_count, local_blocks, BLOCK)
    same_doc = segment_blocks[:, :, :, None] == segment_blocks[:, :, None, :]
    keep_mask = jnp.concatenate([jnp.ones_like(same_doc), same_doc], axis=-1)[:, :, None]
    raw_scores = (
        jnp.einsum("sibhd,sikhd->sihbk", queries, key_cat, preferred_element_type=jnp.float32)
        * scale_factor
    )
    scores = jnp.where(keep_mask, raw_scores, -1000000000.0)
    weights_soft = jax.nn.softmax(scores, axis=-1)
    weights_low = weights_soft.astype(jnp.bfloat16)
    attended = jnp.einsum(
        "sihbk,sikhd->sibhd", weights_low, value_cat, preferred_element_type=jnp.float32
    )
    attended_low = attended.astype(jnp.bfloat16).reshape(token_rows, model_width)
    projected = jnp.dot(attended_low, w_out, preferred_element_type=jnp.float32) + out_bias
    hidden = source + projected.reshape(seq_count, shard_len, model_width)
    unit_two, inverse_two = norm_stats(hidden)
    normed_two = (unit_two * gain_two + shift_two).astype(jnp.bfloat16)
    cot_float = cotangent.astype(jnp.float32)
    gathered_rows = lax.all_gather(normed_two, "mp", axis=1, tiled=True)
    pre_act = jnp.dot(
        gathered_rows, input_weight, preferred_element_type=jnp.float32
    ) + in_bias.astype(jnp.float32)
    active_float, gelu_back = jax.vjp(exact_gelu, pre_act)
    activated_hidden = active_float.astype(jnp.bfloat16)
    partial_out = jnp.dot(activated_hidden, output_weight, preferred_element_type=jnp.float32)
    ffn_out = lax.psum_scatter(
        partial_out.astype(jnp.bfloat16), "mp", scatter_dimension=1, tiled=True
    ).astype(jnp.float32)
    cotangent_gathered = lax.all_gather(cotangent, "mp", axis=1, tiled=True)
    grad_activated_hidden = jnp.einsum(
        "mci,ni->mcn", cotangent_gathered, output_weight, preferred_element_type=jnp.float32
    )
    grad_pre = gelu_back(grad_activated_hidden)[0]
    grad_preactivation_rounded = grad_pre.astype(jnp.bfloat16)
    local_w_in = jnp.einsum(
        "rjy,rjq->yq", gathered_rows, grad_preactivation_rounded, preferred_element_type=jnp.float32
    )
    local_in_bias = jnp.sum(grad_pre, axis=(0, 1))
    local_output_weight = jnp.einsum(
        "wko,wkp->op", activated_hidden, cotangent_gathered, preferred_element_type=jnp.float32
    )
    grad_normed_two = lax.psum_scatter(
        jnp.einsum(
            "giv,cv->gic",
            grad_preactivation_rounded,
            input_weight,
            preferred_element_type=jnp.float32,
        ),
        "mp",
        scatter_dimension=1,
        tiled=True,
    )
    grad_w_in, grad_in_bias, grad_w_back = (
        lax.psum(local_w_in.astype(jnp.bfloat16), "dp").astype(jnp.float32),
        lax.psum(local_in_bias.astype(jnp.bfloat16), "dp").astype(jnp.float32),
        lax.psum(local_output_weight.astype(jnp.bfloat16), "dp").astype(jnp.float32),
    )
    layer_out = hidden + ffn_out + back_bias
    grad_hidden = cot_float + norm_back(grad_normed_two, unit_two, inverse_two, gain_two)
    grad_gain_two = jnp.sum(grad_normed_two * unit_two, axis=(0, 1))
    grad_shift_two = jnp.sum(grad_normed_two, axis=(0, 1))
    grad_back_bias = jnp.sum(cot_float, axis=(0, 1))
    grad_out_bias = jnp.sum(grad_hidden, axis=(0, 1))
    grad_proj_low = grad_hidden.astype(jnp.bfloat16).reshape(token_rows, model_width)
    grad_w_out = jnp.einsum(
        "td,te->de", attended_low, grad_proj_low, preferred_element_type=jnp.float32
    )
    grad_attended = jnp.einsum(
        "te,de->td", grad_proj_low, w_out, preferred_element_type=jnp.float32
    )
    grad_attended = grad_attended.astype(jnp.bfloat16).reshape(
        seq_count, local_blocks, BLOCK, HEADS, head_size
    )
    grad_weights = jnp.einsum(
        "sibhd,sikhd->sihbk", grad_attended, value_cat, preferred_element_type=jnp.float32
    )
    grad_value_cat = jnp.einsum(
        "sihbk,sibhd->sikhd", weights_low, grad_attended, preferred_element_type=jnp.float32
    )
    grad_scores = weights_soft * (
        grad_weights - jnp.sum(grad_weights * weights_soft, axis=-1, keepdims=True)
    )
    grad_scores_low = grad_scores.astype(jnp.bfloat16)
    grad_queries = (
        jnp.einsum(
            "sihbk,sikhd->sibhd", grad_scores_low, key_cat, preferred_element_type=jnp.float32
        )
        * scale_factor
    )
    grad_key_cat = (
        jnp.einsum(
            "sihbk,sibhd->sikhd", grad_scores_low, queries, preferred_element_type=jnp.float32
        )
        * scale_factor
    )
    grad_sorted = jnp.stack(
        [grad_key_cat[:, :, :BLOCK], grad_value_cat[:, :, :BLOCK]], axis=3
    ).astype(jnp.bfloat16)
    grad_pair_own = jnp.stack([grad_key_cat[:, :, BLOCK:], grad_value_cat[:, :, BLOCK:]], axis=3)
    grad_plan = jnp.einsum(
        "sibchd,sjbchd->shij", grad_sorted, pair_all, preferred_element_type=jnp.float32
    )
    term = jnp.einsum(
        "shij,sibchd->jsbchd", plan_local, grad_sorted, preferred_element_type=jnp.float32
    )
    from_sorted = lax.psum_scatter(
        term.reshape(local_blocks * lax.axis_size("mp"), seq_count, BLOCK, 2 * model_width).astype(
            jnp.bfloat16
        ),
        "mp",
        scatter_dimension=0,
        tiled=True,
    ).astype(jnp.float32)
    from_sorted = jnp.moveaxis(from_sorted, 0, 1).reshape(pair_shape)
    grad_pair = grad_pair_own + from_sorted
    grad_mixed = jnp.concatenate([grad_queries[:, :, :, None], grad_pair], axis=3)
    grad_mixed_low = grad_mixed.astype(jnp.bfloat16).reshape(token_rows, 3 * model_width)
    grad_qkv = jnp.einsum(
        "td,te->de", normed_low, grad_mixed_low, preferred_element_type=jnp.float32
    )
    grad_plan_all = lax.all_gather(grad_plan.astype(jnp.bfloat16), "mp", axis=2, tiled=True).astype(
        grad_plan.dtype
    )
    grad_sq_all, grad_sk_all = plan_back(grad_plan_all)
    grad_sq = lax.dynamic_slice_in_dim(grad_sq_all, first_block, local_blocks, 1)
    grad_sk = lax.dynamic_slice_in_dim(grad_sk_all, first_block, local_blocks, 1)
    summary_float = summary_low.astype(jnp.float32)
    grad_sort_query = jnp.einsum("sid,sie->de", summary_float, grad_sq, precision=HIGH)
    grad_sort_key = jnp.einsum("sid,sie->de", summary_float, grad_sk, precision=HIGH)
    grad_summary = jnp.einsum(
        "sie,de->sid", grad_sq, sort_query.astype(jnp.float32), precision=HIGH
    ) + jnp.einsum("sie,de->sid", grad_sk, sort_key.astype(jnp.float32), precision=HIGH)
    spread_summary = jnp.broadcast_to(
        (grad_summary / BLOCK)[:, :, None, :], (seq_count, local_blocks, BLOCK, model_width)
    ).reshape(seq_count, shard_len, model_width)
    grad_normed_one = jnp.einsum(
        "te,de->td", grad_mixed_low, w_qkv, preferred_element_type=jnp.float32
    )
    grad_normed_one = grad_normed_one.reshape(seq_count, shard_len, model_width) + spread_summary
    grad_gain_one = jnp.sum(grad_normed_one * unit_one, axis=(0, 1))
    grad_shift_one = jnp.sum(grad_normed_one, axis=(0, 1))
    grad_tokens = grad_hidden + norm_back(grad_normed_one, unit_one, inverse_one, gain_one)
    (
        grad_gain_one,
        grad_shift_one,
        grad_qkv,
        grad_w_out,
        grad_out_bias,
        grad_sort_query,
        grad_sort_key,
        grad_gain_two,
        grad_shift_two,
        grad_back_bias,
    ) = lax.psum(
        (
            grad_gain_one,
            grad_shift_one,
            grad_qkv,
            grad_w_out,
            grad_out_bias,
            grad_sort_query,
            grad_sort_key,
            grad_gain_two,
            grad_shift_two,
            grad_back_bias,
        ),
        ("dp", "mp"),
    )
    return (
        layer_out,
        grad_tokens,
        grad_gain_one,
        grad_shift_one,
        grad_qkv,
        grad_w_out,
        grad_out_bias,
        grad_sort_query,
        grad_sort_key,
        grad_gain_two,
        grad_shift_two,
        grad_w_in,
        grad_in_bias,
        grad_w_back,
        grad_back_bias,
    )


GROUP_LANES = 256


def dot(left, right, contract=((1,), (0,)), precision=None):
    return lax.dot_general(
        left,
        right,
        (contract, ((), ())),
        precision=precision,
        preferred_element_type=jnp.float32,
    )


def dot_right_t(left, right, precision=None):
    return dot(left, right, ((1,), (1,)), precision)


def dot_left_t(left, right, precision=None):
    return dot(left, right, ((0,), (0,)), precision)


def row_sum(array):
    return jnp.sum(array, axis=0, keepdims=True)


def head_lanes(head_size):
    lane_head = lax.broadcasted_iota(jnp.int32, (1, GROUP_LANES), 1) // head_size
    return [lane_head == h for h in range(GROUP_LANES // head_size)]


def spread_heads(rows, lanes):
    return jnp.concatenate(
        [rows * keep.astype(jnp.float32).astype(rows.dtype) for keep in lanes], axis=0
    )


def fold_heads(stacked, lanes):
    rows = stacked.shape[0] // len(lanes)
    total = stacked[:rows]
    for h, keep in enumerate(lanes[1:], 1):
        total = jnp.where(keep, stacked[h * rows : (h + 1) * rows], total)
    return total


def norm_parts(source):
    centred = source - jnp.mean(source, axis=-1, keepdims=True)
    inverse = lax.rsqrt(jnp.mean(centred * centred, axis=-1, keepdims=True) + EPSILON)
    return (centred * inverse, inverse)


def chunk_blocks(r, some):
    return pl.ds(r * some, some)


def first_norm(k, arrived):
    chunks, chunk_rows, width = k.tok.shape
    some = chunk_rows // BLOCK

    @pl.loop(0, chunks)
    def _(t):
        r = arrived(t)
        unit, _ = norm_parts(k.tok[r].astype(jnp.float32))
        normed = unit * k.gain_one[...] + k.shift_one[...]
        k.means[r] = jnp.mean(normed.reshape(some, BLOCK, width), axis=1)
        low = normed.astype(jnp.bfloat16)
        k.normed_low[r] = low
        mixed = dot(low, k.w_qkv[...]).astype(jnp.bfloat16)
        k.mixed[chunk_blocks(r, some)] = mixed.reshape(some, BLOCK, 3 * width)


def head_rows(rows, head_size):
    blocks, width = rows.shape
    shape = (blocks, HEADS, width)
    mine = lax.broadcasted_iota(jnp.int32, shape, 1) == (
        lax.broadcasted_iota(jnp.int32, shape, 2) // head_size
    )
    return jnp.where(mine, rows[:, None, :], 0.0).reshape(blocks * HEADS, width)


def sort_plan(k):
    width = k.tok.shape[2]
    head_size = width // HEADS
    blocks = k.mixed.shape[0]
    summary = k.means[...].reshape(blocks, width).astype(jnp.bfloat16)
    sort_q = dot(summary, k.sort_query[...])
    sort_k = dot(summary, k.sort_key[...])
    k.summary[...] = summary.astype(jnp.float32)
    k.sort_q[...] = sort_q
    k.sort_k[...] = sort_k
    logits = dot_right_t(head_rows(sort_q, head_size), sort_k, HIGH) * head_size ** (-0.5)
    allowed = (k.mask[k.z] == 1) | (
        lax.broadcasted_iota(jnp.int32, (blocks, blocks), 0)
        == lax.broadcasted_iota(jnp.int32, (blocks, blocks), 1)
    )
    allowed = jnp.where(allowed, 1.0, 0.0)[:, None, :]
    k.allowed[...] = jnp.broadcast_to(allowed, (blocks, HEADS, blocks))
    log_plan = jnp.where(
        k.allowed[...] > 0.5, logits.reshape(blocks, HEADS, blocks) / TEMPER, -1000000000.0
    )

    def sweep(t, log_plan):
        for half, axis in enumerate((2, 0)):
            top = jnp.max(log_plan, axis=axis, keepdims=True)
            total = jnp.sum(jnp.exp(log_plan - top), axis=axis, keepdims=True)
            log_plan = log_plan - (top + jnp.log(total))
            k.log_plans[2 * t + half] = log_plan
        return log_plan

    plan = jnp.exp(lax.fori_loop(0, ITERS, sweep, log_plan))
    spread_plan(k, plan.reshape(blocks * HEADS, blocks))


def spread_plan(k, plan):
    rows, blocks = plan.shape
    side = GROUP_LANES
    part = side // blocks
    columns = (
        lax.broadcasted_iota(jnp.int32, (blocks, side), 1) // part
        == lax.broadcasted_iota(jnp.int32, (blocks, side), 0)
    ).astype(jnp.float32)
    wide = dot(plan.astype(jnp.bfloat16), columns.astype(jnp.bfloat16))
    tall = wide.T.astype(jnp.bfloat16)
    wide = wide.astype(jnp.bfloat16)
    same = (
        lax.broadcasted_iota(jnp.int32, (side, side), 0) % part
        == lax.broadcasted_iota(jnp.int32, (side, side), 1) % part
    )
    block_of = lax.broadcasted_iota(jnp.int32, (side, rows), 0) // part
    row_of = lax.broadcasted_iota(jnp.int32, (side, rows), 1)
    block_at = lax.broadcasted_iota(jnp.int32, (rows, side), 1) // part
    row_at = lax.broadcasted_iota(jnp.int32, (rows, side), 0)
    in_group = HEADS // k.plan_wide.shape[0]
    for h in range(HEADS):
        pick = (row_of == block_of * HEADS + h).astype(jnp.float32).astype(jnp.bfloat16)
        pick_t = (row_at == block_at * HEADS + h).astype(jnp.float32).astype(jnp.bfloat16)
        at = pl.ds((h % in_group) * side, side)
        k.plan_wide[h // in_group, :, at] = jnp.where(same, dot(pick, wide), 0.0).astype(
            jnp.bfloat16
        )
        k.plan_tall[h // in_group, :, at] = jnp.where(same, dot(tall, pick_t), 0.0).astype(
            jnp.bfloat16
        )


def mix_blocks(k, plan_ref, source, source_lane, write):
    blocks, _, _ = source.shape
    width = k.tok.shape[2]
    part = GROUP_LANES // blocks
    lanes = head_lanes(width // HEADS)
    for c in range(BLOCK // part):
        for lane in range(0, 2 * width, GROUP_LANES):
            group = (lane % width) // GROUP_LANES
            rows = source[:, pl.ds(c * part, part), pl.ds(source_lane + lane, GROUP_LANES)]
            rows = spread_heads(rows.reshape(GROUP_LANES, GROUP_LANES), lanes)
            mixed = dot(plan_ref[group], rows)
            write(c * part, part, lane, mixed.reshape(blocks, part, GROUP_LANES))


def sort_forward(k):
    def write(row, rows, lane, mixed):
        k.sorted[:, pl.ds(row, rows), pl.ds(lane, GROUP_LANES)] = mixed.astype(jnp.bfloat16)

    mix_blocks(k, k.plan_wide, k.mixed, k.tok.shape[2], write)


def block_parts(k, i, lane):
    width = k.tok.shape[2]
    queries = k.mixed[i, :, pl.ds(lane, GROUP_LANES)]
    keys = jnp.concatenate(
        [
            k.sorted[i, :, pl.ds(lane, GROUP_LANES)],
            k.mixed[i, :, pl.ds(width + lane, GROUP_LANES)],
        ],
        axis=0,
    )
    values = jnp.concatenate(
        [
            k.sorted[i, :, pl.ds(width + lane, GROUP_LANES)],
            k.mixed[i, :, pl.ds(2 * width + lane, GROUP_LANES)],
        ],
        axis=0,
    )
    return (queries, keys, values)


def attend(k, first, last):
    width = k.tok.shape[2]
    head_size = width // HEADS
    lanes = head_lanes(head_size)
    heads = len(lanes)
    some = k.tok.shape[1] // BLOCK
    lane_at = lax.broadcasted_iota(jnp.int32, (BLOCK, 2 * BLOCK), 1)

    @pl.loop(first, last)
    def _(i):
        ids = jnp.broadcast_to(k.seg[i // some, pl.ds(i % some, 1), :], (BLOCK, 2 * BLOCK))
        row_at = lax.broadcasted_iota(jnp.int32, (BLOCK, 2 * BLOCK), 0)
        own = jnp.sum(jnp.where(lane_at == row_at + BLOCK, ids, 0.0), axis=1, keepdims=True)
        keep = ((lane_at < BLOCK) | (own == ids)).astype(jnp.float32)
        keep = jnp.concatenate([keep] * heads, axis=0) > 0.5
        for group in range(width // GROUP_LANES):
            lane = group * GROUP_LANES
            queries, keys, values = block_parts(k, i, lane)
            scores = dot_right_t(spread_heads(queries, lanes), keys) * head_size ** (-0.5)
            scores = jnp.where(keep, scores, -1000000000.0)
            raised = jnp.exp(scores - jnp.max(scores, axis=-1, keepdims=True))
            weights = raised / jnp.sum(raised, axis=-1, keepdims=True)
            k.weights[i, group] = weights
            mixed = fold_heads(dot(weights.astype(jnp.bfloat16), values), lanes)
            k.attended[i, :, pl.ds(lane, GROUP_LANES)] = mixed.astype(jnp.bfloat16)


def second_norm(k):
    chunks, chunk_rows, width = k.tok.shape
    some = chunk_rows // BLOCK
    shape = (some, BLOCK, width)

    @pl.loop(0, chunks)
    def _(r):
        at = chunk_blocks(r, some)
        projected = dot(k.attended[at].reshape(chunk_rows, width), k.w_out[...]) + k.out_bias[...]
        hidden = k.tok[r].astype(jnp.float32) + projected
        k.hidden[r] = hidden
        unit, _ = norm_parts(hidden)
        k.normed_two[r] = (unit * k.gain_two[...] + k.shift_two[...]).astype(jnp.bfloat16)
        k.out_sum[at] = (hidden + k.back_bias[...]).reshape(shape)
        k.grad_normed[at] = jnp.zeros(shape, jnp.float32)


def feed_forward(k, c):
    chunks, chunk_rows, width = k.tok.shape
    some = chunk_rows // BLOCK
    shape = (some, BLOCK, width)
    units = k.active.shape[2]
    w_in = k.w_in.at[c]
    w_back = k.w_back.at[c]

    def rows(r, in_bias_sum):
        at = chunk_blocks(r, some)
        weight = w_in[...].reshape(width, units)
        weight_back = w_back[...].reshape(units, width)
        pre = dot(k.normed_two[r], weight) + k.in_bias[c, 0:1, :]
        cdf = 0.5 + 0.5 * lax.erf(pre * 0.5**0.5)
        active = (pre * cdf).astype(jnp.bfloat16)
        slope = cdf + pre * (jnp.exp(pre * pre * -0.5) * 0.3989422804014327)
        k.out_sum[at] += dot(active, weight_back).reshape(shape)
        grad_pre = dot_right_t(k.cot[r], weight_back) * slope
        grad_low = grad_pre.astype(jnp.bfloat16)
        k.grad_normed[at] += dot_right_t(grad_low, weight).reshape(shape)
        k.active[r] = active
        k.grad_pre[r] = grad_low
        return in_bias_sum + row_sum(grad_pre)

    total = lax.fori_loop(0, chunks, rows, jnp.zeros((1, units), jnp.float32))
    k.sums[pl.ds(8 + c, 1), :] = total
    rows_in = whole_rows(k.normed_two)
    k.ff_in[c] = as_pack(dot_left_t(rows_in, whole_rows(k.grad_pre)), k.ff_in.shape[1:])
    k.ff_back[c] = as_pack(dot_left_t(whole_rows(k.active), whole_rows(k.cot)), k.ff_back.shape[1:])


def whole_rows(ref):
    return ref[...].reshape(-1, ref.shape[-1])


def as_pack(array, shape):
    return array.astype(jnp.bfloat16).reshape(shape)


def norm_grad(grad_out, unit, inverse, gain):
    scaled = grad_out * gain
    first = jnp.mean(scaled, axis=-1, keepdims=True)
    second = jnp.mean(scaled * unit, axis=-1, keepdims=True)
    return inverse * (scaled - first - unit * second)


def second_norm_back(k, order, leave):
    chunks, chunk_rows, width = k.tok.shape
    some = chunk_rows // BLOCK

    def rows(t, sums):
        r = order(t)
        at = chunk_blocks(r, some)
        k.stage[r] = k.out_sum[at].reshape(chunk_rows, width).astype(jnp.bfloat16)
        leave(t)
        unit, inverse = norm_parts(k.hidden[r])
        grad_normed = k.grad_normed[at].reshape(chunk_rows, width)
        out_grad = k.cot[r].astype(jnp.float32)
        grad_hidden = out_grad + norm_grad(grad_normed, unit, inverse, k.gain_two[...])
        k.hidden[r] = grad_hidden
        low = grad_hidden.astype(jnp.bfloat16)
        k.grad_low[r] = low
        grad_attended = dot_right_t(low, k.w_out[...]).astype(jnp.bfloat16)
        k.grad_attended[at] = grad_attended.reshape(some, BLOCK, width)
        terms = (grad_normed * unit, grad_normed, out_grad, grad_hidden)
        return tuple(total + row_sum(term) for total, term in zip(sums, terms))

    zero = jnp.zeros((1, width), jnp.float32)
    sums = lax.fori_loop(0, chunks, rows, (zero,) * 4)
    for at, total in enumerate(sums):
        k.sums[at : at + 1, :] = total
    grad = dot_left_t(whole_rows(k.attended), whole_rows(k.grad_low))
    put_matrix(k.rest, 0, grad)


def put_matrix(pack, at, matrix):
    shape = pack.shape[:4] + pack.shape[5:]
    pack[:, :, :, :, at] = as_pack(matrix, shape)


def attend_back(k, first, last):
    width = k.tok.shape[2]
    head_size = width // HEADS
    lanes = head_lanes(head_size)
    scale = head_size ** (-0.5)

    @pl.loop(first, last)
    def _(i):
        for group in range(width // GROUP_LANES):
            lane = group * GROUP_LANES
            queries, keys, values = block_parts(k, i, lane)
            queries = spread_heads(queries, lanes)
            grad_out = spread_heads(k.grad_attended[i, :, pl.ds(lane, GROUP_LANES)], lanes)
            weights = k.weights[i, group]
            grad_weights = dot_right_t(grad_out, values)
            grad_values = dot_left_t(weights.astype(jnp.bfloat16), grad_out)
            inner = jnp.sum(grad_weights * weights, axis=-1, keepdims=True)
            grad_scores = (weights * (grad_weights - inner)).astype(jnp.bfloat16)
            grad_queries = fold_heads(dot(grad_scores, keys), lanes) * scale
            grad_keys = dot_left_t(grad_scores, queries) * scale
            place = pl.ds(lane, GROUP_LANES)
            k.mixed[i, :, place] = grad_queries.astype(jnp.bfloat16)
            k.sorted[i, :, place] = grad_keys[:BLOCK].astype(jnp.bfloat16)
            k.out_sum[i, :, place] = grad_keys[BLOCK:]
            k.sorted[i, :, pl.ds(width + lane, GROUP_LANES)] = grad_values[:BLOCK].astype(
                jnp.bfloat16
            )
            k.grad_normed[i, :, place] = grad_values[BLOCK:]


def sort_back(k):
    width = k.tok.shape[2]
    blocks = k.mixed.shape[0]
    side = GROUP_LANES
    part = side // blocks
    lanes = head_lanes(width // HEADS)
    in_group = len(lanes)

    same = (
        lax.broadcasted_iota(jnp.int32, (side, side), 0) % part
        == lax.broadcasted_iota(jnp.int32, (side, side), 1) % part
    )
    fold_columns = (
        lax.broadcasted_iota(jnp.int32, (side, blocks), 0) // part
        == lax.broadcasted_iota(jnp.int32, (side, blocks), 1)
    ).astype(jnp.float32)
    for group in range(width // side):
        total = jnp.zeros((in_group * side, side), jnp.float32)
        for c in range(BLOCK // part):
            for offset in (0, width):
                lane = offset + group * side
                grads = k.sorted[:, pl.ds(c * part, part), pl.ds(lane, side)]
                rows = k.mixed[:, pl.ds(c * part, part), pl.ds(width + lane, side)]
                total = total + dot_right_t(
                    spread_heads(grads.reshape(side, side), lanes), rows.reshape(side, side)
                )
        for h in range(in_group):
            picked = jnp.where(same, total[h * side : (h + 1) * side], 0.0)
            picked = jnp.sum(picked.reshape(blocks, part, side), axis=1)
            k.grad_plan[:, group * in_group + h, :] = dot(picked, fold_columns, precision=HIGH)

    def write(row, rows, lane, mixed):
        own = k.out_sum if lane < width else k.grad_normed
        own = own[:, pl.ds(row, rows), pl.ds(lane % width, side)]
        k.mixed[:, pl.ds(row, rows), pl.ds(width + lane, side)] = (own + mixed).astype(
            jnp.bfloat16
        )

    mix_blocks(k, k.plan_tall, k.sorted, 0, write)


def plan_back(k):
    width = k.tok.shape[2]
    head_size = width // HEADS
    blocks = k.mixed.shape[0]
    grad = k.grad_plan[...] * jnp.exp(k.log_plans[2 * ITERS - 1])

    def sweep(t, grad):
        for half, axis in ((1, 0), (0, 2)):
            share = jnp.exp(k.log_plans[2 * (ITERS - 1 - t) + half])
            grad = grad - share * jnp.sum(grad, axis=axis, keepdims=True)
        return grad

    grad = lax.fori_loop(0, ITERS, sweep, grad)
    grad = jnp.where(k.allowed[...] > 0.5, grad / TEMPER, 0.0) * head_size ** (-0.5)
    grad = grad.reshape(blocks * HEADS, blocks)
    sort_q = k.sort_q[...]
    sort_k = k.sort_k[...]
    shape = (blocks, HEADS, width)
    mine = lax.broadcasted_iota(jnp.int32, shape, 1) == (
        lax.broadcasted_iota(jnp.int32, shape, 2) // head_size
    )
    grad_sq = dot(grad, sort_k, precision=HIGH).reshape(shape)
    grad_sq = jnp.sum(jnp.where(mine, grad_sq, 0.0), axis=1)
    grad_sk = dot_left_t(grad, head_rows(sort_q, head_size), HIGH)
    summary = k.summary[...]
    put_matrix(k.rest, 1, dot_left_t(summary, grad_sq, HIGH))
    put_matrix(k.rest, 2, dot_left_t(summary, grad_sk, HIGH))
    grad_summary = dot_right_t(grad_sq, k.sort_query[...].astype(jnp.float32), HIGH)
    grad_summary += dot_right_t(grad_sk, k.sort_key[...].astype(jnp.float32), HIGH)
    some = k.means.shape[1]
    k.means[...] = (grad_summary / BLOCK).reshape(blocks // some, some, width)


def first_weights(k):
    width = k.tok.shape[2]
    for part in range(3):
        grad = k.mixed[:, :, pl.ds(part * width, width)].reshape(-1, width)
        put_matrix(k.qkv, part, dot_left_t(whole_rows(k.normed_low), grad))


def first_norm_back(k, order, leave):
    chunks, chunk_rows, width = k.tok.shape
    some = chunk_rows // BLOCK

    def rows(t, sums):
        r = order(t)
        grad_mixed = k.mixed[chunk_blocks(r, some)].reshape(chunk_rows, 3 * width)
        spread = jnp.broadcast_to(k.means[r][:, None, :], (some, BLOCK, width))
        grad_normed = dot_right_t(grad_mixed, k.w_qkv[...]) + spread.reshape(chunk_rows, width)
        unit, inverse = norm_parts(k.tok[r].astype(jnp.float32))
        grad = k.hidden[r] + norm_grad(grad_normed, unit, inverse, k.gain_one[...])
        k.stage[r] = grad.astype(jnp.bfloat16)
        leave(t)
        terms = (grad_normed * unit, grad_normed)
        return tuple(total + row_sum(term) for total, term in zip(sums, terms))

    zero = jnp.zeros((1, width), jnp.float32)
    sums = lax.fori_loop(0, chunks, rows, (zero,) * 2)
    for at, total in enumerate(sums, 4):
        k.sums[at : at + 1, :] = total


def flip(index, bit):
    return index + bit - 2 * bit * ((index // bit) % 2)


def flip_both(index, step):
    low, high = index % 2, index // 2
    low_step, high_step = step % 2, step // 2
    return (low + low_step - 2 * low * low_step) + 2 * (
        high + high_step - 2 * high * high_step
    )


class Links:
    def __init__(self, k):
        self.k = k
        self.used = 0
        self.used_here = 0

    def take(self, count):
        self.used += count
        return self.used - count

    def copy(self, at, source, target, peer):
        return pltpu.make_async_remote_copy(
            src_ref=source,
            dst_ref=target,
            send_sem=self.k.send.at[at],
            recv_sem=self.k.recv.at[at],
            device_id=peer,
            device_id_type=pl.DeviceIdType.MESH,
        )

    def here(self, source, target):
        self.used_here += 1
        return pltpu.make_async_copy(source, target, self.k.local.at[self.used_here - 1])


def start(copies):
    for copy in copies:
        copy.start()


def wait(copies):
    for copy in copies:
        copy.wait()


class Reduction:
    def __init__(self, links, pack, lands, out, places, mp_peers, z, whole, parts_apart):
        self.pack, self.lands, self.out, self.whole, self.z = (pack, lands, out, whole, z)
        (c, to_c), (a, to_a), (b, to_b) = places
        self.places = (c, a, b)
        parts = pack.shape[0]
        link = links.copy
        first = links.take(parts if parts_apart else 1)
        if parts_apart:
            self.core_part = lambda part, t: link(
                first + t, pack.at[part, 1 - c], lands[0].at[part], to_c
            )
        else:
            self.core = [link(first, pack.at[:, 1 - c], lands[0], to_c)]
        self.second = [link(links.take(1), pack.at[:, c, 1 - a], lands[1], to_a)]
        self.third = [link(links.take(1), pack.at[:, c, a, 1 - b], lands[2], to_b)]
        self.across = [
            link(links.take(1), pack.at[peer["mp"], c, a, b], lands[3].at[t], peer)
            for t, peer in enumerate(mp_peers)
        ]
        own = z if whole else 0
        self.own = own
        piece = out.at[own, c, a, b]
        self.across_back = (
            [link(links.take(1), piece, piece, peer) for peer in mp_peers] if whole else []
        )
        piece = out.at[:, c, a, b]
        self.third_back = [link(links.take(1), piece, piece, to_b)]
        piece = out.at[:, c, a]
        self.second_back = [link(links.take(1), piece, piece, to_a)]
        piece = out.at[:, c]
        self.core_back = [link(links.take(1), piece, piece, to_c)]

    def add(self, level):
        place = self.places[: level + 1]

        @pl.loop(0, self.pack.shape[0])
        def _(part):
            at = (part,) + place
            total = self.pack[at].astype(jnp.float32) + self.lands[level][part].astype(jnp.float32)
            self.pack[at] = total.astype(jnp.bfloat16)

    def to_second(self):
        wait(self.core)
        self.add(0)
        start(self.second)

    def to_third(self):
        wait(self.second)
        self.add(1)
        start(self.third)

    def to_across(self):
        wait(self.third)
        self.add(2)
        start(self.across)

    def to_back(self):
        wait(self.across)
        total = self.pack[(self.z,) + self.places].astype(jnp.float32)
        for t in range(self.lands[3].shape[0]):
            total = total + self.lands[3][t].astype(jnp.float32)
        self.out[(self.own,) + self.places] = total.astype(jnp.bfloat16)
        start(self.across_back if self.whole else self.third_back)

    def to_third_back(self):
        if self.whole:
            wait(self.across_back)
            start(self.third_back)

    def to_second_back(self):
        wait(self.third_back)
        start(self.second_back)

    def to_core_back(self):
        wait(self.second_back)
        start(self.core_back)

    def finish(self):
        wait(self.core_back)


def layer_kernel(names, *refs):
    k = SimpleNamespace(**dict(zip(names, refs)))
    p = lax.axis_index("dp")
    z = lax.axis_index("mp")
    k.z = z
    core, x, y = p % 2, (p // 2) % 2, p // 4
    to_core, to_x, to_y = ({"dp": flip(p, bit)} for bit in (1, 2, 4))
    across = [{"mp": flip_both(z, t)} for t in (1, 2, 3)]

    barrier = pltpu.get_barrier_semaphore()
    for peer in [to_core, to_x, to_y] + across:
        pl.semaphore_signal(barrier, inc=1, device_id=peer, device_id_type=pl.DeviceIdType.MESH)
    pl.semaphore_wait(barrier, 6)

    links = Links(k)

    def to_sequences(source, target):
        first = links.take(3)
        sends = [
            links.copy(first + t, source.at[peer["mp"]], target.at[z], peer)
            for t, peer in enumerate(across)
        ]
        own = links.here(source.at[z], target.at[z])
        start(sends + [own])
        return (first, sends, own)

    tokens = to_sequences(k.tok_in, k.tok)
    here = [
        links.here(source, target)
        for source, target in (
            (k.w_qkv_in, k.w_qkv),
            (k.sort_query_in, k.sort_query),
            (k.sort_key_in, k.sort_key),
            (k.w_out_in, k.w_out),
            (k.w_in_in, k.w_in.at[z]),
            (k.w_back_in, k.w_back.at[z]),
            (k.in_bias_in, k.in_bias.at[z]),
        )
    ]
    start(here)
    weights = []
    for peer in across:
        weights += [
            links.copy(links.take(1), k.w_in_in.at[core, x, y], k.w_in.at[z, core, x, y], peer),
            links.copy(
                links.take(1), k.w_back_in.at[core, y, x], k.w_back.at[z, core, y, x], peer
            ),
            links.copy(links.take(1), k.in_bias_in, k.in_bias.at[z], peer),
        ]
    start(weights)
    segments = to_sequences(k.seg_in, k.seg)
    k.sums[...] = jnp.zeros_like(k.sums)
    wait(here[:1])

    def arrived(t):
        @pl.when(t == 0)
        def _():
            tokens[2].wait()

        for step, copy in enumerate(tokens[1], 1):

            @pl.when(t == step)
            def _():
                copy.wait()

        return flip_both(z, t)

    first_norm(k, arrived)
    cotangents = to_sequences(k.cot_in, k.cot)

    def pass_on(pick):
        copies = []
        for peer in across:
            m = peer["mp"]
            for source, peer_at in pick(m):
                copies.append(links.copy(links.take(1), source, source, peer_at))
        start(copies)
        return copies

    wait(weights)
    weights = pass_on(
        lambda m: (
            (k.w_in.at[m, core, x, y], to_x),
            (k.w_back.at[m, core, y, x], to_y),
        )
    )
    wait(here[1:3])
    sort_plan(k)
    wait(weights)
    weights = pass_on(
        lambda m: (
            (k.w_in.at[m, core, :, y], to_y),
            (k.w_back.at[m, core, :, x], to_x),
        )
    )
    sort_forward(k)
    wait(segments[1] + [segments[2]])
    blocks = k.mixed.shape[0]
    attend(k, 0, blocks // 2)
    wait(weights)
    weights = pass_on(lambda m: ((k.w_in.at[m, core], to_core), (k.w_back.at[m, core], to_core)))
    attend(k, blocks // 2, blocks)
    wait(here[3:])
    second_norm(k)
    wait(cotangents[1] + [cotangents[2]])

    order_x = ((core, to_core), (x, to_x), (y, to_y))
    order_y = ((core, to_core), (y, to_y), (x, to_x))
    lands = lambda name: [getattr(k, name + str(level)) for level in range(4)]
    ff_in = Reduction(
        links, k.ff_in, lands("ff_in_land"), k.ff_in_out, order_x, across, z, False, True
    )
    ff_back = Reduction(
        links, k.ff_back, lands("ff_back_land"), k.ff_back_out, order_y, across, z, False, True
    )
    qkv = Reduction(links, k.qkv, lands("qkv_land"), k.qkv_out, order_x, across, z, True, False)
    rest = Reduction(links, k.rest, lands("rest_land"), k.rest_out, order_y, across, z, True, False)

    @pl.loop(0, k.w_in.shape[0])
    def _(t):
        @pl.when(t == 1)
        def _():
            wait(weights)

        c = flip_both(z, t)
        feed_forward(k, c)
        ff_in.core_part(c, t).start()
        ff_back.core_part(c, t).start()

    def to_positions(target):
        first = links.take(3)
        sends = [
            links.copy(first + t, k.stage.at[peer["mp"]], target.at[z], peer)
            for t, peer in enumerate(across)
        ]
        own = links.here(k.stage.at[z], target.at[z])

        def leave(t):
            for step, copy in enumerate(sends):

                @pl.when(t == step)
                def _():
                    copy.start()

            @pl.when(t == len(sends))
            def _():
                own.start()

        return (leave, sends + [own])

    def order(t):
        return flip_both(z, (t + 1) % 4)

    leave, outs = to_positions(k.out_land)
    second_norm_back(k, order, leave)
    for t in range(k.w_in.shape[0]):
        c = flip_both(z, t)
        wait([ff_in.core_part(c, t), ff_back.core_part(c, t)])
    both = (ff_in, ff_back)
    for each in both:
        each.core = []
        each.to_second()
    attend_back(k, 0, blocks // 2)
    for each in both:
        each.to_third()
    attend_back(k, blocks // 2, blocks)
    for each in both:
        each.to_across()
    sort_back(k)
    first_weights(k)
    start(qkv.core)
    for each in both:
        each.to_back()
    wait(outs)
    plan_back(k)
    start(rest.core)
    qkv.to_second()
    leave, outs = to_positions(k.tokens_land)
    for each in both:
        each.to_second_back()
    first_norm_back(k, order, leave)
    rest.to_second()
    sums = [
        [links.copy(links.take(1), k.sums, k.sums_land.at[at], peer)]
        for at, peer in enumerate((to_core, to_x, to_y))
    ]
    sums_across = [
        links.copy(links.take(1), k.sums, k.sums_land.at[3 + t], peer)
        for t, peer in enumerate(across)
    ]

    def add_sums(at):
        wait(sums[at])
        k.sums[...] += k.sums_land[at]

    start(sums[0])
    qkv.to_third()
    add_sums(0)
    start(sums[1])
    for each in both:
        each.to_core_back()
    rest.to_third()
    add_sums(1)
    start(sums[2])
    qkv.to_across()
    add_sums(2)
    start(sums_across)
    rest.to_across()
    qkv.to_back()
    rest.to_back()
    wait(sums_across)
    total = (k.sums[...] + k.sums_land[3]) + (k.sums_land[4] + k.sums_land[5])
    k.sums_land[0] = total
    k.vectors[...] = total
    k.vectors[6:7, :] = k.sums_land[0, pl.ds(8 + z, 1), :]
    for each in both:
        each.finish()
    qkv.to_third_back()
    rest.to_third_back()
    qkv.to_second_back()
    rest.to_second_back()
    qkv.to_core_back()
    rest.to_core_back()
    qkv.finish()
    rest.finish()
    wait(outs)


FAR = (
    "tok_in",
    "cot_in",
    "seg_in",
    "w_qkv_in",
    "w_out_in",
    "sort_query_in",
    "sort_key_in",
    "w_in_in",
    "w_back_in",
    "in_bias_in",
)
NEAR = (
    "mask",
    "gain_one",
    "shift_one",
    "out_bias",
    "gain_two",
    "shift_two",
    "back_bias",
)


def buffers_of(parts, chunk_rows, width, units):
    blocks = parts * chunk_rows // BLOCK
    groups = width // GROUP_LANES
    stacked = GROUP_LANES // (width // HEADS) * BLOCK
    rows = (parts, chunk_rows, width)
    in_blocks = (blocks, BLOCK, width)
    small = (blocks, HEADS, blocks)
    plans = (groups, GROUP_LANES, HEADS // groups * GROUP_LANES)
    low, full = jnp.bfloat16, jnp.float32
    ff_in = (1, width // 8, units)
    ff_back = (1, units // 8, width)
    square = (3, width // (8 * parts), width)
    far = dict(out_land=(rows, low), tokens_land=(rows, low))
    near = dict(
        qkv_out=((parts, 2, 2, 2) + square, low),
        rest_out=((parts, 2, 2, 2) + square, low),
        ff_in_out=((1, 2, 2, 2) + ff_in, low),
        ff_back_out=((1, 2, 2, 2) + ff_back, low),
        vectors=((16, width), full),
    )
    scratch = dict(
        tok=(rows, low),
        cot=(rows, low),
        seg=((parts, 8, 2 * BLOCK), full),
        w_qkv=((width, 3 * width), low),
        w_out=((width, width), low),
        sort_query=((width, width), low),
        sort_key=((width, width), low),
        w_in=((parts, 2, 2, 2, width // 8, units), low),
        w_back=((parts, 2, 2, 2, units // 8, width), low),
        in_bias=((parts, 8, units), full),
        means=((parts, chunk_rows // BLOCK, width), full),
        normed_low=(rows, low),
        mixed=((blocks, BLOCK, 3 * width), low),
        summary=((blocks, width), full),
        sort_q=((blocks, width), full),
        sort_k=((blocks, width), full),
        allowed=(small, full),
        log_plans=((2 * ITERS,) + small, full),
        grad_plan=(small, full),
        plan_wide=(plans, low),
        plan_tall=(plans, low),
        sorted=((blocks, BLOCK, 2 * width), low),
        weights=((blocks, groups, stacked, 2 * BLOCK), full),
        attended=(in_blocks, low),
        hidden=(rows, full),
        normed_two=(rows, low),
        out_sum=(in_blocks, full),
        grad_normed=(in_blocks, full),
        active=((parts, chunk_rows, units), low),
        grad_pre=((parts, chunk_rows, units), low),
        grad_low=(rows, low),
        grad_attended=(in_blocks, low),
        stage=(rows, low),
        sums=((16, width), full),
        sums_land=((6, 16, width), full),
    )
    for name, piece in (("ff_in", ff_in), ("ff_back", ff_back), ("qkv", square), ("rest", square)):
        scratch[name] = ((parts, 2, 2, 2) + piece, low)
        scratch[name + "_land0"] = ((parts, 2, 2) + piece, low)
        scratch[name + "_land1"] = ((parts, 2) + piece, low)
        scratch[name + "_land2"] = ((parts,) + piece, low)
        scratch[name + "_land3"] = ((parts - 1,) + piece, low)
    return (far, near, scratch)


def layer_call(inputs):
    parts, chunk_rows, width = inputs["tok_in"].shape
    units = inputs["w_in_in"].shape[-1]
    far, near, scratch = buffers_of(parts, chunk_rows, width, units)
    outs = far | near
    in_vmem = pl.BlockSpec(memory_space=pltpu.VMEM)
    anywhere = pl.BlockSpec(memory_space=pl.ANY)
    results = pl.pallas_call(
        partial(layer_kernel, FAR + NEAR + tuple(outs) + tuple(scratch) + ("send", "recv", "local")),
        out_shape=[jax.ShapeDtypeStruct(*entry) for entry in outs.values()],
        in_specs=[anywhere] * len(FAR) + [in_vmem] * len(NEAR),
        out_specs=[anywhere] * len(far) + [in_vmem] * len(near),
        scratch_shapes=[pltpu.VMEM(*entry) for entry in scratch.values()]
        + [
            pltpu.SemaphoreType.DMA((COPIES,)),
            pltpu.SemaphoreType.DMA((COPIES,)),
            pltpu.SemaphoreType.DMA((LOCAL_COPIES,)),
        ],
        compiler_params=pltpu.CompilerParams(
            collective_id=0, has_side_effects=True, vmem_limit_bytes=VMEM_BYTES
        ),
        name="layer",
    )(*[inputs[name] for name in FAR + NEAR])
    return dict(zip(outs, results))


def widen_kernel(out, tokens, qkv, rest, ff_in, ff_back, vectors, *results):
    wide = lambda array: array.astype(jnp.float32)
    layer_out, grad_tokens, grad_qkv, grad_w_out, grad_sq, grad_sk, grad_w_in, grad_w_back = results[:8]
    layer_out[...] = wide(out[...])
    grad_tokens[...] = wide(tokens[...])
    width = grad_w_out.shape[1]
    matrix = lambda pack, at: wide(pack[0, :, :, :, at]).reshape(-1, width)
    for at in range(3):
        grad_qkv[:, at * width : (at + 1) * width] = matrix(qkv, at)
    for at, result in enumerate((grad_w_out, grad_sq, grad_sk)):
        result[...] = matrix(rest, at)
    grad_w_in[...] = wide(ff_in[...])
    grad_w_back[...] = wide(ff_back[...])
    for at, result in enumerate(results[8:]):
        result[...] = vectors[at : at + 1, :]


def widen_call(results):
    parts, chunk_rows, width = results["out_land"].shape
    units = results["ff_in_out"].shape[-1]
    square = (width, width)
    ins = [
        results["out_land"],
        results["tokens_land"],
        results["qkv_out"],
        results["rest_out"],
        results["ff_in_out"].reshape(width, units),
        results["ff_back_out"].reshape(units, width),
        results["vectors"],
    ]
    shapes = [ins[0].shape, ins[1].shape, (width, 3 * width), square, square, square]
    shapes += [(width, units), (units, width)] + [(1, width)] * 6 + [(1, units)]

    def part_of(shape):
        if shape[0] < parts or shape == ins[-1].shape:
            return pl.BlockSpec(shape, lambda i: (0,) * len(shape))
        return pl.BlockSpec(
            (shape[0] // parts,) + shape[1:], lambda i: (i,) + (0,) * (len(shape) - 1)
        )

    return pl.pallas_call(
        widen_kernel,
        grid=(parts,),
        out_shape=[jax.ShapeDtypeStruct(shape, jnp.float32) for shape in shapes],
        in_specs=[part_of(array.shape) for array in ins],
        out_specs=[part_of(shape) for shape in shapes],
        compiler_params=pltpu.CompilerParams(vmem_limit_bytes=VMEM_BYTES),
        name="widen",
    )(*ins)


def per_sequence(
    tokens,
    segment_ids,
    block_mask,
    gain_one,
    shift_one,
    w_qkv,
    w_out,
    out_bias,
    sort_query,
    sort_key,
    gain_two,
    shift_two,
    input_weight,
    in_bias,
    output_weight,
    back_bias,
    cotangent,
):
    parts, chunk_rows, width = tokens.shape
    units = input_weight.shape[1]
    row = lambda vector: vector.reshape(1, -1)
    ids = segment_ids.astype(jnp.float32).reshape(parts, chunk_rows // BLOCK, BLOCK)
    bias = in_bias.astype(jnp.float32)
    results = layer_call(
        dict(
            tok_in=tokens,
            cot_in=cotangent,
            seg_in=jnp.pad(ids, ((0, 0), (0, 8 - chunk_rows // BLOCK), (BLOCK, 0))),
            w_qkv_in=w_qkv,
            w_out_in=w_out,
            sort_query_in=sort_query,
            sort_key_in=sort_key,
            w_in_in=input_weight.reshape(2, 2, 2, width // 8, units),
            w_back_in=output_weight.reshape(2, 2, 2, units // 8, width),
            in_bias_in=jnp.broadcast_to(bias, (8, units)),
            mask=block_mask,
            gain_one=row(gain_one),
            shift_one=row(shift_one),
            out_bias=row(out_bias),
            gain_two=row(gain_two),
            shift_two=row(shift_two),
            back_bias=row(back_bias),
        )
    )
    wide = widen_call(results)
    flat = [array.reshape(-1) for array in wide[8:]]
    gain_two, shift_two, back_bias, out_bias, gain_one, shift_one, in_bias = flat
    layer_out, grad_tokens, grad_qkv, grad_w_out, grad_sq, grad_sk, grad_w_in, grad_w_back = wide[:8]
    return (
        layer_out,
        grad_tokens,
        gain_one,
        shift_one,
        grad_qkv,
        grad_w_out,
        out_bias,
        grad_sq,
        grad_sk,
        gain_two,
        shift_two,
        grad_w_in,
        in_bias,
        grad_w_back,
        back_bias,
    )


def solution(mesh):
    in_specs = (
        P("dp", "mp", None),
        P("dp", "mp"),
        P("dp", None, None),
        P(),
        P(),
        P(),
        P(),
        P(),
        P(),
        P(),
        P(),
        P(),
        P(None, "mp"),
        P("mp"),
        P("mp", None),
        P(),
        P("dp", "mp", None),
    )
    out_specs = (
        P("dp", "mp", None),
        P("dp", "mp", None),
        P(),
        P(),
        P(),
        P(),
        P(),
        P(),
        P(),
        P(),
        P(),
        P(None, "mp"),
        P("mp"),
        P("mp", None),
        P(),
    )

    def per_shard(tokens, *others):
        sizes = (mesh.shape["dp"], mesh.shape["mp"])
        sequences, positions, width = tokens.shape
        whole = sizes == (8, 4) and sequences == 4
        whole = whole and (positions, width) == (256, 512)
        return (per_sequence if whole else per_device)(tokens, *others)

    return jax.shard_map(
        per_shard, mesh=mesh, in_specs=in_specs, out_specs=out_specs, check_vma=False
    )
```

```python
from functools import partial
from types import SimpleNamespace

import jax
import jax.numpy as jnp
from jax import lax
from jax.experimental import pallas as pl
from jax.experimental.pallas import tpu as pltpu
from jax.sharding import PartitionSpec as P

HEADS = 8
BLOCK = 64
ITERS = 8
VMEM_BYTES = 62 * 2**20
COPIES = 160
LOCAL_COPIES = 16
UNROLL = 4
TEMPER = 0.75
EPSILON = 1e-05
HIGH = lax.Precision.HIGHEST


def norm_stats(source):
    centred = source - jnp.mean(source, axis=-1, keepdims=True)
    inverse = lax.rsqrt(jnp.mean(centred * centred, axis=-1, keepdims=True) + EPSILON)
    return (centred * inverse, inverse)


def norm_back(grad_out, unit_rows, inverse, gain_vec):
    scaled = grad_out * gain_vec
    first_mean = jnp.mean(scaled, axis=-1, keepdims=True)
    second_mean = jnp.mean(scaled * unit_rows, axis=-1, keepdims=True)
    return inverse * (scaled - first_mean - unit_rows * second_mean)


def exact_gelu(pre_act):
    return jax.nn.gelu(pre_act, approximate=False)


def transport_plan(sort_q, sort_k, allowed):
    seq_count, blocks, model_width = sort_q.shape
    head_size = model_width // HEADS
    query_heads = sort_q.reshape(seq_count, blocks, HEADS, head_size)
    key_heads = sort_k.reshape(seq_count, blocks, HEADS, head_size)
    logits = jnp.einsum("sihe,sjhe->shij", query_heads, key_heads, precision=HIGH) * head_size ** (
        -0.5
    )
    log_plan = jnp.where(allowed[:, None], logits / TEMPER, -1000000000.0)
    for sweep_index in range(ITERS):
        log_plan = log_plan - jax.nn.logsumexp(log_plan, axis=-1, keepdims=True)
        log_plan = log_plan - jax.nn.logsumexp(log_plan, axis=-2, keepdims=True)
    return jnp.exp(log_plan)


def per_device(
    tokens,
    segment_ids,
    block_mask,
    gain_one,
    shift_one,
    w_qkv,
    w_out,
    out_bias,
    sort_query,
    sort_key,
    gain_two,
    shift_two,
    input_weight,
    in_bias,
    output_weight,
    back_bias,
    cotangent,
):
    seq_count, shard_len, model_width = tokens.shape
    head_size = model_width // HEADS
    local_blocks = shard_len // BLOCK
    all_blocks = block_mask.shape[1]
    first_block = lax.axis_index("mp") * local_blocks
    scale_factor = head_size ** (-0.5)
    token_rows = seq_count * shard_len
    pair_shape = (seq_count, local_blocks, BLOCK, 2, HEADS, head_size)
    source = tokens.astype(jnp.float32)
    unit_one, inverse_one = norm_stats(source)
    normed_one = unit_one * gain_one + shift_one
    normed_low = normed_one.astype(jnp.bfloat16).reshape(token_rows, model_width)
    mixed_rows = jnp.dot(normed_low, w_qkv, preferred_element_type=jnp.float32).astype(jnp.bfloat16)
    mixed_rows = mixed_rows.reshape(seq_count, local_blocks, BLOCK, 3, HEADS, head_size)
    queries = mixed_rows[:, :, :, 0]
    key_value = mixed_rows[:, :, :, 1:]
    pair_flat = key_value.reshape(seq_count, local_blocks, BLOCK, 2 * model_width)
    summary_low = jnp.mean(
        normed_one.reshape(seq_count, local_blocks, BLOCK, model_width), axis=2
    ).astype(jnp.bfloat16)
    summary_all = lax.all_gather(summary_low, "mp", axis=1, tiled=True)
    sort_q = jnp.dot(summary_all, sort_query, preferred_element_type=jnp.float32)
    sort_k = jnp.dot(summary_all, sort_key, preferred_element_type=jnp.float32)
    diagonal = jnp.arange(all_blocks)[:, None] == jnp.arange(all_blocks)[None, :]
    allowed = (block_mask == 1) | diagonal[None]
    plan_full, plan_back = jax.vjp(partial(transport_plan, allowed=allowed), sort_q, sort_k)
    plan_local = lax.dynamic_slice_in_dim(plan_full, first_block, local_blocks, 2).astype(
        jnp.bfloat16
    )
    pair_all = lax.all_gather(pair_flat, "mp", axis=1, tiled=True).reshape(
        seq_count, all_blocks, BLOCK, 2, HEADS, head_size
    )
    sorted_pair = jnp.einsum(
        "shij,sjbchd->sibchd", plan_local, pair_all, preferred_element_type=jnp.float32
    )
    sorted_low = sorted_pair.astype(jnp.bfloat16)
    key_cat = jnp.concatenate([sorted_low[:, :, :, 0], key_value[:, :, :, 0]], axis=2)
    value_cat = jnp.concatenate([sorted_low[:, :, :, 1], key_value[:, :, :, 1]], axis=2)
    segment_blocks = segment_ids.reshape(seq_count, local_blocks, BLOCK)
    same_doc = segment_blocks[:, :, :, None] == segment_blocks[:, :, None, :]
    keep_mask = jnp.concatenate([jnp.ones_like(same_doc), same_doc], axis=-1)[:, :, None]
    raw_scores = (
        jnp.einsum("sibhd,sikhd->sihbk", queries, key_cat, preferred_element_type=jnp.float32)
        * scale_factor
    )
    scores = jnp.where(keep_mask, raw_scores, -1000000000.0)
    weights_soft = jax.nn.softmax(scores, axis=-1)
    weights_low = weights_soft.astype(jnp.bfloat16)
    attended = jnp.einsum(
        "sihbk,sikhd->sibhd", weights_low, value_cat, preferred_element_type=jnp.float32
    )
    attended_low = attended.astype(jnp.bfloat16).reshape(token_rows, model_width)
    projected = jnp.dot(attended_low, w_out, preferred_element_type=jnp.float32) + out_bias
    hidden = source + projected.reshape(seq_count, shard_len, model_width)
    unit_two, inverse_two = norm_stats(hidden)
    normed_two = (unit_two * gain_two + shift_two).astype(jnp.bfloat16)
    cot_float = cotangent.astype(jnp.float32)
    gathered_rows = lax.all_gather(normed_two, "mp", axis=1, tiled=True)
    pre_act = jnp.dot(
        gathered_rows, input_weight, preferred_element_type=jnp.float32
    ) + in_bias.astype(jnp.float32)
    active_float, gelu_back = jax.vjp(exact_gelu, pre_act)
    activated_hidden = active_float.astype(jnp.bfloat16)
    partial_out = jnp.dot(activated_hidden, output_weight, preferred_element_type=jnp.float32)
    ffn_out = lax.psum_scatter(
        partial_out.astype(jnp.bfloat16), "mp", scatter_dimension=1, tiled=True
    ).astype(jnp.float32)
    cotangent_gathered = lax.all_gather(cotangent, "mp", axis=1, tiled=True)
    grad_activated_hidden = jnp.einsum(
        "mci,ni->mcn", cotangent_gathered, output_weight, preferred_element_type=jnp.float32
    )
    grad_pre = gelu_back(grad_activated_hidden)[0]
    grad_preactivation_rounded = grad_pre.astype(jnp.bfloat16)
    local_w_in = jnp.einsum(
        "rjy,rjq->yq", gathered_rows, grad_preactivation_rounded, preferred_element_type=jnp.float32
    )
    local_in_bias = jnp.sum(grad_pre, axis=(0, 1))
    local_output_weight = jnp.einsum(
        "wko,wkp->op", activated_hidden, cotangent_gathered, preferred_element_type=jnp.float32
    )
    grad_normed_two = lax.psum_scatter(
        jnp.einsum(
            "giv,cv->gic",
            grad_preactivation_rounded,
            input_weight,
            preferred_element_type=jnp.float32,
        ),
        "mp",
        scatter_dimension=1,
        tiled=True,
    )
    grad_w_in, grad_in_bias, grad_w_back = (
        lax.psum(local_w_in.astype(jnp.bfloat16), "dp").astype(jnp.float32),
        lax.psum(local_in_bias.astype(jnp.bfloat16), "dp").astype(jnp.float32),
        lax.psum(local_output_weight.astype(jnp.bfloat16), "dp").astype(jnp.float32),
    )
    layer_out = hidden + ffn_out + back_bias
    grad_hidden = cot_float + norm_back(grad_normed_two, unit_two, inverse_two, gain_two)
    grad_gain_two = jnp.sum(grad_normed_two * unit_two, axis=(0, 1))
    grad_shift_two = jnp.sum(grad_normed_two, axis=(0, 1))
    grad_back_bias = jnp.sum(cot_float, axis=(0, 1))
    grad_out_bias = jnp.sum(grad_hidden, axis=(0, 1))
    grad_proj_low = grad_hidden.astype(jnp.bfloat16).reshape(token_rows, model_width)
    grad_w_out = jnp.einsum(
        "td,te->de", attended_low, grad_proj_low, preferred_element_type=jnp.float32
    )
    grad_attended = jnp.einsum(
        "te,de->td", grad_proj_low, w_out, preferred_element_type=jnp.float32
    )
    grad_attended = grad_attended.astype(jnp.bfloat16).reshape(
        seq_count, local_blocks, BLOCK, HEADS, head_size
    )
    grad_weights = jnp.einsum(
        "sibhd,sikhd->sihbk", grad_attended, value_cat, preferred_element_type=jnp.float32
    )
    grad_value_cat = jnp.einsum(
        "sihbk,sibhd->sikhd", weights_low, grad_attended, preferred_element_type=jnp.float32
    )
    grad_scores = weights_soft * (
        grad_weights - jnp.sum(grad_weights * weights_soft, axis=-1, keepdims=True)
    )
    grad_scores_low = grad_scores.astype(jnp.bfloat16)
    grad_queries = (
        jnp.einsum(
            "sihbk,sikhd->sibhd", grad_scores_low, key_cat, preferred_element_type=jnp.float32
        )
        * scale_factor
    )
    grad_key_cat = (
        jnp.einsum(
            "sihbk,sibhd->sikhd", grad_scores_low, queries, preferred_element_type=jnp.float32
        )
        * scale_factor
    )
    grad_sorted = jnp.stack(
        [grad_key_cat[:, :, :BLOCK], grad_value_cat[:, :, :BLOCK]], axis=3
    ).astype(jnp.bfloat16)
    grad_pair_own = jnp.stack([grad_key_cat[:, :, BLOCK:], grad_value_cat[:, :, BLOCK:]], axis=3)
    grad_plan = jnp.einsum(
        "sibchd,sjbchd->shij", grad_sorted, pair_all, preferred_element_type=jnp.float32
    )
    term = jnp.einsum(
        "shij,sibchd->jsbchd", plan_local, grad_sorted, preferred_element_type=jnp.float32
    )
    from_sorted = lax.psum_scatter(
        term.reshape(local_blocks * lax.axis_size("mp"), seq_count, BLOCK, 2 * model_width).astype(
            jnp.bfloat16
        ),
        "mp",
        scatter_dimension=0,
        tiled=True,
    ).astype(jnp.float32)
    from_sorted = jnp.moveaxis(from_sorted, 0, 1).reshape(pair_shape)
    grad_pair = grad_pair_own + from_sorted
    grad_mixed = jnp.concatenate([grad_queries[:, :, :, None], grad_pair], axis=3)
    grad_mixed_low = grad_mixed.astype(jnp.bfloat16).reshape(token_rows, 3 * model_width)
    grad_qkv = jnp.einsum(
        "td,te->de", normed_low, grad_mixed_low, preferred_element_type=jnp.float32
    )
    grad_plan_all = lax.all_gather(grad_plan.astype(jnp.bfloat16), "mp", axis=2, tiled=True).astype(
        grad_plan.dtype
    )
    grad_sq_all, grad_sk_all = plan_back(grad_plan_all)
    grad_sq = lax.dynamic_slice_in_dim(grad_sq_all, first_block, local_blocks, 1)
    grad_sk = lax.dynamic_slice_in_dim(grad_sk_all, first_block, local_blocks, 1)
    summary_float = summary_low.astype(jnp.float32)
    grad_sort_query = jnp.einsum("sid,sie->de", summary_float, grad_sq, precision=HIGH)
    grad_sort_key = jnp.einsum("sid,sie->de", summary_float, grad_sk, precision=HIGH)
    grad_summary = jnp.einsum(
        "sie,de->sid", grad_sq, sort_query.astype(jnp.float32), precision=HIGH
    ) + jnp.einsum("sie,de->sid", grad_sk, sort_key.astype(jnp.float32), precision=HIGH)
    spread_summary = jnp.broadcast_to(
        (grad_summary / BLOCK)[:, :, None, :], (seq_count, local_blocks, BLOCK, model_width)
    ).reshape(seq_count, shard_len, model_width)
    grad_normed_one = jnp.einsum(
        "te,de->td", grad_mixed_low, w_qkv, preferred_element_type=jnp.float32
    )
    grad_normed_one = grad_normed_one.reshape(seq_count, shard_len, model_width) + spread_summary
    grad_gain_one = jnp.sum(grad_normed_one * unit_one, axis=(0, 1))
    grad_shift_one = jnp.sum(grad_normed_one, axis=(0, 1))
    grad_tokens = grad_hidden + norm_back(grad_normed_one, unit_one, inverse_one, gain_one)
    (
        grad_gain_one,
        grad_shift_one,
        grad_qkv,
        grad_w_out,
        grad_out_bias,
        grad_sort_query,
        grad_sort_key,
        grad_gain_two,
        grad_shift_two,
        grad_back_bias,
    ) = lax.psum(
        (
            grad_gain_one,
            grad_shift_one,
            grad_qkv,
            grad_w_out,
            grad_out_bias,
            grad_sort_query,
            grad_sort_key,
            grad_gain_two,
            grad_shift_two,
            grad_back_bias,
        ),
        ("dp", "mp"),
    )
    return (
        layer_out,
        grad_tokens,
        grad_gain_one,
        grad_shift_one,
        grad_qkv,
        grad_w_out,
        grad_out_bias,
        grad_sort_query,
        grad_sort_key,
        grad_gain_two,
        grad_shift_two,
        grad_w_in,
        grad_in_bias,
        grad_w_back,
        grad_back_bias,
    )


GROUP_LANES = 256


def dot(left, right, contract=((1,), (0,)), precision=None):
    return lax.dot_general(
        left,
        right,
        (contract, ((), ())),
        precision=precision,
        preferred_element_type=jnp.float32,
    )


def dot_right_t(left, right, precision=None):
    return dot(left, right, ((1,), (1,)), precision)


def dot_left_t(left, right, precision=None):
    return dot(left, right, ((0,), (0,)), precision)


def row_sum(array):
    return jnp.sum(array, axis=0, keepdims=True)


def head_lanes(head_size):
    lane_head = lax.broadcasted_iota(jnp.int32, (1, GROUP_LANES), 1) // head_size
    return [lane_head == h for h in range(GROUP_LANES // head_size)]


def spread_heads(rows, lanes, amount=1.0):
    return jnp.concatenate(
        [rows * jnp.where(keep, amount, 0.0).astype(rows.dtype) for keep in lanes], axis=0
    )


def fold_heads(stacked, lanes):
    rows = stacked.shape[0] // len(lanes)
    total = stacked[:rows]
    for h, keep in enumerate(lanes[1:], 1):
        total = jnp.where(keep, stacked[h * rows : (h + 1) * rows], total)
    return total


def norm_parts(source):
    centred = source - jnp.mean(source, axis=-1, keepdims=True)
    inverse = lax.rsqrt(jnp.mean(centred * centred, axis=-1, keepdims=True) + EPSILON)
    return (centred * inverse, inverse)


def chunk_blocks(r, some):
    return pl.ds(r * some, some)


def first_norm(k, r):
    _, chunk_rows, width = k.tok.shape
    some = chunk_rows // BLOCK
    unit, _ = norm_parts(k.tok[r].astype(jnp.float32))
    normed = unit * k.gain_one[...] + k.shift_one[...]
    k.means[r] = jnp.mean(normed.reshape(some, BLOCK, width), axis=1)
    low = normed.astype(jnp.bfloat16)
    k.normed_low[r] = low
    mixed = dot(low, k.w_qkv[...]).astype(jnp.bfloat16)
    k.mixed[chunk_blocks(r, some)] = mixed.reshape(some, BLOCK, 3 * width)


def head_rows(rows, head_size):
    blocks, width = rows.shape
    shape = (blocks, HEADS, width)
    mine = lax.broadcasted_iota(jnp.int32, shape, 1) == (
        lax.broadcasted_iota(jnp.int32, shape, 2) // head_size
    )
    return jnp.where(mine, rows[:, None, :], 0.0).reshape(blocks * HEADS, width)


def sort_plan(k):
    width = k.tok.shape[2]
    head_size = width // HEADS
    blocks = k.mixed.shape[0]
    summary = k.means[...].reshape(blocks, width).astype(jnp.bfloat16)
    sort_q = dot(summary, k.sort_query[...])
    sort_k = dot(summary, k.sort_key[...])
    k.summary_all[k.place] = summary
    k.sort_q[...] = sort_q
    k.sort_k[...] = sort_k
    logits = dot_right_t(head_rows(sort_q, head_size), sort_k, HIGH) * head_size ** (-0.5)
    allowed = (k.mask[k.z] == 1) | (
        lax.broadcasted_iota(jnp.int32, (blocks, blocks), 0)
        == lax.broadcasted_iota(jnp.int32, (blocks, blocks), 1)
    )
    allowed = jnp.where(allowed, 1.0, 0.0)[:, None, :]
    k.allowed[...] = jnp.broadcast_to(allowed, (blocks, HEADS, blocks))
    log_plan = jnp.where(
        k.allowed[...] > 0.5, logits.reshape(blocks, HEADS, blocks) / TEMPER, -1000000000.0
    )

    def sweep(t, log_plan):
        for half, axis in enumerate((2, 0)):
            top = jnp.max(log_plan, axis=axis, keepdims=True)
            total = jnp.sum(jnp.exp(log_plan - top), axis=axis, keepdims=True)
            log_plan = log_plan - (top + jnp.log(total))
            k.log_plans[2 * t + half] = log_plan
        return log_plan

    plan = jnp.exp(lax.fori_loop(0, ITERS, sweep, log_plan))
    spread_plan(k, plan.reshape(blocks * HEADS, blocks))


def spread_plan(k, plan):
    rows, blocks = plan.shape
    side = GROUP_LANES
    part = side // blocks
    columns = (
        lax.broadcasted_iota(jnp.int32, (blocks, side), 1) // part
        == lax.broadcasted_iota(jnp.int32, (blocks, side), 0)
    ).astype(jnp.float32)
    wide = dot(plan.astype(jnp.bfloat16), columns.astype(jnp.bfloat16))
    tall = wide.T.astype(jnp.bfloat16)
    wide = wide.astype(jnp.bfloat16)
    same = (
        lax.broadcasted_iota(jnp.int32, (side, side), 0) % part
        == lax.broadcasted_iota(jnp.int32, (side, side), 1) % part
    )
    block_of = lax.broadcasted_iota(jnp.int32, (side, rows), 0) // part
    row_of = lax.broadcasted_iota(jnp.int32, (side, rows), 1)
    block_at = lax.broadcasted_iota(jnp.int32, (rows, side), 1) // part
    row_at = lax.broadcasted_iota(jnp.int32, (rows, side), 0)
    in_group = HEADS // k.plan_wide.shape[0]
    for h in range(HEADS):
        pick = (row_of == block_of * HEADS + h).astype(jnp.float32).astype(jnp.bfloat16)
        pick_t = (row_at == block_at * HEADS + h).astype(jnp.float32).astype(jnp.bfloat16)
        at = pl.ds((h % in_group) * side, side)
        k.plan_wide[h // in_group, :, at] = jnp.where(same, dot(pick, wide), 0.0).astype(
            jnp.bfloat16
        )
        k.plan_tall[h // in_group, :, at] = jnp.where(same, dot(tall, pick_t), 0.0).astype(
            jnp.bfloat16
        )


def mix_blocks(k, plan_ref, source, source_lane, groups, write):
    blocks, _, _ = source.shape
    width = k.tok.shape[2]
    part = GROUP_LANES // blocks
    lanes = head_lanes(width // HEADS)
    for c in range(BLOCK // part):
        for lane in range(0, 2 * width, GROUP_LANES):
            group = (lane % width) // GROUP_LANES
            if group not in groups:
                continue
            rows = source[:, pl.ds(c * part, part), pl.ds(source_lane + lane, GROUP_LANES)]
            rows = spread_heads(rows.reshape(GROUP_LANES, GROUP_LANES), lanes)
            mixed = dot(plan_ref[group], rows)
            write(c * part, part, lane, mixed.reshape(blocks, part, GROUP_LANES))


def sort_forward(k):
    def write(row, rows, lane, mixed):
        k.sorted[:, pl.ds(row, rows), pl.ds(lane, GROUP_LANES)] = mixed.astype(jnp.bfloat16)

    mix_blocks(k, k.plan_wide, k.mixed, k.tok.shape[2], range(k.plan_wide.shape[0]), write)


def block_parts(k, i, lane):
    width = k.tok.shape[2]
    queries = k.mixed[i, :, pl.ds(lane, GROUP_LANES)]
    keys = jnp.concatenate(
        [
            k.sorted[i, :, pl.ds(lane, GROUP_LANES)],
            k.mixed[i, :, pl.ds(width + lane, GROUP_LANES)],
        ],
        axis=0,
    )
    values = jnp.concatenate(
        [
            k.sorted[i, :, pl.ds(width + lane, GROUP_LANES)],
            k.mixed[i, :, pl.ds(2 * width + lane, GROUP_LANES)],
        ],
        axis=0,
    )
    return (queries, keys, values)


def attend(k):
    width = k.tok.shape[2]
    head_size = width // HEADS
    lanes = head_lanes(head_size)
    some = k.tok.shape[1] // BLOCK
    diagonal = lax.broadcasted_iota(jnp.int32, (BLOCK, 2 * BLOCK), 1) == (
        lax.broadcasted_iota(jnp.int32, (BLOCK, 2 * BLOCK), 0)
    )

    @pl.loop(0, k.mixed.shape[0], unroll=UNROLL)
    def _(i):
        ids = k.seg[i // some, pl.ds(i % some, 1), :]
        of_query = jnp.concatenate([ids] * (len(lanes) // 2), axis=1)
        of_key = jnp.sum(jnp.where(diagonal, ids, 0.0), axis=1, keepdims=True)
        keep = of_key == of_query
        for group in range(width // GROUP_LANES):
            lane = group * GROUP_LANES
            queries, keys, values = block_parts(k, i, lane)
            scores = dot_right_t(keys, spread_heads(queries, lanes, head_size ** (-0.5)))
            sorted_part = scores[:BLOCK]
            own_part = jnp.where(keep, scores[BLOCK:], -1000000000.0)
            top = jnp.maximum(
                jnp.max(sorted_part, axis=0, keepdims=True), jnp.max(own_part, axis=0, keepdims=True)
            )
            raised = jnp.exp(jnp.concatenate([sorted_part, own_part], axis=0) - top)
            weights = raised * (1.0 / row_sum(raised))
            k.weights[i, group] = weights
            mixed = fold_heads(dot_left_t(weights.astype(jnp.bfloat16), values), lanes)
            k.attended[i, :, pl.ds(lane, GROUP_LANES)] = mixed.astype(jnp.bfloat16)


def feed_forward(k):
    chunks, chunk_rows, width = k.tok.shape
    parts = k.w_in.shape[0]
    some = chunk_rows // BLOCK
    units = k.active.shape[3]

    @pl.loop(0, chunks)
    def _(r):
        at = chunk_blocks(r, some)
        projected = dot(k.attended[at].reshape(chunk_rows, width), k.w_out[...]) + k.out_bias[...]
        hidden = k.tok[r].astype(jnp.float32) + projected
        k.hidden[r] = hidden
        unit, _ = norm_parts(hidden)
        normed = (unit * k.gain_two[...] + k.shift_two[...]).astype(jnp.bfloat16)
        k.normed_two[r] = normed
        total = hidden + k.back_bias[...]
        for c in range(parts):
            pre = dot(normed, k.w_in[c].reshape(width, units)) + k.in_bias[c, 0:1, :]
            cdf = 0.5 + 0.5 * lax.erf(pre * 0.5**0.5)
            active = (pre * cdf).astype(jnp.bfloat16)
            slope = cdf + pre * (jnp.exp(pre * pre * -0.5) * 0.3989422804014327)
            k.active[c, at] = active.reshape(some, BLOCK, units)
            k.slope[c, r] = slope.astype(jnp.bfloat16)
            total = total + dot(active, k.w_back[c].reshape(units, width))
        k.stage[r] = total.astype(jnp.bfloat16)


def feed_back(k, arrived):
    chunks, chunk_rows, width = k.tok.shape
    parts = k.w_in.shape[0]
    some = chunk_rows // BLOCK
    units = k.active.shape[3]

    def rows(t, sums):
        r = arrived(t)
        at = chunk_blocks(r, some)
        out_grad = k.cot[r]
        grad_normed = jnp.zeros((chunk_rows, width), jnp.float32)
        terms = []
        for c in range(parts):
            grad = dot_right_t(out_grad, k.w_back[c].reshape(units, width))
            grad = grad * k.slope[c, r].astype(jnp.float32)
            low = grad.astype(jnp.bfloat16)
            k.slope[c, r] = low
            grad_normed = grad_normed + dot_right_t(low, k.w_in[c].reshape(width, units))
            terms.append(grad)
        unit, inverse = norm_parts(k.hidden[r])
        out_grad = out_grad.astype(jnp.float32)
        grad_hidden = out_grad + norm_grad(grad_normed, unit, inverse, k.gain_two[...])
        k.hidden[r] = grad_hidden
        low = grad_hidden.astype(jnp.bfloat16)
        k.grad_low[r] = low
        grad_attended = dot_right_t(low, k.w_out[...]).astype(jnp.bfloat16)
        k.grad_attended[at] = grad_attended.reshape(some, BLOCK, width)
        terms = [grad_normed * unit, grad_normed, out_grad, grad_hidden] + terms
        return tuple(total + row_sum(term) for total, term in zip(sums, terms))

    zeros = [jnp.zeros((1, width), jnp.float32)] * 4 + [jnp.zeros((1, units), jnp.float32)] * parts
    sums = lax.fori_loop(0, chunks, rows, tuple(zeros))
    for total, at in zip(sums, (0, 1, 2, 3, 8, 9, 10, 11)):
        k.sums[at : at + 1, :] = total


def feed_weights(k, c):
    units = k.active.shape[3]
    grads = k.slope[c].reshape(-1, units)
    k.ff_in[c] = as_pack(dot_left_t(whole_rows(k.normed_two), grads), k.ff_in.shape[1:])
    active = k.active[c].reshape(-1, units)
    k.ff_back[c] = as_pack(dot_left_t(active, whole_rows(k.cot)), k.ff_back.shape[1:])


def out_weights(k):
    grad = dot_left_t(whole_rows(k.attended), whole_rows(k.grad_low))
    for half in range(2):
        put_matrix(k.first, half, grad[:, half * GROUP_LANES : (half + 1) * GROUP_LANES])


def whole_rows(ref):
    return ref[...].reshape(-1, ref.shape[-1])


def as_pack(array, shape):
    return array.astype(jnp.bfloat16).reshape(shape)


def norm_grad(grad_out, unit, inverse, gain):
    scaled = grad_out * gain
    first = jnp.mean(scaled, axis=-1, keepdims=True)
    second = jnp.mean(scaled * unit, axis=-1, keepdims=True)
    return inverse * (scaled - first - unit * second)


def put_matrix(pack, at, matrix):
    shape = pack.shape[:4] + pack.shape[5:]
    pack[:, :, :, :, at] = as_pack(matrix, shape)


def attend_back(k, group, first, last):
    width = k.tok.shape[2]
    head_size = width // HEADS
    lanes = head_lanes(head_size)
    scale = head_size ** (-0.5)

    @pl.loop(first, last, unroll=UNROLL)
    def _(i):
        lane = group * GROUP_LANES
        queries, keys, values = block_parts(k, i, lane)
        queries = spread_heads(queries, lanes, scale)
        grad_out = spread_heads(k.grad_attended[i, :, pl.ds(lane, GROUP_LANES)], lanes)
        weights = k.weights[i, group]
        grad_weights = dot_right_t(values, grad_out)
        grad_values = dot(weights.astype(jnp.bfloat16), grad_out)
        inner = row_sum(grad_weights * weights)
        grad_scores = (weights * (grad_weights - inner)).astype(jnp.bfloat16)
        grad_queries = fold_heads(dot_left_t(grad_scores, keys), lanes) * scale
        grad_keys = dot(grad_scores, queries)
        place = pl.ds(lane, GROUP_LANES)
        k.mixed[i, :, place] = grad_queries.astype(jnp.bfloat16)
        k.sorted[i, :, place] = grad_keys[:BLOCK].astype(jnp.bfloat16)
        k.sorted[i, :, pl.ds(width + lane, GROUP_LANES)] = grad_values[:BLOCK].astype(
            jnp.bfloat16
        )
        k.weights[i, group] = jnp.concatenate([grad_keys[BLOCK:], grad_values[BLOCK:]], axis=0)


def mix_back(k, group):
    width = k.tok.shape[2]

    def write(row, rows, lane, mixed):
        half = lane // width
        own = k.weights[:, group, pl.ds(half * BLOCK + row, rows), :]
        k.active[half, :, pl.ds(row, rows), pl.ds(lane % width, GROUP_LANES)] = (
            own + mixed
        ).astype(jnp.bfloat16)

    mix_blocks(k, k.plan_tall, k.sorted, 0, (group,), write)


def plan_grad(k, group):
    width = k.tok.shape[2]
    blocks = k.mixed.shape[0]
    side = GROUP_LANES
    part = side // blocks
    lanes = head_lanes(width // HEADS)
    in_group = len(lanes)

    same = (
        lax.broadcasted_iota(jnp.int32, (side, side), 0) % part
        == lax.broadcasted_iota(jnp.int32, (side, side), 1) % part
    )
    fold_columns = (
        lax.broadcasted_iota(jnp.int32, (side, blocks), 0) // part
        == lax.broadcasted_iota(jnp.int32, (side, blocks), 1)
    ).astype(jnp.float32)
    total = jnp.zeros((in_group * side, side), jnp.float32)
    for c in range(BLOCK // part):
        at = pl.ds(c * part, part)
        lane = group * side
        grads, rows = (
            [
                ref[:, at, pl.ds(offset + lane, side)].reshape(side, side)
                for offset in (start_lane, start_lane + width)
            ]
            for ref, start_lane in ((k.sorted, 0), (k.mixed, width))
        )
        grads = jnp.concatenate([spread_heads(grad, lanes) for grad in grads], axis=1)
        total = total + dot_right_t(grads, jnp.concatenate(rows, axis=1))
    for h in range(in_group):
        picked = jnp.where(same, total[h * side : (h + 1) * side], 0.0)
        picked = jnp.sum(picked.reshape(blocks, part, side), axis=1)
        k.grad_plan[:, group * in_group + h, :] = dot(picked, fold_columns, precision=HIGH)


def plan_back(k):
    width = k.tok.shape[2]
    head_size = width // HEADS
    blocks = k.mixed.shape[0]
    grad = k.grad_plan[...] * jnp.exp(k.log_plans[2 * ITERS - 1])

    def sweep(t, grad):
        for half, axis in ((1, 0), (0, 2)):
            share = jnp.exp(k.log_plans[2 * (ITERS - 1 - t) + half])
            grad = grad - share * jnp.sum(grad, axis=axis, keepdims=True)
        return grad

    grad = lax.fori_loop(0, ITERS, sweep, grad)
    grad = jnp.where(k.allowed[...] > 0.5, grad / TEMPER, 0.0) * head_size ** (-0.5)
    grad = grad.reshape(blocks * HEADS, blocks)
    sort_q = k.sort_q[...]
    sort_k = k.sort_k[...]
    shape = (blocks, HEADS, width)
    mine = lax.broadcasted_iota(jnp.int32, shape, 1) == (
        lax.broadcasted_iota(jnp.int32, shape, 2) // head_size
    )
    grad_sq = dot(grad, sort_k, precision=HIGH).reshape(shape)
    grad_sq = jnp.sum(jnp.where(mine, grad_sq, 0.0), axis=1)
    grad_sk = dot_left_t(grad, head_rows(sort_q, head_size), HIGH)
    k.factors[k.place + (0,)] = grad_sq.astype(jnp.bfloat16)
    k.factors[k.place + (1,)] = grad_sk.astype(jnp.bfloat16)
    grad_summary = dot_right_t(grad_sq, k.sort_query[...].astype(jnp.float32), HIGH)
    grad_summary += dot_right_t(grad_sk, k.sort_key[...].astype(jnp.float32), HIGH)
    some = k.means.shape[1]
    k.means[...] = (grad_summary / BLOCK).reshape(blocks // some, some, width)


def first_weights(k, group, pack, first):
    rows = whole_rows(k.normed_low)
    lanes = pl.ds(group * GROUP_LANES, GROUP_LANES)
    grads = (k.mixed[:, :, lanes], k.active[0, :, :, lanes], k.active[1, :, :, lanes])
    for at, grad in enumerate(grads, first):
        put_matrix(pack, at, dot_left_t(rows, grad.reshape(-1, GROUP_LANES)))


def first_norm_back(k, order, between):
    chunks, chunk_rows, width = k.tok.shape
    some = chunk_rows // BLOCK
    sums = (jnp.zeros((1, width), jnp.float32),) * 2
    for t in range(chunks):
        r = order(t)
        at = chunk_blocks(r, some)
        grads = (k.mixed[at, :, pl.ds(0, width)], k.active[0, at], k.active[1, at])
        grad_mixed = jnp.concatenate([grad.reshape(chunk_rows, width) for grad in grads], axis=1)
        spread = jnp.broadcast_to(k.means[r][:, None, :], (some, BLOCK, width))
        grad_normed = dot_right_t(grad_mixed, k.w_qkv[...]) + spread.reshape(chunk_rows, width)
        unit, inverse = norm_parts(k.tok[r].astype(jnp.float32))
        grad = k.hidden[r] + norm_grad(grad_normed, unit, inverse, k.gain_one[...])
        k.stage[r] = grad.astype(jnp.bfloat16)
        terms = (grad_normed * unit, grad_normed)
        sums = tuple(total + row_sum(term) for total, term in zip(sums, terms))
        between[t]()
    for at, total in enumerate(sums, 4):
        k.sums[at : at + 1, :] = total


def flip(index, bit):
    return index + bit - 2 * bit * ((index // bit) % 2)


def flip_both(index, step):
    low, high = index % 2, index // 2
    low_step, high_step = step % 2, step // 2
    return (low + low_step - 2 * low * low_step) + 2 * (
        high + high_step - 2 * high * high_step
    )


class Links:
    def __init__(self, k):
        self.k = k
        self.used = 0
        self.used_here = 0

    def take(self, count):
        self.used += count
        return self.used - count

    def copy(self, at, source, target, peer):
        return pltpu.make_async_remote_copy(
            src_ref=source,
            dst_ref=target,
            send_sem=self.k.send.at[at],
            recv_sem=self.k.recv.at[at],
            device_id=peer,
            device_id_type=pl.DeviceIdType.MESH,
        )

    def here(self, source, target):
        self.used_here += 1
        return pltpu.make_async_copy(source, target, self.k.local.at[self.used_here - 1])


def start(copies):
    for copy in copies:
        copy.start()


def wait(copies):
    for copy in copies:
        copy.wait()


class Exchange:
    def __init__(self):
        self.under_way = []
        self.steps = []

    def then(self, copies, work=None):
        self.steps.append((copies, work))

    def step(self):
        copies, work = self.steps.pop(0)
        wait(self.under_way)
        if work is not None:
            work()
        start(copies)
        self.under_way = copies

    def finish(self):
        while self.steps:
            self.step()
        wait(self.under_way)


def add_to(pack, place, land):
    @pl.loop(0, pack.shape[0])
    def _(part):
        at = (part,) + place
        pack[at] = pack[at] + land[part]


def sum_of(pieces):
    total = pieces[0].astype(jnp.float32)
    for piece in pieces[1:]:
        total = total + piece.astype(jnp.float32)
    return total.astype(jnp.bfloat16)


def own_parts(links, pack, lands, out, places, across, z):
    (c, to_c), (a, to_a), (b, to_b) = places
    fresh = lambda source, target, to: links.copy(links.take(1), source, target, to)
    first = links.take(pack.shape[0])
    core_part = lambda part, t: links.copy(
        first + t, pack.at[part, 1 - c], lands[0].at[part], to_c
    )
    steps = Exchange()
    steps.then(
        [fresh(pack.at[:, c, 1 - a], lands[1], to_a)], lambda: add_to(pack, (c,), lands[0])
    )
    steps.then(
        [fresh(pack.at[:, c, a, 1 - b], lands[2], to_b)], lambda: add_to(pack, (c, a), lands[1])
    )
    low, high = z % 2, z // 2
    to_near, to_middle, _ = across
    steps.then(
        [
            fresh(pack.at[1 - low + 2 * half, c, a, b], lands[3].at[half], to_near)
            for half in range(2)
        ],
        lambda: add_to(pack, (c, a, b), lands[2]),
    )

    def add_near():
        for half in range(2):
            at = (low + 2 * half, c, a, b)
            pack[at] = pack[at] + lands[3][half]

    far_part = pack.at[low + 2 * (1 - high), c, a, b]
    steps.then([fresh(far_part, lands[3].at[2], to_middle)], add_near)

    def total():
        out[0, c, a, b] = sum_of([pack[z, c, a, b], lands[3][2]])

    steps.then([fresh(out.at[:, c, a, b], out.at[:, c, a, b], to_b)], total)
    steps.then([fresh(out.at[:, c, a], out.at[:, c, a], to_a)])
    steps.then([fresh(out.at[:, c], out.at[:, c], to_c)])
    return (steps, core_part)


def all_parts(links, pack, lands, out, place, plane, to_core, across):
    z, core, x, y = place
    fresh = lambda source, target, to: links.copy(links.take(1), source, target, to)
    steps = Exchange()
    steps.then([fresh(pack.at[:, 1 - core], lands[0], to_core)])
    steps.then(
        [
            fresh(pack.at[:, core, at_x, at_y], lands[1].at[t], to)
            for t, (at_x, at_y, to) in enumerate(plane)
        ],
        lambda: add_to(pack, (core,), lands[0]),
    )

    def add_plane():
        @pl.loop(0, pack.shape[0])
        def _(part):
            at = (part, core, x, y)
            pack[at] = sum_of([pack[at]] + [lands[1][t, part] for t in range(len(plane))])

    steps.then(
        [
            fresh(pack.at[peer["mp"], core, x, y], lands[2].at[t], peer)
            for t, peer in enumerate(across)
        ],
        add_plane,
    )

    def total():
        pieces = [lands[2][t] for t in range(len(across))]
        out[place] = sum_of([pack[place]] + pieces)

    spread_out(links, steps, out, place, plane, to_core, across, total)
    return steps


def spread_out(links, steps, array, place, plane, to_core, across, work=None):
    z, core, x, y = place
    fresh = lambda ref, to: links.copy(links.take(1), ref, ref, to)
    steps.then([fresh(array.at[place], peer) for peer in across], work)
    steps.then([fresh(array.at[:, core, x, y], to) for _, _, to in plane])
    steps.then([fresh(array.at[:, core], to_core)])


def layer_kernel(names, *refs):
    k = SimpleNamespace(**dict(zip(names, refs)))
    p = lax.axis_index("dp")
    z = lax.axis_index("mp")
    core, x, y = p % 2, (p // 2) % 2, p // 4
    k.z = z
    k.place = (z, core, x, y)
    to_core, to_x, to_y, to_far = (
        {"dp": other} for other in (flip(p, 1), flip(p, 2), flip(p, 4), flip(flip(p, 2), 4))
    )
    across = [{"mp": flip_both(z, t)} for t in (1, 2, 3)]
    plane = ((1 - x, y, to_x), (x, 1 - y, to_y), (1 - x, 1 - y, to_far))
    parts = k.w_in.shape[0]

    barrier = pltpu.get_barrier_semaphore()
    for peer in [to_core, to_x, to_y, to_far] + across:
        pl.semaphore_signal(barrier, inc=1, device_id=peer, device_id_type=pl.DeviceIdType.MESH)
    links = Links(k)
    fresh = lambda source, target, to: links.copy(links.take(1), source, target, to)
    here = [
        links.here(source, target)
        for source, target in (
            (k.w_qkv_in, k.w_qkv),
            (k.sort_query_in, k.sort_query),
            (k.sort_key_in, k.sort_key),
            (k.w_out_in, k.w_out),
            (k.w_in_in, k.w_in.at[z]),
            (k.w_back_in, k.w_back.at[z]),
        )
    ]
    start(here)
    lay_out_small(k)
    pl.semaphore_wait(barrier, 7)

    def to_sequences(source, target):
        copies = [links.here(source.at[z], target.at[z])]
        copies += [fresh(source.at[peer["mp"]], target.at[z], peer) for peer in across]
        start(copies)
        return copies

    def weight_part(peer):
        m = peer["mp"]
        same = lambda ref, to: fresh(ref, ref, to)
        steps = Exchange()
        steps.then(
            [
                fresh(k.w_in_in.at[core, x, y], k.w_in.at[z, core, x, y], peer),
                fresh(k.w_back_in.at[core, y, x], k.w_back.at[z, core, y, x], peer),
            ]
        )
        steps.then(
            [same(k.w_in.at[m, core, x, y], to_x), same(k.w_back.at[m, core, y, x], to_y)]
        )
        steps.then(
            [same(k.w_in.at[m, core, :, y], to_y), same(k.w_back.at[m, core, :, x], to_x)]
        )
        steps.then([same(k.w_in.at[m, core], to_core), same(k.w_back.at[m, core], to_core)])
        return steps

    near, middle, far = (weight_part(peer) for peer in across)
    near.step()
    middle.step()
    far.step()
    tokens = to_sequences(k.tok_in, k.tok)
    segments = to_sequences(k.seg_stage, k.seg)
    biases = [fresh(k.in_bias_stage, k.in_bias.at[z], peer) for peer in across]
    start(biases)
    k.in_bias[z] = k.in_bias_stage[...]
    k.sums[...] = jnp.zeros_like(k.sums)
    wait(here[:1] + tokens[:1])
    first_norm(k, z)
    near.step()
    for t, steps in ((1, (near, middle, far)), (2, (near, middle, far)), (3, (middle, far))):
        tokens[t].wait()
        first_norm(k, flip_both(z, t))
        if t == 3:
            cotangents = to_sequences(k.cot_in, k.cot)
        for each in steps:
            each.step()
    wait(here[1:3])
    sort_plan(k)
    summaries = Exchange()
    spread_out(links, summaries, k.summary_all, k.place, plane, to_core, across)
    summaries.step()
    sort_forward(k)
    wait(segments)
    attend(k)
    summaries.step()
    wait(here[3:] + biases)
    for each in (near, middle, far):
        each.finish()
    feed_forward(k)

    def to_positions(target):
        copies = [fresh(k.stage.at[peer["mp"]], target.at[z], peer) for peer in across]
        return copies + [links.here(k.stage.at[z], target.at[z])]

    outs = to_positions(k.out_land)

    def arrived(t):
        for step, copy in enumerate(cotangents):

            @pl.when(t == step)
            def _():
                copy.wait()
                if step == len(cotangents) - 1:
                    start(outs)

        return flip_both(z, t)

    feed_back(k, arrived)
    summaries.step()

    def lands(name, levels):
        return [getattr(k, name + "_land" + str(level)) for level in range(levels)]

    order_x = ((core, to_core), (x, to_x), (y, to_y))
    order_y = ((core, to_core), (y, to_y), (x, to_x))
    ff_in, ff_in_part = own_parts(
        links, k.ff_in, lands("ff_in", 4), k.ff_in_out, order_x, across, z
    )
    ff_back, ff_back_part = own_parts(
        links, k.ff_back, lands("ff_back", 4), k.ff_back_out, order_y, across, z
    )
    first, second = (
        all_parts(
            links,
            getattr(k, name),
            lands(name, 3),
            getattr(k, name + "_out"),
            k.place,
            plane,
            to_core,
            across,
        )
        for name in ("first", "second")
    )
    factors = Exchange()
    spread_out(links, factors, k.factors, k.place, plane, to_core, across)

    @pl.loop(0, parts)
    def _(t):
        c = flip_both(z, t)
        feed_weights(k, c)
        ff_in_part(c, t).start()
        ff_back_part(c, t).start()

    for t in range(parts):
        c = flip_both(z, t)
        ff_in.under_way.append(ff_in_part(c, t))
        ff_back.under_way.append(ff_back_part(c, t))

    sums = Exchange()
    lands = k.sums_land

    def add_core():
        k.sums[...] += lands[0]

    def add_plane():
        k.sums[...] = (k.sums[...] + lands[1]) + (lands[2] + lands[3])

    sums.then([fresh(k.sums, lands.at[0], to_core)])
    sums.then([fresh(k.sums, lands.at[1 + t], to) for t, (_, _, to) in enumerate(plane)], add_core)
    sums.then([fresh(k.sums, lands.at[4 + t], peer) for t, peer in enumerate(across)], add_plane)

    def step(*exchanges):
        for each in exchanges:
            each.step()

    blocks = k.mixed.shape[0]
    out_weights(k)
    attend_back(k, 0, 0, blocks // 2)
    step(ff_back)
    attend_back(k, 0, blocks // 2, blocks)
    step(ff_in)
    mix_back(k, 0)
    first_weights(k, 0, k.first, 2)
    step(first)
    plan_grad(k, 0)
    attend_back(k, 1, 0, blocks // 2)
    step(first, ff_back)
    attend_back(k, 1, blocks // 2, blocks)
    mix_back(k, 1)
    first_weights(k, 1, k.second, 0)
    step(ff_in, second)
    plan_grad(k, 1)
    step(second)
    plan_back(k)
    step(first, factors)
    wait(outs)
    outs = to_positions(k.tokens_land)
    first_norm_back(
        k,
        lambda t: flip_both(z, (t + 1) % parts),
        (lambda: step(ff_back), lambda: step(ff_in), lambda: None, lambda: None),
    )
    step(sums, first, second, factors, sums, ff_back, ff_in, first, sums, second)
    start(outs)
    step(factors, ff_back, ff_in, second, first, ff_back, ff_in, second, ff_back, ff_in)
    for each in (summaries, factors, first, ff_in, ff_back, second, sums):
        each.finish()
    total = (k.sums[...] + lands[4]) + (lands[5] + lands[6])
    lands[0] = total
    k.vectors[...] = total
    k.vectors[6:7, :] = lands[0, pl.ds(8 + z, 1), :]
    wait(outs)


def lay_out_small(k):
    sequences, positions = k.seg_in.shape
    k.seg_stage[...] = jnp.zeros_like(k.seg_stage)
    for s in range(sequences):
        ids = k.seg_in[s : s + 1, :].astype(jnp.float32)
        for at in range(positions // BLOCK):
            row = ids[:, at * BLOCK : (at + 1) * BLOCK]
            k.seg_stage[s, at : at + 1, :] = jnp.concatenate([row, row], axis=1)
    k.in_bias_stage[...] = jnp.broadcast_to(k.in_bias_in[...], k.in_bias_stage.shape)


FAR = (
    "tok_in",
    "cot_in",
    "w_qkv_in",
    "w_out_in",
    "sort_query_in",
    "sort_key_in",
    "w_in_in",
    "w_back_in",
)
NEAR = (
    "seg_in",
    "in_bias_in",
    "mask",
    "gain_one",
    "shift_one",
    "out_bias",
    "gain_two",
    "shift_two",
    "back_bias",
)


def buffers_of(parts, chunk_rows, width, units):
    blocks = parts * chunk_rows // BLOCK
    groups = width // GROUP_LANES
    stacked = GROUP_LANES // (width // HEADS) * BLOCK
    rows = (parts, chunk_rows, width)
    in_blocks = (blocks, BLOCK, width)
    small = (blocks, HEADS, blocks)
    plans = (groups, GROUP_LANES, HEADS // groups * GROUP_LANES)
    low, full = jnp.bfloat16, jnp.float32
    ff_in = (1, width // 8, units)
    ff_back = (1, units // 8, width)
    rows_of = width // (8 * parts)
    pieces = dict(
        ff_in=ff_in,
        ff_back=ff_back,
        first=(5, rows_of, GROUP_LANES),
        second=(3, rows_of, GROUP_LANES),
    )
    everywhere = (parts, 2, 2, 2)
    far = dict(out_land=(rows, low), tokens_land=(rows, low))
    near = dict(
        vectors=((16, width), full),
        summary_all=(everywhere + (blocks, width), low),
        factors=(everywhere + (2, blocks, width), low),
    )
    for name, piece in pieces.items():
        whole = 1 if name.startswith("ff") else parts
        near[name + "_out"] = ((whole, 2, 2, 2) + piece, low)
    scratch = dict(
        tok=(rows, low),
        cot=(rows, low),
        seg=((parts, 8, 2 * BLOCK), full),
        seg_stage=((parts, 8, 2 * BLOCK), full),
        in_bias_stage=((8, units), full),
        w_qkv=((width, 3 * width), low),
        w_out=((width, width), low),
        sort_query=((width, width), low),
        sort_key=((width, width), low),
        w_in=((parts, 2, 2, 2, width // 8, units), low),
        w_back=((parts, 2, 2, 2, units // 8, width), low),
        in_bias=((parts, 8, units), full),
        means=((parts, chunk_rows // BLOCK, width), full),
        normed_low=(rows, low),
        mixed=((blocks, BLOCK, 3 * width), low),
        sort_q=((blocks, width), full),
        sort_k=((blocks, width), full),
        allowed=(small, full),
        log_plans=((2 * ITERS,) + small, full),
        grad_plan=(small, full),
        plan_wide=(plans, low),
        plan_tall=(plans, low),
        sorted=((blocks, BLOCK, 2 * width), low),
        weights=((blocks, groups, 2 * BLOCK, stacked), full),
        attended=(in_blocks, low),
        hidden=(rows, full),
        normed_two=(rows, low),
        active=((parts, blocks, BLOCK, units), low),
        slope=((parts, parts, chunk_rows, units), low),
        grad_low=(rows, low),
        grad_attended=(in_blocks, low),
        stage=(rows, low),
        sums=((16, width), full),
        sums_land=((7, 16, width), full),
    )
    for name, piece in pieces.items():
        scratch[name] = (everywhere + piece, low)
        scratch[name + "_land0"] = ((parts, 2, 2) + piece, low)
    for name in ("ff_in", "ff_back"):
        scratch[name + "_land1"] = ((parts, 2) + pieces[name], low)
        scratch[name + "_land2"] = ((parts,) + pieces[name], low)
        scratch[name + "_land3"] = ((parts - 1,) + pieces[name], low)
    for name in ("first", "second"):
        scratch[name + "_land1"] = ((3, parts) + pieces[name], low)
        scratch[name + "_land2"] = ((parts - 1,) + pieces[name], low)
    return (far, near, scratch)


def layer_call(inputs):
    parts, chunk_rows, width = inputs["tok_in"].shape
    units = inputs["w_in_in"].shape[-1]
    far, near, scratch = buffers_of(parts, chunk_rows, width, units)
    outs = far | near
    in_vmem = pl.BlockSpec(memory_space=pltpu.VMEM)
    anywhere = pl.BlockSpec(memory_space=pl.ANY)
    results = pl.pallas_call(
        partial(layer_kernel, FAR + NEAR + tuple(outs) + tuple(scratch) + ("send", "recv", "local")),
        out_shape=[jax.ShapeDtypeStruct(*entry) for entry in outs.values()],
        in_specs=[anywhere] * len(FAR) + [in_vmem] * len(NEAR),
        out_specs=[anywhere] * len(far) + [in_vmem] * len(near),
        scratch_shapes=[pltpu.VMEM(*entry) for entry in scratch.values()]
        + [
            pltpu.SemaphoreType.DMA((COPIES,)),
            pltpu.SemaphoreType.DMA((COPIES,)),
            pltpu.SemaphoreType.DMA((LOCAL_COPIES,)),
        ],
        compiler_params=pltpu.CompilerParams(
            collective_id=0, has_side_effects=True, vmem_limit_bytes=VMEM_BYTES
        ),
        name="layer",
    )(*[inputs[name] for name in FAR + NEAR])
    return dict(zip(outs, results))


def widen_kernel(out, tokens, first, second, summary, factors, ff_in, ff_back, vectors, *results):
    wide = lambda array: array.astype(jnp.float32)
    layer_out, grad_tokens, grad_qkv, grad_w_out, grad_sq, grad_sk, grad_w_in, grad_w_back = results[:8]
    layer_out[...] = wide(out[...])
    grad_tokens[...] = wide(tokens[...])
    lanes = first.shape[-1]
    width = grad_w_out.shape[1]
    half = lambda pack, at: wide(pack[0, :, :, :, at]).reshape(-1, lanes)
    for at in range(2):
        grad_w_out[:, at * lanes : (at + 1) * lanes] = half(first, at)
    for part in range(3):
        for at, (pack, place) in enumerate(((first, 2 + part), (second, part))):
            place_at = part * width + at * lanes
            grad_qkv[:, place_at : place_at + lanes] = half(pack, place)
    rows = grad_sq.shape[0]
    columns = pl.ds(pl.multiple_of(pl.program_id(0) * rows, rows), rows)
    left = summary[:, columns]
    for at, result in enumerate((grad_sq, grad_sk)):
        result[...] = dot_left_t(left, factors[:, at].reshape(-1, width))
    grad_w_in[...] = wide(ff_in[...])
    grad_w_back[...] = wide(ff_back[...])
    for at, result in enumerate(results[8:]):
        result[...] = vectors[at : at + 1, :]


def widen_call(results):
    parts, chunk_rows, width = results["out_land"].shape
    units = results["ff_in_out"].shape[-1]
    square = (width, width)
    blocks = results["factors"].shape[-2]
    ins = [
        results["out_land"],
        results["tokens_land"],
        results["first_out"],
        results["second_out"],
        results["summary_all"].reshape(-1, width),
        results["factors"].reshape(-1, 2, blocks, width),
        results["ff_in_out"].reshape(width, units),
        results["ff_back_out"].reshape(units, width),
        results["vectors"],
    ]
    shapes = [ins[0].shape, ins[1].shape, (width, 3 * width), square, square, square]
    shapes += [(width, units), (units, width)] + [(1, width)] * 6 + [(1, units)]

    def part_of(shape):
        if shape[0] < parts:
            return pl.BlockSpec(shape, lambda i: (0,) * len(shape))
        return pl.BlockSpec(
            (shape[0] // parts,) + shape[1:], lambda i: (i,) + (0,) * (len(shape) - 1)
        )

    return pl.pallas_call(
        widen_kernel,
        grid=(parts,),
        out_shape=[jax.ShapeDtypeStruct(shape, jnp.float32) for shape in shapes],
        in_specs=[
            pl.BlockSpec(memory_space=pltpu.VMEM) if at in (4, 5, 8) else part_of(array.shape)
            for at, array in enumerate(ins)
        ],
        out_specs=[part_of(shape) for shape in shapes],
        compiler_params=pltpu.CompilerParams(vmem_limit_bytes=VMEM_BYTES),
        name="widen",
    )(*ins)


def per_sequence(
    tokens,
    segment_ids,
    block_mask,
    gain_one,
    shift_one,
    w_qkv,
    w_out,
    out_bias,
    sort_query,
    sort_key,
    gain_two,
    shift_two,
    input_weight,
    in_bias,
    output_weight,
    back_bias,
    cotangent,
):
    parts, chunk_rows, width = tokens.shape
    units = input_weight.shape[1]
    row = lambda vector: vector.reshape(1, -1)
    results = layer_call(
        dict(
            tok_in=tokens,
            cot_in=cotangent,
            seg_in=segment_ids,
            w_qkv_in=w_qkv,
            w_out_in=w_out,
            sort_query_in=sort_query,
            sort_key_in=sort_key,
            w_in_in=input_weight.reshape(2, 2, 2, width // 8, units),
            w_back_in=output_weight.reshape(2, 2, 2, units // 8, width),
            in_bias_in=row(in_bias.astype(jnp.float32)),
            mask=block_mask,
            gain_one=row(gain_one),
            shift_one=row(shift_one),
            out_bias=row(out_bias),
            gain_two=row(gain_two),
            shift_two=row(shift_two),
            back_bias=row(back_bias),
        )
    )
    wide = widen_call(results)
    flat = [array.reshape(-1) for array in wide[8:]]
    gain_two, shift_two, back_bias, out_bias, gain_one, shift_one, in_bias = flat
    layer_out, grad_tokens, grad_qkv, grad_w_out, grad_sq, grad_sk, grad_w_in, grad_w_back = wide[:8]
    return (
        layer_out,
        grad_tokens,
        gain_one,
        shift_one,
        grad_qkv,
        grad_w_out,
        out_bias,
        grad_sq,
        grad_sk,
        gain_two,
        shift_two,
        grad_w_in,
        in_bias,
        grad_w_back,
        back_bias,
    )


def solution(mesh):
    in_specs = (
        P("dp", "mp", None),
        P("dp", "mp"),
        P("dp", None, None),
        P(),
        P(),
        P(),
        P(),
        P(),
        P(),
        P(),
        P(),
        P(),
        P(None, "mp"),
        P("mp"),
        P("mp", None),
        P(),
        P("dp", "mp", None),
    )
    out_specs = (
        P("dp", "mp", None),
        P("dp", "mp", None),
        P(),
        P(),
        P(),
        P(),
        P(),
        P(),
        P(),
        P(),
        P(),
        P(None, "mp"),
        P("mp"),
        P("mp", None),
        P(),
    )

    def per_shard(tokens, *others):
        sizes = (mesh.shape["dp"], mesh.shape["mp"])
        sequences, positions, width = tokens.shape
        whole = sizes == (8, 4) and sequences == 4
        whole = whole and (positions, width) == (256, 512)
        whole = whole and others[11].shape[1] == width
        return (per_sequence if whole else per_device)(tokens, *others)

    return jax.shard_map(
        per_shard, mesh=mesh, in_specs=in_specs, out_specs=out_specs, check_vma=False
    )
```

```python
from functools import partial
from types import SimpleNamespace

import jax
import jax.numpy as jnp
from jax import lax
from jax.experimental import pallas as pl
from jax.experimental.pallas import tpu as pltpu
from jax.sharding import PartitionSpec as P

HEADS = 8
BLOCK = 64
ITERS = 8
VMEM_BYTES = 62 * 2**20
COPIES = 160
LOCAL_COPIES = 16
UNROLL = 4
TEMPER = 0.75
EPSILON = 1e-05
HIGH = lax.Precision.HIGHEST


def norm_stats(source):
    centred = source - jnp.mean(source, axis=-1, keepdims=True)
    inverse = lax.rsqrt(jnp.mean(centred * centred, axis=-1, keepdims=True) + EPSILON)
    return (centred * inverse, inverse)


def norm_back(grad_out, unit_rows, inverse, gain_vec):
    scaled = grad_out * gain_vec
    first_mean = jnp.mean(scaled, axis=-1, keepdims=True)
    second_mean = jnp.mean(scaled * unit_rows, axis=-1, keepdims=True)
    return inverse * (scaled - first_mean - unit_rows * second_mean)


def exact_gelu(pre_act):
    return jax.nn.gelu(pre_act, approximate=False)


def transport_plan(sort_q, sort_k, allowed):
    seq_count, blocks, model_width = sort_q.shape
    head_size = model_width // HEADS
    query_heads = sort_q.reshape(seq_count, blocks, HEADS, head_size)
    key_heads = sort_k.reshape(seq_count, blocks, HEADS, head_size)
    logits = jnp.einsum("sihe,sjhe->shij", query_heads, key_heads, precision=HIGH) * head_size ** (
        -0.5
    )
    log_plan = jnp.where(allowed[:, None], logits / TEMPER, -1000000000.0)
    for sweep_index in range(ITERS):
        log_plan = log_plan - jax.nn.logsumexp(log_plan, axis=-1, keepdims=True)
        log_plan = log_plan - jax.nn.logsumexp(log_plan, axis=-2, keepdims=True)
    return jnp.exp(log_plan)


def per_device(
    tokens,
    segment_ids,
    block_mask,
    gain_one,
    shift_one,
    w_qkv,
    w_out,
    out_bias,
    sort_query,
    sort_key,
    gain_two,
    shift_two,
    input_weight,
    in_bias,
    output_weight,
    back_bias,
    cotangent,
):
    seq_count, shard_len, model_width = tokens.shape
    head_size = model_width // HEADS
    local_blocks = shard_len // BLOCK
    all_blocks = block_mask.shape[1]
    first_block = lax.axis_index("mp") * local_blocks
    scale_factor = head_size ** (-0.5)
    token_rows = seq_count * shard_len
    pair_shape = (seq_count, local_blocks, BLOCK, 2, HEADS, head_size)
    source = tokens.astype(jnp.float32)
    unit_one, inverse_one = norm_stats(source)
    normed_one = unit_one * gain_one + shift_one
    normed_low = normed_one.astype(jnp.bfloat16).reshape(token_rows, model_width)
    mixed_rows = jnp.dot(normed_low, w_qkv, preferred_element_type=jnp.float32).astype(jnp.bfloat16)
    mixed_rows = mixed_rows.reshape(seq_count, local_blocks, BLOCK, 3, HEADS, head_size)
    queries = mixed_rows[:, :, :, 0]
    key_value = mixed_rows[:, :, :, 1:]
    pair_flat = key_value.reshape(seq_count, local_blocks, BLOCK, 2 * model_width)
    summary_low = jnp.mean(
        normed_one.reshape(seq_count, local_blocks, BLOCK, model_width), axis=2
    ).astype(jnp.bfloat16)
    summary_all = lax.all_gather(summary_low, "mp", axis=1, tiled=True)
    sort_q = jnp.dot(summary_all, sort_query, preferred_element_type=jnp.float32)
    sort_k = jnp.dot(summary_all, sort_key, preferred_element_type=jnp.float32)
    diagonal = jnp.arange(all_blocks)[:, None] == jnp.arange(all_blocks)[None, :]
    allowed = (block_mask == 1) | diagonal[None]
    plan_full, plan_back = jax.vjp(partial(transport_plan, allowed=allowed), sort_q, sort_k)
    plan_local = lax.dynamic_slice_in_dim(plan_full, first_block, local_blocks, 2).astype(
        jnp.bfloat16
    )
    pair_all = lax.all_gather(pair_flat, "mp", axis=1, tiled=True).reshape(
        seq_count, all_blocks, BLOCK, 2, HEADS, head_size
    )
    sorted_pair = jnp.einsum(
        "shij,sjbchd->sibchd", plan_local, pair_all, preferred_element_type=jnp.float32
    )
    sorted_low = sorted_pair.astype(jnp.bfloat16)
    key_cat = jnp.concatenate([sorted_low[:, :, :, 0], key_value[:, :, :, 0]], axis=2)
    value_cat = jnp.concatenate([sorted_low[:, :, :, 1], key_value[:, :, :, 1]], axis=2)
    segment_blocks = segment_ids.reshape(seq_count, local_blocks, BLOCK)
    same_doc = segment_blocks[:, :, :, None] == segment_blocks[:, :, None, :]
    keep_mask = jnp.concatenate([jnp.ones_like(same_doc), same_doc], axis=-1)[:, :, None]
    raw_scores = (
        jnp.einsum("sibhd,sikhd->sihbk", queries, key_cat, preferred_element_type=jnp.float32)
        * scale_factor
    )
    scores = jnp.where(keep_mask, raw_scores, -1000000000.0)
    weights_soft = jax.nn.softmax(scores, axis=-1)
    weights_low = weights_soft.astype(jnp.bfloat16)
    attended = jnp.einsum(
        "sihbk,sikhd->sibhd", weights_low, value_cat, preferred_element_type=jnp.float32
    )
    attended_low = attended.astype(jnp.bfloat16).reshape(token_rows, model_width)
    projected = jnp.dot(attended_low, w_out, preferred_element_type=jnp.float32) + out_bias
    hidden = source + projected.reshape(seq_count, shard_len, model_width)
    unit_two, inverse_two = norm_stats(hidden)
    normed_two = (unit_two * gain_two + shift_two).astype(jnp.bfloat16)
    cot_float = cotangent.astype(jnp.float32)
    gathered_rows = lax.all_gather(normed_two, "mp", axis=1, tiled=True)
    pre_act = jnp.dot(
        gathered_rows, input_weight, preferred_element_type=jnp.float32
    ) + in_bias.astype(jnp.float32)
    active_float, gelu_back = jax.vjp(exact_gelu, pre_act)
    activated_hidden = active_float.astype(jnp.bfloat16)
    partial_out = jnp.dot(activated_hidden, output_weight, preferred_element_type=jnp.float32)
    ffn_out = lax.psum_scatter(
        partial_out.astype(jnp.bfloat16), "mp", scatter_dimension=1, tiled=True
    ).astype(jnp.float32)
    cotangent_gathered = lax.all_gather(cotangent, "mp", axis=1, tiled=True)
    grad_activated_hidden = jnp.einsum(
        "mci,ni->mcn", cotangent_gathered, output_weight, preferred_element_type=jnp.float32
    )
    grad_pre = gelu_back(grad_activated_hidden)[0]
    grad_preactivation_rounded = grad_pre.astype(jnp.bfloat16)
    local_w_in = jnp.einsum(
        "rjy,rjq->yq", gathered_rows, grad_preactivation_rounded, preferred_element_type=jnp.float32
    )
    local_in_bias = jnp.sum(grad_pre, axis=(0, 1))
    local_output_weight = jnp.einsum(
        "wko,wkp->op", activated_hidden, cotangent_gathered, preferred_element_type=jnp.float32
    )
    grad_normed_two = lax.psum_scatter(
        jnp.einsum(
            "giv,cv->gic",
            grad_preactivation_rounded,
            input_weight,
            preferred_element_type=jnp.float32,
        ),
        "mp",
        scatter_dimension=1,
        tiled=True,
    )
    grad_w_in, grad_in_bias, grad_w_back = (
        lax.psum(local_w_in.astype(jnp.bfloat16), "dp").astype(jnp.float32),
        lax.psum(local_in_bias.astype(jnp.bfloat16), "dp").astype(jnp.float32),
        lax.psum(local_output_weight.astype(jnp.bfloat16), "dp").astype(jnp.float32),
    )
    layer_out = hidden + ffn_out + back_bias
    grad_hidden = cot_float + norm_back(grad_normed_two, unit_two, inverse_two, gain_two)
    grad_gain_two = jnp.sum(grad_normed_two * unit_two, axis=(0, 1))
    grad_shift_two = jnp.sum(grad_normed_two, axis=(0, 1))
    grad_back_bias = jnp.sum(cot_float, axis=(0, 1))
    grad_out_bias = jnp.sum(grad_hidden, axis=(0, 1))
    grad_proj_low = grad_hidden.astype(jnp.bfloat16).reshape(token_rows, model_width)
    grad_w_out = jnp.einsum(
        "td,te->de", attended_low, grad_proj_low, preferred_element_type=jnp.float32
    )
    grad_attended = jnp.einsum(
        "te,de->td", grad_proj_low, w_out, preferred_element_type=jnp.float32
    )
    grad_attended = grad_attended.astype(jnp.bfloat16).reshape(
        seq_count, local_blocks, BLOCK, HEADS, head_size
    )
    grad_weights = jnp.einsum(
        "sibhd,sikhd->sihbk", grad_attended, value_cat, preferred_element_type=jnp.float32
    )
    grad_value_cat = jnp.einsum(
        "sihbk,sibhd->sikhd", weights_low, grad_attended, preferred_element_type=jnp.float32
    )
    grad_scores = weights_soft * (
        grad_weights - jnp.sum(grad_weights * weights_soft, axis=-1, keepdims=True)
    )
    grad_scores_low = grad_scores.astype(jnp.bfloat16)
    grad_queries = (
        jnp.einsum(
            "sihbk,sikhd->sibhd", grad_scores_low, key_cat, preferred_element_type=jnp.float32
        )
        * scale_factor
    )
    grad_key_cat = (
        jnp.einsum(
            "sihbk,sibhd->sikhd", grad_scores_low, queries, preferred_element_type=jnp.float32
        )
        * scale_factor
    )
    grad_sorted = jnp.stack(
        [grad_key_cat[:, :, :BLOCK], grad_value_cat[:, :, :BLOCK]], axis=3
    ).astype(jnp.bfloat16)
    grad_pair_own = jnp.stack([grad_key_cat[:, :, BLOCK:], grad_value_cat[:, :, BLOCK:]], axis=3)
    grad_plan = jnp.einsum(
        "sibchd,sjbchd->shij", grad_sorted, pair_all, preferred_element_type=jnp.float32
    )
    term = jnp.einsum(
        "shij,sibchd->jsbchd", plan_local, grad_sorted, preferred_element_type=jnp.float32
    )
    from_sorted = lax.psum_scatter(
        term.reshape(local_blocks * lax.axis_size("mp"), seq_count, BLOCK, 2 * model_width).astype(
            jnp.bfloat16
        ),
        "mp",
        scatter_dimension=0,
        tiled=True,
    ).astype(jnp.float32)
    from_sorted = jnp.moveaxis(from_sorted, 0, 1).reshape(pair_shape)
    grad_pair = grad_pair_own + from_sorted
    grad_mixed = jnp.concatenate([grad_queries[:, :, :, None], grad_pair], axis=3)
    grad_mixed_low = grad_mixed.astype(jnp.bfloat16).reshape(token_rows, 3 * model_width)
    grad_qkv = jnp.einsum(
        "td,te->de", normed_low, grad_mixed_low, preferred_element_type=jnp.float32
    )
    grad_plan_all = lax.all_gather(grad_plan.astype(jnp.bfloat16), "mp", axis=2, tiled=True).astype(
        grad_plan.dtype
    )
    grad_sq_all, grad_sk_all = plan_back(grad_plan_all)
    grad_sq = lax.dynamic_slice_in_dim(grad_sq_all, first_block, local_blocks, 1)
    grad_sk = lax.dynamic_slice_in_dim(grad_sk_all, first_block, local_blocks, 1)
    summary_float = summary_low.astype(jnp.float32)
    grad_sort_query = jnp.einsum("sid,sie->de", summary_float, grad_sq, precision=HIGH)
    grad_sort_key = jnp.einsum("sid,sie->de", summary_float, grad_sk, precision=HIGH)
    grad_summary = jnp.einsum(
        "sie,de->sid", grad_sq, sort_query.astype(jnp.float32), precision=HIGH
    ) + jnp.einsum("sie,de->sid", grad_sk, sort_key.astype(jnp.float32), precision=HIGH)
    spread_summary = jnp.broadcast_to(
        (grad_summary / BLOCK)[:, :, None, :], (seq_count, local_blocks, BLOCK, model_width)
    ).reshape(seq_count, shard_len, model_width)
    grad_normed_one = jnp.einsum(
        "te,de->td", grad_mixed_low, w_qkv, preferred_element_type=jnp.float32
    )
    grad_normed_one = grad_normed_one.reshape(seq_count, shard_len, model_width) + spread_summary
    grad_gain_one = jnp.sum(grad_normed_one * unit_one, axis=(0, 1))
    grad_shift_one = jnp.sum(grad_normed_one, axis=(0, 1))
    grad_tokens = grad_hidden + norm_back(grad_normed_one, unit_one, inverse_one, gain_one)
    (
        grad_gain_one,
        grad_shift_one,
        grad_qkv,
        grad_w_out,
        grad_out_bias,
        grad_sort_query,
        grad_sort_key,
        grad_gain_two,
        grad_shift_two,
        grad_back_bias,
    ) = lax.psum(
        (
            grad_gain_one,
            grad_shift_one,
            grad_qkv,
            grad_w_out,
            grad_out_bias,
            grad_sort_query,
            grad_sort_key,
            grad_gain_two,
            grad_shift_two,
            grad_back_bias,
        ),
        ("dp", "mp"),
    )
    return (
        layer_out,
        grad_tokens,
        grad_gain_one,
        grad_shift_one,
        grad_qkv,
        grad_w_out,
        grad_out_bias,
        grad_sort_query,
        grad_sort_key,
        grad_gain_two,
        grad_shift_two,
        grad_w_in,
        grad_in_bias,
        grad_w_back,
        grad_back_bias,
    )


GROUP_LANES = 256


def dot(left, right, contract=((1,), (0,)), precision=None):
    return lax.dot_general(
        left,
        right,
        (contract, ((), ())),
        precision=precision,
        preferred_element_type=jnp.float32,
    )


def dot_right_t(left, right, precision=None):
    return dot(left, right, ((1,), (1,)), precision)


def dot_left_t(left, right, precision=None):
    return dot(left, right, ((0,), (0,)), precision)


def row_sum(array):
    return jnp.sum(array, axis=0, keepdims=True)


def head_lanes(head_size):
    lane_head = lax.broadcasted_iota(jnp.int32, (1, GROUP_LANES), 1) // head_size
    return [lane_head == h for h in range(GROUP_LANES // head_size)]


def spread_heads(rows, lanes, amount=1.0):
    return jnp.concatenate(
        [rows * jnp.where(keep, amount, 0.0).astype(rows.dtype) for keep in lanes], axis=0
    )


def fold_heads(stacked, lanes):
    rows = stacked.shape[0] // len(lanes)
    total = stacked[:rows]
    for h, keep in enumerate(lanes[1:], 1):
        total = jnp.where(keep, stacked[h * rows : (h + 1) * rows], total)
    return total


def norm_parts(source):
    centred = source - jnp.mean(source, axis=-1, keepdims=True)
    inverse = lax.rsqrt(jnp.mean(centred * centred, axis=-1, keepdims=True) + EPSILON)
    return (centred * inverse, inverse)


def chunk_blocks(r, some):
    return pl.ds(r * some, some)


def first_norm(k, r):
    _, chunk_rows, width = k.tok.shape
    some = chunk_rows // BLOCK
    unit, _ = norm_parts(k.tok[r].astype(jnp.float32))
    normed = unit * k.gain_one[...] + k.shift_one[...]
    k.means[r] = jnp.mean(normed.reshape(some, BLOCK, width), axis=1)
    low = normed.astype(jnp.bfloat16)
    k.normed_low[r] = low
    mixed = dot(low, k.w_qkv[...]).astype(jnp.bfloat16)
    k.mixed[chunk_blocks(r, some)] = mixed.reshape(some, BLOCK, 3 * width)


def summarize(k):
    means = k.means[...]
    k.summary_all[k.place] = means.reshape(-1, means.shape[-1]).astype(jnp.bfloat16)


def head_rows(rows, head_size):
    blocks, width = rows.shape
    shape = (blocks, HEADS, width)
    mine = lax.broadcasted_iota(jnp.int32, shape, 1) == (
        lax.broadcasted_iota(jnp.int32, shape, 2) // head_size
    )
    return jnp.where(mine, rows[:, None, :], 0.0).reshape(blocks * HEADS, width)


def sort_plan(k):
    width = k.tok.shape[2]
    head_size = width // HEADS
    blocks = k.mixed.shape[0]
    summary = k.summary_all[k.place]
    sort_q = dot(summary, k.sort_query[...])
    sort_k = dot(summary, k.sort_key[...])
    k.sort_q[...] = sort_q
    k.sort_k[...] = sort_k
    logits = dot_right_t(head_rows(sort_q, head_size), sort_k, HIGH) * head_size ** (-0.5)
    allowed = (k.mask[k.z] == 1) | (
        lax.broadcasted_iota(jnp.int32, (blocks, blocks), 0)
        == lax.broadcasted_iota(jnp.int32, (blocks, blocks), 1)
    )
    allowed = jnp.where(allowed, 1.0, 0.0)[:, None, :]
    k.allowed[...] = jnp.broadcast_to(allowed, (blocks, HEADS, blocks))
    log_plan = jnp.where(
        k.allowed[...] > 0.5, logits.reshape(blocks, HEADS, blocks) / TEMPER, -1000000000.0
    )

    def sweep(t, log_plan):
        for half, axis in enumerate((2, 0)):
            top = jnp.max(log_plan, axis=axis, keepdims=True)
            total = jnp.sum(jnp.exp(log_plan - top), axis=axis, keepdims=True)
            log_plan = log_plan - (top + jnp.log(total))
            k.log_plans[2 * t + half] = log_plan
        return log_plan

    plan = jnp.exp(lax.fori_loop(0, ITERS, sweep, log_plan))
    spread_plan(k, plan.reshape(blocks * HEADS, blocks))


def spread_plan(k, plan):
    rows, blocks = plan.shape
    side = GROUP_LANES
    part = side // blocks
    columns = (
        lax.broadcasted_iota(jnp.int32, (blocks, side), 1) // part
        == lax.broadcasted_iota(jnp.int32, (blocks, side), 0)
    ).astype(jnp.float32)
    wide = dot(plan.astype(jnp.bfloat16), columns.astype(jnp.bfloat16))
    tall = wide.T.astype(jnp.bfloat16)
    wide = wide.astype(jnp.bfloat16)
    same = (
        lax.broadcasted_iota(jnp.int32, (side, side), 0) % part
        == lax.broadcasted_iota(jnp.int32, (side, side), 1) % part
    )
    block_of = lax.broadcasted_iota(jnp.int32, (side, rows), 0) // part
    row_of = lax.broadcasted_iota(jnp.int32, (side, rows), 1)
    block_at = lax.broadcasted_iota(jnp.int32, (rows, side), 1) // part
    row_at = lax.broadcasted_iota(jnp.int32, (rows, side), 0)
    in_group = HEADS // k.plan_wide.shape[0]
    for h in range(HEADS):
        pick = (row_of == block_of * HEADS + h).astype(jnp.float32).astype(jnp.bfloat16)
        pick_t = (row_at == block_at * HEADS + h).astype(jnp.float32).astype(jnp.bfloat16)
        at = pl.ds((h % in_group) * side, side)
        k.plan_wide[h // in_group, :, at] = jnp.where(same, dot(pick, wide), 0.0).astype(
            jnp.bfloat16
        )
        k.plan_tall[h // in_group, :, at] = jnp.where(same, dot(tall, pick_t), 0.0).astype(
            jnp.bfloat16
        )


def mix_blocks(k, plan_ref, source, source_lane, groups, write):
    blocks, _, _ = source.shape
    width = k.tok.shape[2]
    part = GROUP_LANES // blocks
    lanes = head_lanes(width // HEADS)
    for c in range(BLOCK // part):
        for lane in range(0, 2 * width, GROUP_LANES):
            group = (lane % width) // GROUP_LANES
            if group not in groups:
                continue
            rows = source[:, pl.ds(c * part, part), pl.ds(source_lane + lane, GROUP_LANES)]
            rows = spread_heads(rows.reshape(GROUP_LANES, GROUP_LANES), lanes)
            mixed = dot(plan_ref[group], rows)
            write(c * part, part, lane, mixed.reshape(blocks, part, GROUP_LANES))


def sort_forward(k):
    def write(row, rows, lane, mixed):
        k.sorted[:, pl.ds(row, rows), pl.ds(lane, GROUP_LANES)] = mixed.astype(jnp.bfloat16)

    mix_blocks(k, k.plan_wide, k.mixed, k.tok.shape[2], range(k.plan_wide.shape[0]), write)


def block_parts(k, i, lane):
    width = k.tok.shape[2]
    queries = k.mixed[i, :, pl.ds(lane, GROUP_LANES)]
    keys = jnp.concatenate(
        [
            k.sorted[i, :, pl.ds(lane, GROUP_LANES)],
            k.mixed[i, :, pl.ds(width + lane, GROUP_LANES)],
        ],
        axis=0,
    )
    values = jnp.concatenate(
        [
            k.sorted[i, :, pl.ds(width + lane, GROUP_LANES)],
            k.mixed[i, :, pl.ds(2 * width + lane, GROUP_LANES)],
        ],
        axis=0,
    )
    return (queries, keys, values)


def attend(k):
    width = k.tok.shape[2]
    head_size = width // HEADS
    lanes = head_lanes(head_size)
    some = k.tok.shape[1] // BLOCK
    diagonal = lax.broadcasted_iota(jnp.int32, (BLOCK, 2 * BLOCK), 1) == (
        lax.broadcasted_iota(jnp.int32, (BLOCK, 2 * BLOCK), 0)
    )

    @pl.loop(0, k.mixed.shape[0], unroll=UNROLL)
    def _(i):
        ids = k.seg[i // some, pl.ds(i % some, 1), :]
        of_query = jnp.concatenate([ids] * (len(lanes) // 2), axis=1)
        of_key = jnp.sum(jnp.where(diagonal, ids, 0.0), axis=1, keepdims=True)
        keep = of_key == of_query
        for group in range(width // GROUP_LANES):
            lane = group * GROUP_LANES
            queries, keys, values = block_parts(k, i, lane)
            scores = dot_right_t(keys, spread_heads(queries, lanes, head_size ** (-0.5)))
            sorted_part = scores[:BLOCK]
            own_part = jnp.where(keep, scores[BLOCK:], -1000000000.0)
            top = jnp.maximum(
                jnp.max(sorted_part, axis=0, keepdims=True), jnp.max(own_part, axis=0, keepdims=True)
            )
            raised = jnp.exp(jnp.concatenate([sorted_part, own_part], axis=0) - top)
            weights = raised * (1.0 / row_sum(raised))
            k.weights[i, group] = weights
            mixed = fold_heads(dot_left_t(weights.astype(jnp.bfloat16), values), lanes)
            k.attended[i, :, pl.ds(lane, GROUP_LANES)] = mixed.astype(jnp.bfloat16)


def feed_forward(k):
    chunks, chunk_rows, width = k.tok.shape
    parts = k.w_in.shape[0]
    some = chunk_rows // BLOCK
    units = k.active.shape[3]

    @pl.loop(0, chunks)
    def _(r):
        at = chunk_blocks(r, some)
        projected = dot(k.attended[at].reshape(chunk_rows, width), k.w_out[...]) + k.out_bias[...]
        hidden = k.tok[r].astype(jnp.float32) + projected
        k.hidden[r] = hidden
        unit, _ = norm_parts(hidden)
        normed = (unit * k.gain_two[...] + k.shift_two[...]).astype(jnp.bfloat16)
        k.normed_two[r] = normed
        total = hidden + k.back_bias[...]
        for c in range(parts):
            pre = dot(normed, k.w_in[c].reshape(width, units)) + k.in_bias[c, 0:1, :]
            cdf = 0.5 + 0.5 * lax.erf(pre * 0.5**0.5)
            active = (pre * cdf).astype(jnp.bfloat16)
            slope = cdf + pre * (jnp.exp(pre * pre * -0.5) * 0.3989422804014327)
            k.active[c, at] = active.reshape(some, BLOCK, units)
            k.slope[c, r] = slope.astype(jnp.bfloat16)
            total = total + dot(active, k.w_back[c].reshape(units, width))
        k.stage[r] = total.astype(jnp.bfloat16)
        k.grad_normed[r] = jnp.zeros((chunk_rows, width), jnp.float32)


def feed_back(k, c):
    chunks, chunk_rows, width = k.tok.shape
    units = k.active.shape[3]
    w_in = k.w_in.at[c]
    w_back = k.w_back.at[c]

    def rows(r, in_bias_sum):
        grad = dot_right_t(k.cot[r], w_back[...].reshape(units, width))
        grad = grad * k.slope[c, r].astype(jnp.float32)
        low = grad.astype(jnp.bfloat16)
        k.slope[c, r] = low
        k.grad_normed[r] += dot_right_t(low, w_in[...].reshape(width, units))
        return in_bias_sum + row_sum(grad)

    total = jnp.zeros((1, units), jnp.float32)
    total = lax.fori_loop(0, chunks, rows, total, unroll=UNROLL)
    k.sums[pl.ds(8 + c, 1), :] = total
    grads = k.slope[c].reshape(-1, units)
    k.ff_in[c] = as_pack(dot_left_t(whole_rows(k.normed_two), grads), k.ff_in.shape[1:])
    active = k.active[c].reshape(-1, units)
    k.ff_back[c] = as_pack(dot_left_t(active, whole_rows(k.cot)), k.ff_back.shape[1:])


def second_norm_back(k):
    chunks, chunk_rows, width = k.tok.shape
    some = chunk_rows // BLOCK

    def rows(r, sums):
        out_grad = k.cot[r].astype(jnp.float32)
        grad_normed = k.grad_normed[r]
        unit, inverse = norm_parts(k.hidden[r])
        grad_hidden = out_grad + norm_grad(grad_normed, unit, inverse, k.gain_two[...])
        k.hidden[r] = grad_hidden
        low = grad_hidden.astype(jnp.bfloat16)
        k.normed_two[r] = low
        grad_attended = dot_right_t(low, k.w_out[...]).astype(jnp.bfloat16)
        k.grad_attended[chunk_blocks(r, some)] = grad_attended.reshape(some, BLOCK, width)
        terms = (grad_normed * unit, grad_normed, out_grad, grad_hidden)
        return tuple(total + row_sum(term) for total, term in zip(sums, terms))

    zero = jnp.zeros((1, width), jnp.float32)
    sums = lax.fori_loop(0, chunks, rows, (zero,) * 4)
    for at, total in enumerate(sums):
        k.sums[at : at + 1, :] = total


def out_weights(k):
    grad = dot_left_t(whole_rows(k.attended), whole_rows(k.normed_two))
    for half in range(2):
        put_matrix(k.first, half, grad[:, half * GROUP_LANES : (half + 1) * GROUP_LANES])


def whole_rows(ref):
    return ref[...].reshape(-1, ref.shape[-1])


def as_pack(array, shape):
    return array.astype(jnp.bfloat16).reshape(shape)


def norm_grad(grad_out, unit, inverse, gain):
    scaled = grad_out * gain
    first = jnp.mean(scaled, axis=-1, keepdims=True)
    second = jnp.mean(scaled * unit, axis=-1, keepdims=True)
    return inverse * (scaled - first - unit * second)


def put_matrix(pack, at, matrix):
    shape = pack.shape[:4] + pack.shape[5:]
    pack[:, :, :, :, at] = as_pack(matrix, shape)


def attend_back(k, group, first, last):
    width = k.tok.shape[2]
    head_size = width // HEADS
    lanes = head_lanes(head_size)
    scale = head_size ** (-0.5)

    @pl.loop(first, last, unroll=UNROLL)
    def _(i):
        lane = group * GROUP_LANES
        queries, keys, values = block_parts(k, i, lane)
        queries = spread_heads(queries, lanes, scale)
        grad_out = spread_heads(k.grad_attended[i, :, pl.ds(lane, GROUP_LANES)], lanes)
        weights = k.weights[i, group]
        grad_weights = dot_right_t(values, grad_out)
        grad_values = dot(weights.astype(jnp.bfloat16), grad_out)
        inner = row_sum(grad_weights * weights)
        grad_scores = (weights * (grad_weights - inner)).astype(jnp.bfloat16)
        grad_queries = fold_heads(dot_left_t(grad_scores, keys), lanes) * scale
        grad_keys = dot(grad_scores, queries)
        place = pl.ds(lane, GROUP_LANES)
        k.mixed[i, :, place] = grad_queries.astype(jnp.bfloat16)
        k.sorted[i, :, place] = grad_keys[:BLOCK].astype(jnp.bfloat16)
        k.sorted[i, :, pl.ds(width + lane, GROUP_LANES)] = grad_values[:BLOCK].astype(
            jnp.bfloat16
        )
        k.weights[i, group] = jnp.concatenate([grad_keys[BLOCK:], grad_values[BLOCK:]], axis=0)


def mix_back(k, group):
    width = k.tok.shape[2]

    def write(row, rows, lane, mixed):
        half = lane // width
        own = k.weights[:, group, pl.ds(half * BLOCK + row, rows), :]
        k.active[half, :, pl.ds(row, rows), pl.ds(lane % width, GROUP_LANES)] = (
            own + mixed
        ).astype(jnp.bfloat16)

    mix_blocks(k, k.plan_tall, k.sorted, 0, (group,), write)


def plan_grad(k, group):
    width = k.tok.shape[2]
    blocks = k.mixed.shape[0]
    side = GROUP_LANES
    part = side // blocks
    lanes = head_lanes(width // HEADS)
    in_group = len(lanes)

    same = (
        lax.broadcasted_iota(jnp.int32, (side, side), 0) % part
        == lax.broadcasted_iota(jnp.int32, (side, side), 1) % part
    )
    fold_columns = (
        lax.broadcasted_iota(jnp.int32, (side, blocks), 0) // part
        == lax.broadcasted_iota(jnp.int32, (side, blocks), 1)
    ).astype(jnp.float32)
    total = jnp.zeros((in_group * side, side), jnp.float32)
    for c in range(BLOCK // part):
        at = pl.ds(c * part, part)
        lane = group * side
        grads, rows = (
            [
                ref[:, at, pl.ds(offset + lane, side)].reshape(side, side)
                for offset in (start_lane, start_lane + width)
            ]
            for ref, start_lane in ((k.sorted, 0), (k.mixed, width))
        )
        grads = jnp.concatenate([spread_heads(grad, lanes) for grad in grads], axis=1)
        total = total + dot_right_t(grads, jnp.concatenate(rows, axis=1))
    for h in range(in_group):
        picked = jnp.where(same, total[h * side : (h + 1) * side], 0.0)
        picked = jnp.sum(picked.reshape(blocks, part, side), axis=1)
        k.grad_plan[:, group * in_group + h, :] = dot(picked, fold_columns, precision=HIGH)


def plan_back(k):
    width = k.tok.shape[2]
    head_size = width // HEADS
    blocks = k.mixed.shape[0]
    grad = k.grad_plan[...] * jnp.exp(k.log_plans[2 * ITERS - 1])

    def sweep(t, grad):
        for half, axis in ((1, 0), (0, 2)):
            share = jnp.exp(k.log_plans[2 * (ITERS - 1 - t) + half])
            grad = grad - share * jnp.sum(grad, axis=axis, keepdims=True)
        return grad

    grad = lax.fori_loop(0, ITERS, sweep, grad)
    grad = jnp.where(k.allowed[...] > 0.5, grad / TEMPER, 0.0) * head_size ** (-0.5)
    grad = grad.reshape(blocks * HEADS, blocks)
    sort_q = k.sort_q[...]
    sort_k = k.sort_k[...]
    shape = (blocks, HEADS, width)
    mine = lax.broadcasted_iota(jnp.int32, shape, 1) == (
        lax.broadcasted_iota(jnp.int32, shape, 2) // head_size
    )
    grad_sq = dot(grad, sort_k, precision=HIGH).reshape(shape)
    grad_sq = jnp.sum(jnp.where(mine, grad_sq, 0.0), axis=1)
    grad_sk = dot_left_t(grad, head_rows(sort_q, head_size), HIGH)
    k.factors[k.place + (0,)] = grad_sq.astype(jnp.bfloat16)
    k.factors[k.place + (1,)] = grad_sk.astype(jnp.bfloat16)
    grad_summary = dot_right_t(grad_sq, k.sort_query[...].astype(jnp.float32), HIGH)
    grad_summary += dot_right_t(grad_sk, k.sort_key[...].astype(jnp.float32), HIGH)
    some = k.means.shape[1]
    k.means[...] = (grad_summary / BLOCK).reshape(blocks // some, some, width)


def first_weights(k, group, pack, first):
    rows = whole_rows(k.normed_low)
    lanes = pl.ds(group * GROUP_LANES, GROUP_LANES)
    grads = (k.mixed[:, :, lanes], k.active[0, :, :, lanes], k.active[1, :, :, lanes])
    for at, grad in enumerate(grads, first):
        put_matrix(pack, at, dot_left_t(rows, grad.reshape(-1, GROUP_LANES)))


def first_norm_back(k, order, between):
    chunks, chunk_rows, width = k.tok.shape
    some = chunk_rows // BLOCK
    sums = (jnp.zeros((1, width), jnp.float32),) * 2
    for t in range(chunks):
        r = order(t)
        at = chunk_blocks(r, some)
        grads = (k.mixed[at, :, pl.ds(0, width)], k.active[0, at], k.active[1, at])
        grad_mixed = jnp.concatenate([grad.reshape(chunk_rows, width) for grad in grads], axis=1)
        spread = jnp.broadcast_to(k.means[r][:, None, :], (some, BLOCK, width))
        grad_normed = dot_right_t(grad_mixed, k.w_qkv[...]) + spread.reshape(chunk_rows, width)
        unit, inverse = norm_parts(k.tok[r].astype(jnp.float32))
        grad = k.hidden[r] + norm_grad(grad_normed, unit, inverse, k.gain_one[...])
        k.stage[r] = grad.astype(jnp.bfloat16)
        terms = (grad_normed * unit, grad_normed)
        sums = tuple(total + row_sum(term) for total, term in zip(sums, terms))
        between[t]()
    for at, total in enumerate(sums, 4):
        k.sums[at : at + 1, :] = total


def flip(index, bit):
    return index + bit - 2 * bit * ((index // bit) % 2)


def flip_both(index, step):
    low, high = index % 2, index // 2
    low_step, high_step = step % 2, step // 2
    return (low + low_step - 2 * low * low_step) + 2 * (
        high + high_step - 2 * high * high_step
    )


class Links:
    def __init__(self, k):
        self.k = k
        self.used = 0
        self.used_here = 0

    def take(self, count):
        self.used += count
        return self.used - count

    def copy(self, at, source, target, peer):
        return pltpu.make_async_remote_copy(
            src_ref=source,
            dst_ref=target,
            send_sem=self.k.send.at[at],
            recv_sem=self.k.recv.at[at],
            device_id=peer,
            device_id_type=pl.DeviceIdType.MESH,
        )

    def here(self, source, target):
        self.used_here += 1
        return pltpu.make_async_copy(source, target, self.k.local.at[self.used_here - 1])


def start(copies):
    for copy in copies:
        copy.start()


def wait(copies):
    for copy in copies:
        copy.wait()


class Exchange:
    def __init__(self):
        self.under_way = []
        self.steps = []

    def then(self, copies, work=None):
        self.steps.append((copies, work))

    def step(self):
        copies, work = self.steps.pop(0)
        wait(self.under_way)
        if work is not None:
            work()
        start(copies)
        self.under_way = copies

    def finish(self):
        while self.steps:
            self.step()
        wait(self.under_way)


def add_to(pack, place, land):
    @pl.loop(0, pack.shape[0])
    def _(part):
        at = (part,) + place
        pack[at] = pack[at] + land[part]


def sum_of(pieces):
    total = pieces[0].astype(jnp.float32)
    for piece in pieces[1:]:
        total = total + piece.astype(jnp.float32)
    return total.astype(jnp.bfloat16)


def own_parts(links, pack, lands, out, places, across, z):
    (c, to_c), (a, to_a), (b, to_b) = places
    fresh = lambda source, target, to: links.copy(links.take(1), source, target, to)
    parts = pack.shape[0]
    first, second = links.take(parts), links.take(parts)
    core_part = lambda part, t: links.copy(
        first + t, pack.at[part, 1 - c], lands[0].at[part], to_c
    )
    next_part = lambda part, t: links.copy(
        second + t, pack.at[part, c, 1 - a], lands[1].at[part], to_a
    )

    def go_on(part, t):
        core_part(part, t).wait()
        pack[part, c] = pack[part, c] + lands[0][part]
        next_part(part, t).start()

    steps = Exchange()
    steps.under_way = [next_part(flip_both(z, t), t) for t in range(parts)]
    steps.then(
        [fresh(pack.at[:, c, a, 1 - b], lands[2], to_b)], lambda: add_to(pack, (c, a), lands[1])
    )
    low, high = z % 2, z // 2
    to_near, to_middle, _ = across
    steps.then(
        [
            fresh(pack.at[1 - low + 2 * half, c, a, b], lands[3].at[half], to_near)
            for half in range(2)
        ],
        lambda: add_to(pack, (c, a, b), lands[2]),
    )

    def add_near():
        for half in range(2):
            at = (low + 2 * half, c, a, b)
            pack[at] = pack[at] + lands[3][half]

    far_part = pack.at[low + 2 * (1 - high), c, a, b]
    steps.then([fresh(far_part, lands[3].at[2], to_middle)], add_near)

    def total():
        out[0, c, a, b] = sum_of([pack[z, c, a, b], lands[3][2]])

    steps.then([fresh(out.at[:, c, a, b], out.at[:, c, a, b], to_b)], total)
    steps.then([fresh(out.at[:, c, a], out.at[:, c, a], to_a)])
    steps.then([fresh(out.at[:, c], out.at[:, c], to_c)])
    return (steps, lambda part, t: core_part(part, t).start(), go_on)


def all_parts(links, pack, lands, out, place, plane, to_core, across):
    z, core, x, y = place
    fresh = lambda source, target, to: links.copy(links.take(1), source, target, to)
    steps = Exchange()
    steps.then([fresh(pack.at[:, 1 - core], lands[0], to_core)])
    steps.then(
        [
            fresh(pack.at[:, core, at_x, at_y], lands[1].at[t], to)
            for t, (at_x, at_y, to) in enumerate(plane)
        ],
        lambda: add_to(pack, (core,), lands[0]),
    )

    def add_plane():
        @pl.loop(0, pack.shape[0])
        def _(part):
            at = (part, core, x, y)
            pack[at] = sum_of([pack[at]] + [lands[1][t, part] for t in range(len(plane))])

    steps.then(
        [
            fresh(pack.at[peer["mp"], core, x, y], lands[2].at[t], peer)
            for t, peer in enumerate(across)
        ],
        add_plane,
    )

    def total():
        pieces = [lands[2][t] for t in range(len(across))]
        out[place] = sum_of([pack[place]] + pieces)

    spread_out(links, steps, out, place, plane, to_core, across, total)
    return steps


def spread_out(links, steps, array, place, plane, to_core, across, work=None):
    z, core, x, y = place
    fresh = lambda ref, to: links.copy(links.take(1), ref, ref, to)
    steps.then([fresh(array.at[place], peer) for peer in across], work)
    steps.then([fresh(array.at[:, core, x, y], to) for _, _, to in plane])
    steps.then([fresh(array.at[:, core], to_core)])


def layer_kernel(names, *refs):
    k = SimpleNamespace(**dict(zip(names, refs)))
    p = lax.axis_index("dp")
    z = lax.axis_index("mp")
    core, x, y = p % 2, (p // 2) % 2, p // 4
    k.z = z
    k.place = (z, core, x, y)
    to_core, to_x, to_y, to_far = (
        {"dp": other} for other in (flip(p, 1), flip(p, 2), flip(p, 4), flip(flip(p, 2), 4))
    )
    across = [{"mp": flip_both(z, t)} for t in (1, 2, 3)]
    plane = ((1 - x, y, to_x), (x, 1 - y, to_y), (1 - x, 1 - y, to_far))
    parts = k.w_in.shape[0]

    barrier = pltpu.get_barrier_semaphore()
    for peer in [to_core, to_x, to_y, to_far] + across:
        pl.semaphore_signal(barrier, inc=1, device_id=peer, device_id_type=pl.DeviceIdType.MESH)
    links = Links(k)
    fresh = lambda source, target, to: links.copy(links.take(1), source, target, to)
    here = [
        links.here(source, target)
        for source, target in (
            (k.w_qkv_in, k.w_qkv),
            (k.sort_query_in, k.sort_query),
            (k.sort_key_in, k.sort_key),
            (k.w_out_in, k.w_out),
            (k.w_in_in, k.w_in.at[z]),
            (k.w_back_in, k.w_back.at[z]),
        )
    ]
    start(here)
    lay_out_small(k)
    pl.semaphore_wait(barrier, 7)

    def to_sequences(source, target):
        copies = [links.here(source.at[z], target.at[z])]
        copies += [fresh(source.at[peer["mp"]], target.at[z], peer) for peer in across]
        start(copies)
        return copies

    def weight_part(peer):
        m = peer["mp"]
        same = lambda ref, to: fresh(ref, ref, to)
        steps = Exchange()
        steps.then(
            [
                fresh(k.w_in_in.at[core, x, y], k.w_in.at[z, core, x, y], peer),
                fresh(k.w_back_in.at[core, y, x], k.w_back.at[z, core, y, x], peer),
            ]
        )
        steps.then(
            [same(k.w_in.at[m, core, x, y], to_x), same(k.w_back.at[m, core, y, x], to_y)]
        )
        steps.then(
            [same(k.w_in.at[m, core, :, y], to_y), same(k.w_back.at[m, core, :, x], to_x)]
        )
        steps.then([same(k.w_in.at[m, core], to_core), same(k.w_back.at[m, core], to_core)])
        return steps

    near, middle, far = (weight_part(peer) for peer in across)
    near.step()
    middle.step()
    far.step()
    tokens = to_sequences(k.tok_in, k.tok)
    segments = to_sequences(k.seg_stage, k.seg)
    biases = [fresh(k.in_bias_stage, k.in_bias.at[z], peer) for peer in across]
    start(biases)
    k.in_bias[z] = k.in_bias_stage[...]
    k.sums[...] = jnp.zeros_like(k.sums)
    wait(here[:1] + tokens[:1])
    first_norm(k, z)
    near.step()
    for t, steps in ((1, (near, middle, far)), (2, (near, middle, far)), (3, (middle, far))):
        tokens[t].wait()
        first_norm(k, flip_both(z, t))
        if t < 3:
            for each in steps:
                each.step()
    summarize(k)
    summaries = Exchange()
    spread_out(links, summaries, k.summary_all, k.place, plane, to_core, across)
    summaries.step()
    cotangents = to_sequences(k.cot_in, k.cot)
    middle.step()
    far.step()
    wait(here[1:3])
    sort_plan(k)
    sort_forward(k)
    summaries.step()
    wait(segments)
    attend(k)
    summaries.step()
    wait(here[3:] + biases)
    for each in (near, middle, far):
        each.finish()
    feed_forward(k)

    def to_positions(target):
        copies = [fresh(k.stage.at[peer["mp"]], target.at[z], peer) for peer in across]
        return copies + [links.here(k.stage.at[z], target.at[z])]

    outs = to_positions(k.out_land)

    wait(cotangents)
    start(outs)

    def lands(name, levels):
        return [getattr(k, name + "_land" + str(level)) for level in range(levels)]

    order_x = ((core, to_core), (x, to_x), (y, to_y))
    order_y = ((core, to_core), (y, to_y), (x, to_x))
    ff_in, ff_in_start, ff_in_on = own_parts(
        links, k.ff_in, lands("ff_in", 4), k.ff_in_out, order_x, across, z
    )
    ff_back, ff_back_start, ff_back_on = own_parts(
        links, k.ff_back, lands("ff_back", 4), k.ff_back_out, order_y, across, z
    )
    first, second = (
        all_parts(
            links,
            getattr(k, name),
            lands(name, 3),
            getattr(k, name + "_out"),
            k.place,
            plane,
            to_core,
            across,
        )
        for name in ("first", "second")
    )
    factors = Exchange()
    spread_out(links, factors, k.factors, k.place, plane, to_core, across)

    @pl.loop(0, parts)
    def _(t):
        c = flip_both(z, t)
        feed_back(k, c)
        ff_in_start(c, t)
        ff_back_start(c, t)

        @pl.when(t > 0)
        def _():
            before = flip_both(z, t - 1)
            ff_in_on(before, t - 1)
            ff_back_on(before, t - 1)

    second_norm_back(k)
    last = flip_both(z, parts - 1)
    ff_in_on(last, parts - 1)
    ff_back_on(last, parts - 1)
    sums = Exchange()
    lands = k.sums_land

    def add_core():
        k.sums[...] += lands[0]

    def add_plane():
        k.sums[...] = (k.sums[...] + lands[1]) + (lands[2] + lands[3])

    sums.then([fresh(k.sums, lands.at[0], to_core)])
    sums.then([fresh(k.sums, lands.at[1 + t], to) for t, (_, _, to) in enumerate(plane)], add_core)
    sums.then([fresh(k.sums, lands.at[4 + t], peer) for t, peer in enumerate(across)], add_plane)

    def step(*exchanges):
        for each in exchanges:
            each.step()

    blocks = k.mixed.shape[0]
    out_weights(k)
    attend_back(k, 0, 0, blocks // 2)
    step(ff_in, ff_back)
    attend_back(k, 0, blocks // 2, blocks)
    mix_back(k, 0)
    first_weights(k, 0, k.first, 2)
    step(first)
    plan_grad(k, 0)
    step(first)
    attend_back(k, 1, 0, blocks // 2)
    step(ff_in, ff_back)
    attend_back(k, 1, blocks // 2, blocks)
    mix_back(k, 1)
    first_weights(k, 1, k.second, 0)
    step(second, ff_in, ff_back)
    plan_grad(k, 1)
    step(second, first)
    plan_back(k)
    step(factors, second, first)
    wait(outs)
    outs = to_positions(k.tokens_land)
    nothing = lambda: None
    first_norm_back(
        k,
        lambda t: flip_both(z, (t + 1) % parts),
        (nothing, lambda: step(ff_in, ff_back), nothing, nothing),
    )
    step(sums, factors, second, sums, first, sums)
    start(outs)
    step(ff_in, ff_back, factors, second, first, ff_in, ff_back, second)
    for each in (summaries, factors, first, ff_in, ff_back, second, sums):
        each.finish()
    total = (k.sums[...] + lands[4]) + (lands[5] + lands[6])
    lands[0] = total
    k.vectors[...] = total
    k.vectors[6:7, :] = lands[0, pl.ds(8 + z, 1), :]
    wait(outs)


def lay_out_small(k):
    sequences, positions = k.seg_in.shape
    k.seg_stage[...] = jnp.zeros_like(k.seg_stage)
    for s in range(sequences):
        ids = k.seg_in[s : s + 1, :].astype(jnp.float32)
        for at in range(positions // BLOCK):
            row = ids[:, at * BLOCK : (at + 1) * BLOCK]
            k.seg_stage[s, at : at + 1, :] = jnp.concatenate([row, row], axis=1)
    k.in_bias_stage[...] = jnp.broadcast_to(k.in_bias_in[...], k.in_bias_stage.shape)


FAR = (
    "tok_in",
    "cot_in",
    "w_qkv_in",
    "w_out_in",
    "sort_query_in",
    "sort_key_in",
    "w_in_in",
    "w_back_in",
)
NEAR = (
    "seg_in",
    "in_bias_in",
    "mask",
    "gain_one",
    "shift_one",
    "out_bias",
    "gain_two",
    "shift_two",
    "back_bias",
)


def buffers_of(parts, chunk_rows, width, units):
    blocks = parts * chunk_rows // BLOCK
    groups = width // GROUP_LANES
    stacked = GROUP_LANES // (width // HEADS) * BLOCK
    rows = (parts, chunk_rows, width)
    in_blocks = (blocks, BLOCK, width)
    small = (blocks, HEADS, blocks)
    plans = (groups, GROUP_LANES, HEADS // groups * GROUP_LANES)
    low, full = jnp.bfloat16, jnp.float32
    ff_in = (1, width // 8, units)
    ff_back = (1, units // 8, width)
    rows_of = width // (8 * parts)
    pieces = dict(
        ff_in=ff_in,
        ff_back=ff_back,
        first=(5, rows_of, GROUP_LANES),
        second=(3, rows_of, GROUP_LANES),
    )
    everywhere = (parts, 2, 2, 2)
    far = dict(out_land=(rows, low), tokens_land=(rows, low))
    near = dict(
        vectors=((16, width), full),
        summary_all=(everywhere + (blocks, width), low),
        factors=(everywhere + (2, blocks, width), low),
    )
    for name, piece in pieces.items():
        whole = 1 if name.startswith("ff") else parts
        near[name + "_out"] = ((whole, 2, 2, 2) + piece, low)
    scratch = dict(
        tok=(rows, low),
        cot=(rows, low),
        seg=((parts, 8, 2 * BLOCK), full),
        seg_stage=((parts, 8, 2 * BLOCK), full),
        in_bias_stage=((8, units), full),
        w_qkv=((width, 3 * width), low),
        w_out=((width, width), low),
        sort_query=((width, width), low),
        sort_key=((width, width), low),
        w_in=((parts, 2, 2, 2, width // 8, units), low),
        w_back=((parts, 2, 2, 2, units // 8, width), low),
        in_bias=((parts, 8, units), full),
        means=((parts, chunk_rows // BLOCK, width), full),
        normed_low=(rows, low),
        mixed=((blocks, BLOCK, 3 * width), low),
        sort_q=((blocks, width), full),
        sort_k=((blocks, width), full),
        allowed=(small, full),
        log_plans=((2 * ITERS,) + small, full),
        grad_plan=(small, full),
        plan_wide=(plans, low),
        plan_tall=(plans, low),
        sorted=((blocks, BLOCK, 2 * width), low),
        weights=((blocks, groups, 2 * BLOCK, stacked), full),
        attended=(in_blocks, low),
        hidden=(rows, full),
        normed_two=(rows, low),
        active=((parts, blocks, BLOCK, units), low),
        slope=((parts, parts, chunk_rows, units), low),
        grad_normed=(rows, full),
        grad_attended=(in_blocks, low),
        stage=(rows, low),
        sums=((16, width), full),
        sums_land=((7, 16, width), full),
    )
    for name, piece in pieces.items():
        scratch[name] = (everywhere + piece, low)
        scratch[name + "_land0"] = ((parts, 2, 2) + piece, low)
    for name in ("ff_in", "ff_back"):
        scratch[name + "_land1"] = ((parts, 2) + pieces[name], low)
        scratch[name + "_land2"] = ((parts,) + pieces[name], low)
        scratch[name + "_land3"] = ((parts - 1,) + pieces[name], low)
    for name in ("first", "second"):
        scratch[name + "_land1"] = ((3, parts) + pieces[name], low)
        scratch[name + "_land2"] = ((parts - 1,) + pieces[name], low)
    return (far, near, scratch)


def layer_call(inputs):
    parts, chunk_rows, width = inputs["tok_in"].shape
    units = inputs["w_in_in"].shape[-1]
    far, near, scratch = buffers_of(parts, chunk_rows, width, units)
    outs = far | near
    in_vmem = pl.BlockSpec(memory_space=pltpu.VMEM)
    anywhere = pl.BlockSpec(memory_space=pl.ANY)
    results = pl.pallas_call(
        partial(layer_kernel, FAR + NEAR + tuple(outs) + tuple(scratch) + ("send", "recv", "local")),
        out_shape=[jax.ShapeDtypeStruct(*entry) for entry in outs.values()],
        in_specs=[anywhere] * len(FAR) + [in_vmem] * len(NEAR),
        out_specs=[anywhere] * len(far) + [in_vmem] * len(near),
        scratch_shapes=[pltpu.VMEM(*entry) for entry in scratch.values()]
        + [
            pltpu.SemaphoreType.DMA((COPIES,)),
            pltpu.SemaphoreType.DMA((COPIES,)),
            pltpu.SemaphoreType.DMA((LOCAL_COPIES,)),
        ],
        compiler_params=pltpu.CompilerParams(
            collective_id=0, has_side_effects=True, vmem_limit_bytes=VMEM_BYTES
        ),
        name="layer",
    )(*[inputs[name] for name in FAR + NEAR])
    return dict(zip(outs, results))


def widen_kernel(out, tokens, first, second, summary, factors, ff_in, ff_back, vectors, *results):
    wide = lambda array: array.astype(jnp.float32)
    layer_out, grad_tokens, grad_qkv, grad_w_out, grad_sq, grad_sk, grad_w_in, grad_w_back = results[:8]
    layer_out[...] = wide(out[...])
    grad_tokens[...] = wide(tokens[...])
    lanes = first.shape[-1]
    width = grad_w_out.shape[1]
    half = lambda pack, at: wide(pack[0, :, :, :, at]).reshape(-1, lanes)
    for at in range(2):
        grad_w_out[:, at * lanes : (at + 1) * lanes] = half(first, at)
    for part in range(3):
        for at, (pack, place) in enumerate(((first, 2 + part), (second, part))):
            place_at = part * width + at * lanes
            grad_qkv[:, place_at : place_at + lanes] = half(pack, place)
    rows = grad_sq.shape[0]
    columns = pl.ds(pl.multiple_of(pl.program_id(0) * rows, rows), rows)
    left = summary[:, columns]
    for at, result in enumerate((grad_sq, grad_sk)):
        result[...] = dot_left_t(left, factors[:, at].reshape(-1, width))
    grad_w_in[...] = wide(ff_in[...])
    grad_w_back[...] = wide(ff_back[...])
    for at, result in enumerate(results[8:]):
        result[...] = vectors[at : at + 1, :]


def widen_call(results):
    parts, chunk_rows, width = results["out_land"].shape
    units = results["ff_in_out"].shape[-1]
    square = (width, width)
    blocks = results["factors"].shape[-2]
    ins = [
        results["out_land"],
        results["tokens_land"],
        results["first_out"],
        results["second_out"],
        results["summary_all"].reshape(-1, width),
        results["factors"].reshape(-1, 2, blocks, width),
        results["ff_in_out"].reshape(width, units),
        results["ff_back_out"].reshape(units, width),
        results["vectors"],
    ]
    shapes = [ins[0].shape, ins[1].shape, (width, 3 * width), square, square, square]
    shapes += [(width, units), (units, width)] + [(1, width)] * 6 + [(1, units)]

    def part_of(shape):
        if shape[0] < parts:
            return pl.BlockSpec(shape, lambda i: (0,) * len(shape))
        return pl.BlockSpec(
            (shape[0] // parts,) + shape[1:], lambda i: (i,) + (0,) * (len(shape) - 1)
        )

    return pl.pallas_call(
        widen_kernel,
        grid=(parts,),
        out_shape=[jax.ShapeDtypeStruct(shape, jnp.float32) for shape in shapes],
        in_specs=[
            pl.BlockSpec(memory_space=pltpu.VMEM) if at in (4, 5, 8) else part_of(array.shape)
            for at, array in enumerate(ins)
        ],
        out_specs=[part_of(shape) for shape in shapes],
        compiler_params=pltpu.CompilerParams(vmem_limit_bytes=VMEM_BYTES),
        name="widen",
    )(*ins)


def per_sequence(
    tokens,
    segment_ids,
    block_mask,
    gain_one,
    shift_one,
    w_qkv,
    w_out,
    out_bias,
    sort_query,
    sort_key,
    gain_two,
    shift_two,
    input_weight,
    in_bias,
    output_weight,
    back_bias,
    cotangent,
):
    parts, chunk_rows, width = tokens.shape
    units = input_weight.shape[1]
    row = lambda vector: vector.reshape(1, -1)
    results = layer_call(
        dict(
            tok_in=tokens,
            cot_in=cotangent,
            seg_in=segment_ids,
            w_qkv_in=w_qkv,
            w_out_in=w_out,
            sort_query_in=sort_query,
            sort_key_in=sort_key,
            w_in_in=input_weight.reshape(2, 2, 2, width // 8, units),
            w_back_in=output_weight.reshape(2, 2, 2, units // 8, width),
            in_bias_in=row(in_bias.astype(jnp.float32)),
            mask=block_mask,
            gain_one=row(gain_one),
            shift_one=row(shift_one),
            out_bias=row(out_bias),
            gain_two=row(gain_two),
            shift_two=row(shift_two),
            back_bias=row(back_bias),
        )
    )
    wide = widen_call(results)
    flat = [array.reshape(-1) for array in wide[8:]]
    gain_two, shift_two, back_bias, out_bias, gain_one, shift_one, in_bias = flat
    layer_out, grad_tokens, grad_qkv, grad_w_out, grad_sq, grad_sk, grad_w_in, grad_w_back = wide[:8]
    return (
        layer_out,
        grad_tokens,
        gain_one,
        shift_one,
        grad_qkv,
        grad_w_out,
        out_bias,
        grad_sq,
        grad_sk,
        gain_two,
        shift_two,
        grad_w_in,
        in_bias,
        grad_w_back,
        back_bias,
    )


def solution(mesh):
    in_specs = (
        P("dp", "mp", None),
        P("dp", "mp"),
        P("dp", None, None),
        P(),
        P(),
        P(),
        P(),
        P(),
        P(),
        P(),
        P(),
        P(),
        P(None, "mp"),
        P("mp"),
        P("mp", None),
        P(),
        P("dp", "mp", None),
    )
    out_specs = (
        P("dp", "mp", None),
        P("dp", "mp", None),
        P(),
        P(),
        P(),
        P(),
        P(),
        P(),
        P(),
        P(),
        P(),
        P(None, "mp"),
        P("mp"),
        P("mp", None),
        P(),
    )

    def per_shard(tokens, *others):
        sizes = (mesh.shape["dp"], mesh.shape["mp"])
        sequences, positions, width = tokens.shape
        whole = sizes == (8, 4) and sequences == 4
        whole = whole and (positions, width) == (256, 512)
        whole = whole and others[11].shape[1] == width
        return (per_sequence if whole else per_device)(tokens, *others)

    return jax.shard_map(
        per_shard, mesh=mesh, in_specs=in_specs, out_specs=out_specs, check_vma=False
    )
```

```python
from functools import partial
from types import SimpleNamespace

import jax
import jax.numpy as jnp
from jax import lax
from jax.experimental import pallas as pl
from jax.experimental.pallas import tpu as pltpu
from jax.sharding import PartitionSpec as P

HEADS = 8
BLOCK = 64
ITERS = 8
VMEM_BYTES = 62 * 2**20
COPIES = 135
LOCAL_COPIES = 11
UNROLL = 4
TEMPER = 0.75
EPSILON = 1e-05
HIGH = lax.Precision.HIGHEST


def norm_stats(source):
    centred = source - jnp.mean(source, axis=-1, keepdims=True)
    inverse = lax.rsqrt(jnp.mean(centred * centred, axis=-1, keepdims=True) + EPSILON)
    return (centred * inverse, inverse)


def norm_back(grad_out, unit_rows, inverse, gain_vec):
    scaled = grad_out * gain_vec
    first_mean = jnp.mean(scaled, axis=-1, keepdims=True)
    second_mean = jnp.mean(scaled * unit_rows, axis=-1, keepdims=True)
    return inverse * (scaled - first_mean - unit_rows * second_mean)


def exact_gelu(pre_act):
    return jax.nn.gelu(pre_act, approximate=False)


def transport_plan(sort_q, sort_k, allowed):
    seq_count, blocks, model_width = sort_q.shape
    head_size = model_width // HEADS
    query_heads = sort_q.reshape(seq_count, blocks, HEADS, head_size)
    key_heads = sort_k.reshape(seq_count, blocks, HEADS, head_size)
    logits = jnp.einsum("sihe,sjhe->shij", query_heads, key_heads, precision=HIGH) * head_size ** (
        -0.5
    )
    log_plan = jnp.where(allowed[:, None], logits / TEMPER, -1000000000.0)
    for sweep_index in range(ITERS):
        log_plan = log_plan - jax.nn.logsumexp(log_plan, axis=-1, keepdims=True)
        log_plan = log_plan - jax.nn.logsumexp(log_plan, axis=-2, keepdims=True)
    return jnp.exp(log_plan)


def per_device(
    tokens,
    segment_ids,
    block_mask,
    gain_one,
    shift_one,
    w_qkv,
    w_out,
    out_bias,
    sort_query,
    sort_key,
    gain_two,
    shift_two,
    input_weight,
    in_bias,
    output_weight,
    back_bias,
    cotangent,
):
    seq_count, shard_len, model_width = tokens.shape
    head_size = model_width // HEADS
    local_blocks = shard_len // BLOCK
    all_blocks = block_mask.shape[1]
    first_block = lax.axis_index("mp") * local_blocks
    scale_factor = head_size ** (-0.5)
    token_rows = seq_count * shard_len
    pair_shape = (seq_count, local_blocks, BLOCK, 2, HEADS, head_size)
    source = tokens.astype(jnp.float32)
    unit_one, inverse_one = norm_stats(source)
    normed_one = unit_one * gain_one + shift_one
    normed_low = normed_one.astype(jnp.bfloat16).reshape(token_rows, model_width)
    mixed_rows = jnp.dot(normed_low, w_qkv, preferred_element_type=jnp.float32).astype(jnp.bfloat16)
    mixed_rows = mixed_rows.reshape(seq_count, local_blocks, BLOCK, 3, HEADS, head_size)
    queries = mixed_rows[:, :, :, 0]
    key_value = mixed_rows[:, :, :, 1:]
    pair_flat = key_value.reshape(seq_count, local_blocks, BLOCK, 2 * model_width)
    summary_low = jnp.mean(
        normed_one.reshape(seq_count, local_blocks, BLOCK, model_width), axis=2
    ).astype(jnp.bfloat16)
    summary_all = lax.all_gather(summary_low, "mp", axis=1, tiled=True)
    sort_q = jnp.dot(summary_all, sort_query, preferred_element_type=jnp.float32)
    sort_k = jnp.dot(summary_all, sort_key, preferred_element_type=jnp.float32)
    diagonal = jnp.arange(all_blocks)[:, None] == jnp.arange(all_blocks)[None, :]
    allowed = (block_mask == 1) | diagonal[None]
    plan_full, plan_back = jax.vjp(partial(transport_plan, allowed=allowed), sort_q, sort_k)
    plan_local = lax.dynamic_slice_in_dim(plan_full, first_block, local_blocks, 2).astype(
        jnp.bfloat16
    )
    pair_all = lax.all_gather(pair_flat, "mp", axis=1, tiled=True).reshape(
        seq_count, all_blocks, BLOCK, 2, HEADS, head_size
    )
    sorted_pair = jnp.einsum(
        "shij,sjbchd->sibchd", plan_local, pair_all, preferred_element_type=jnp.float32
    )
    sorted_low = sorted_pair.astype(jnp.bfloat16)
    key_cat = jnp.concatenate([sorted_low[:, :, :, 0], key_value[:, :, :, 0]], axis=2)
    value_cat = jnp.concatenate([sorted_low[:, :, :, 1], key_value[:, :, :, 1]], axis=2)
    segment_blocks = segment_ids.reshape(seq_count, local_blocks, BLOCK)
    same_doc = segment_blocks[:, :, :, None] == segment_blocks[:, :, None, :]
    keep_mask = jnp.concatenate([jnp.ones_like(same_doc), same_doc], axis=-1)[:, :, None]
    raw_scores = (
        jnp.einsum("sibhd,sikhd->sihbk", queries, key_cat, preferred_element_type=jnp.float32)
        * scale_factor
    )
    scores = jnp.where(keep_mask, raw_scores, -1000000000.0)
    weights_soft = jax.nn.softmax(scores, axis=-1)
    weights_low = weights_soft.astype(jnp.bfloat16)
    attended = jnp.einsum(
        "sihbk,sikhd->sibhd", weights_low, value_cat, preferred_element_type=jnp.float32
    )
    attended_low = attended.astype(jnp.bfloat16).reshape(token_rows, model_width)
    projected = jnp.dot(attended_low, w_out, preferred_element_type=jnp.float32) + out_bias
    hidden = source + projected.reshape(seq_count, shard_len, model_width)
    unit_two, inverse_two = norm_stats(hidden)
    normed_two = (unit_two * gain_two + shift_two).astype(jnp.bfloat16)
    cot_float = cotangent.astype(jnp.float32)
    gathered_rows = lax.all_gather(normed_two, "mp", axis=1, tiled=True)
    pre_act = jnp.dot(
        gathered_rows, input_weight, preferred_element_type=jnp.float32
    ) + in_bias.astype(jnp.float32)
    active_float, gelu_back = jax.vjp(exact_gelu, pre_act)
    activated_hidden = active_float.astype(jnp.bfloat16)
    partial_out = jnp.dot(activated_hidden, output_weight, preferred_element_type=jnp.float32)
    ffn_out = lax.psum_scatter(
        partial_out.astype(jnp.bfloat16), "mp", scatter_dimension=1, tiled=True
    ).astype(jnp.float32)
    cotangent_gathered = lax.all_gather(cotangent, "mp", axis=1, tiled=True)
    grad_activated_hidden = jnp.einsum(
        "mci,ni->mcn", cotangent_gathered, output_weight, preferred_element_type=jnp.float32
    )
    grad_pre = gelu_back(grad_activated_hidden)[0]
    grad_preactivation_rounded = grad_pre.astype(jnp.bfloat16)
    local_w_in = jnp.einsum(
        "rjy,rjq->yq", gathered_rows, grad_preactivation_rounded, preferred_element_type=jnp.float32
    )
    local_in_bias = jnp.sum(grad_pre, axis=(0, 1))
    local_output_weight = jnp.einsum(
        "wko,wkp->op", activated_hidden, cotangent_gathered, preferred_element_type=jnp.float32
    )
    grad_normed_two = lax.psum_scatter(
        jnp.einsum(
            "giv,cv->gic",
            grad_preactivation_rounded,
            input_weight,
            preferred_element_type=jnp.float32,
        ),
        "mp",
        scatter_dimension=1,
        tiled=True,
    )
    grad_w_in, grad_in_bias, grad_w_back = (
        lax.psum(local_w_in.astype(jnp.bfloat16), "dp").astype(jnp.float32),
        lax.psum(local_in_bias.astype(jnp.bfloat16), "dp").astype(jnp.float32),
        lax.psum(local_output_weight.astype(jnp.bfloat16), "dp").astype(jnp.float32),
    )
    layer_out = hidden + ffn_out + back_bias
    grad_hidden = cot_float + norm_back(grad_normed_two, unit_two, inverse_two, gain_two)
    grad_gain_two = jnp.sum(grad_normed_two * unit_two, axis=(0, 1))
    grad_shift_two = jnp.sum(grad_normed_two, axis=(0, 1))
    grad_back_bias = jnp.sum(cot_float, axis=(0, 1))
    grad_out_bias = jnp.sum(grad_hidden, axis=(0, 1))
    grad_proj_low = grad_hidden.astype(jnp.bfloat16).reshape(token_rows, model_width)
    grad_w_out = jnp.einsum(
        "td,te->de", attended_low, grad_proj_low, preferred_element_type=jnp.float32
    )
    grad_attended = jnp.einsum(
        "te,de->td", grad_proj_low, w_out, preferred_element_type=jnp.float32
    )
    grad_attended = grad_attended.astype(jnp.bfloat16).reshape(
        seq_count, local_blocks, BLOCK, HEADS, head_size
    )
    grad_weights = jnp.einsum(
        "sibhd,sikhd->sihbk", grad_attended, value_cat, preferred_element_type=jnp.float32
    )
    grad_value_cat = jnp.einsum(
        "sihbk,sibhd->sikhd", weights_low, grad_attended, preferred_element_type=jnp.float32
    )
    grad_scores = weights_soft * (
        grad_weights - jnp.sum(grad_weights * weights_soft, axis=-1, keepdims=True)
    )
    grad_scores_low = grad_scores.astype(jnp.bfloat16)
    grad_queries = (
        jnp.einsum(
            "sihbk,sikhd->sibhd", grad_scores_low, key_cat, preferred_element_type=jnp.float32
        )
        * scale_factor
    )
    grad_key_cat = (
        jnp.einsum(
            "sihbk,sibhd->sikhd", grad_scores_low, queries, preferred_element_type=jnp.float32
        )
        * scale_factor
    )
    grad_sorted = jnp.stack(
        [grad_key_cat[:, :, :BLOCK], grad_value_cat[:, :, :BLOCK]], axis=3
    ).astype(jnp.bfloat16)
    grad_pair_own = jnp.stack([grad_key_cat[:, :, BLOCK:], grad_value_cat[:, :, BLOCK:]], axis=3)
    grad_plan = jnp.einsum(
        "sibchd,sjbchd->shij", grad_sorted, pair_all, preferred_element_type=jnp.float32
    )
    term = jnp.einsum(
        "shij,sibchd->jsbchd", plan_local, grad_sorted, preferred_element_type=jnp.float32
    )
    from_sorted = lax.psum_scatter(
        term.reshape(local_blocks * lax.axis_size("mp"), seq_count, BLOCK, 2 * model_width).astype(
            jnp.bfloat16
        ),
        "mp",
        scatter_dimension=0,
        tiled=True,
    ).astype(jnp.float32)
    from_sorted = jnp.moveaxis(from_sorted, 0, 1).reshape(pair_shape)
    grad_pair = grad_pair_own + from_sorted
    grad_mixed = jnp.concatenate([grad_queries[:, :, :, None], grad_pair], axis=3)
    grad_mixed_low = grad_mixed.astype(jnp.bfloat16).reshape(token_rows, 3 * model_width)
    grad_qkv = jnp.einsum(
        "td,te->de", normed_low, grad_mixed_low, preferred_element_type=jnp.float32
    )
    grad_plan_all = lax.all_gather(grad_plan.astype(jnp.bfloat16), "mp", axis=2, tiled=True).astype(
        grad_plan.dtype
    )
    grad_sq_all, grad_sk_all = plan_back(grad_plan_all)
    grad_sq = lax.dynamic_slice_in_dim(grad_sq_all, first_block, local_blocks, 1)
    grad_sk = lax.dynamic_slice_in_dim(grad_sk_all, first_block, local_blocks, 1)
    summary_float = summary_low.astype(jnp.float32)
    grad_sort_query = jnp.einsum("sid,sie->de", summary_float, grad_sq, precision=HIGH)
    grad_sort_key = jnp.einsum("sid,sie->de", summary_float, grad_sk, precision=HIGH)
    grad_summary = jnp.einsum(
        "sie,de->sid", grad_sq, sort_query.astype(jnp.float32), precision=HIGH
    ) + jnp.einsum("sie,de->sid", grad_sk, sort_key.astype(jnp.float32), precision=HIGH)
    spread_summary = jnp.broadcast_to(
        (grad_summary / BLOCK)[:, :, None, :], (seq_count, local_blocks, BLOCK, model_width)
    ).reshape(seq_count, shard_len, model_width)
    grad_normed_one = jnp.einsum(
        "te,de->td", grad_mixed_low, w_qkv, preferred_element_type=jnp.float32
    )
    grad_normed_one = grad_normed_one.reshape(seq_count, shard_len, model_width) + spread_summary
    grad_gain_one = jnp.sum(grad_normed_one * unit_one, axis=(0, 1))
    grad_shift_one = jnp.sum(grad_normed_one, axis=(0, 1))
    grad_tokens = grad_hidden + norm_back(grad_normed_one, unit_one, inverse_one, gain_one)
    (
        grad_gain_one,
        grad_shift_one,
        grad_qkv,
        grad_w_out,
        grad_out_bias,
        grad_sort_query,
        grad_sort_key,
        grad_gain_two,
        grad_shift_two,
        grad_back_bias,
    ) = lax.psum(
        (
            grad_gain_one,
            grad_shift_one,
            grad_qkv,
            grad_w_out,
            grad_out_bias,
            grad_sort_query,
            grad_sort_key,
            grad_gain_two,
            grad_shift_two,
            grad_back_bias,
        ),
        ("dp", "mp"),
    )
    return (
        layer_out,
        grad_tokens,
        grad_gain_one,
        grad_shift_one,
        grad_qkv,
        grad_w_out,
        grad_out_bias,
        grad_sort_query,
        grad_sort_key,
        grad_gain_two,
        grad_shift_two,
        grad_w_in,
        grad_in_bias,
        grad_w_back,
        grad_back_bias,
    )


GROUP_LANES = 256


def dot(left, right, contract=((1,), (0,)), precision=None):
    return lax.dot_general(
        left,
        right,
        (contract, ((), ())),
        precision=precision,
        preferred_element_type=jnp.float32,
    )


def dot_right_t(left, right, precision=None):
    return dot(left, right, ((1,), (1,)), precision)


def dot_left_t(left, right, precision=None):
    return dot(left, right, ((0,), (0,)), precision)


def row_sum(array):
    return jnp.sum(array, axis=0, keepdims=True)


def head_lanes(head_size):
    lane_head = lax.broadcasted_iota(jnp.int32, (1, GROUP_LANES), 1) // head_size
    return [lane_head == h for h in range(GROUP_LANES // head_size)]


def spread_heads(rows, lanes, amount=1.0):
    return jnp.concatenate(
        [rows * jnp.where(keep, amount, 0.0).astype(rows.dtype) for keep in lanes], axis=0
    )


def fold_heads(stacked, lanes):
    rows = stacked.shape[0] // len(lanes)
    total = stacked[:rows]
    for h, keep in enumerate(lanes[1:], 1):
        total = jnp.where(keep, stacked[h * rows : (h + 1) * rows], total)
    return total


def norm_parts(source):
    centred = source - jnp.mean(source, axis=-1, keepdims=True)
    inverse = lax.rsqrt(jnp.mean(centred * centred, axis=-1, keepdims=True) + EPSILON)
    return (centred * inverse, inverse)


def chunk_blocks(r, some):
    return pl.ds(r * some, some)


def first_norm(k, r):
    _, chunk_rows, width = k.tok.shape
    some = chunk_rows // BLOCK
    unit, _ = norm_parts(k.tok[r].astype(jnp.float32))
    normed = unit * k.gain_one[...] + k.shift_one[...]
    k.means[r] = jnp.mean(normed.reshape(some, BLOCK, width), axis=1)
    low = normed.astype(jnp.bfloat16)
    k.normed_low[r] = low
    mixed = dot(low, k.w_qkv[...]).astype(jnp.bfloat16)
    k.mixed[chunk_blocks(r, some)] = mixed.reshape(some, BLOCK, 3 * width)


def summarize(k):
    means = k.means[...]
    k.summary_all[k.place] = means.reshape(-1, means.shape[-1]).astype(jnp.bfloat16)


def head_rows(rows, head_size):
    blocks, width = rows.shape
    shape = (blocks, HEADS, width)
    mine = lax.broadcasted_iota(jnp.int32, shape, 1) == (
        lax.broadcasted_iota(jnp.int32, shape, 2) // head_size
    )
    return jnp.where(mine, rows[:, None, :], 0.0).reshape(blocks * HEADS, width)


def sort_plan(k):
    width = k.tok.shape[2]
    head_size = width // HEADS
    blocks = k.mixed.shape[0]
    summary = k.summary_all[k.place]
    sort_q = dot(summary, k.sort_query[...])
    sort_k = dot(summary, k.sort_key[...])
    k.sort_q[...] = sort_q
    k.sort_k[...] = sort_k
    logits = dot_right_t(head_rows(sort_q, head_size), sort_k, HIGH) * head_size ** (-0.5)
    allowed = (k.mask[k.z] == 1) | (
        lax.broadcasted_iota(jnp.int32, (blocks, blocks), 0)
        == lax.broadcasted_iota(jnp.int32, (blocks, blocks), 1)
    )
    allowed = jnp.where(allowed, 1.0, 0.0)[:, None, :]
    k.allowed[...] = jnp.broadcast_to(allowed, (blocks, HEADS, blocks))
    log_plan = jnp.where(
        k.allowed[...] > 0.5, logits.reshape(blocks, HEADS, blocks) / TEMPER, -1000000000.0
    )

    def sweep(t, log_plan):
        for half, axis in enumerate((2, 0)):
            top = jnp.max(log_plan, axis=axis, keepdims=True)
            total = jnp.sum(jnp.exp(log_plan - top), axis=axis, keepdims=True)
            log_plan = log_plan - (top + jnp.log(total))
            k.log_plans[2 * t + half] = log_plan
        return log_plan

    plan = jnp.exp(lax.fori_loop(0, ITERS, sweep, log_plan))
    spread_plan(k, plan.reshape(blocks * HEADS, blocks))


def spread_plan(k, plan):
    rows, blocks = plan.shape
    side = GROUP_LANES
    part = side // blocks
    columns = (
        lax.broadcasted_iota(jnp.int32, (blocks, side), 1) // part
        == lax.broadcasted_iota(jnp.int32, (blocks, side), 0)
    ).astype(jnp.float32)
    wide = dot(plan.astype(jnp.bfloat16), columns.astype(jnp.bfloat16))
    tall = wide.T.astype(jnp.bfloat16)
    wide = wide.astype(jnp.bfloat16)
    same = (
        lax.broadcasted_iota(jnp.int32, (side, side), 0) % part
        == lax.broadcasted_iota(jnp.int32, (side, side), 1) % part
    )
    block_of = lax.broadcasted_iota(jnp.int32, (side, rows), 0) // part
    row_of = lax.broadcasted_iota(jnp.int32, (side, rows), 1)
    block_at = lax.broadcasted_iota(jnp.int32, (rows, side), 1) // part
    row_at = lax.broadcasted_iota(jnp.int32, (rows, side), 0)
    in_group = HEADS // k.plan_wide.shape[0]
    for h in range(HEADS):
        pick = (row_of == block_of * HEADS + h).astype(jnp.float32).astype(jnp.bfloat16)
        pick_t = (row_at == block_at * HEADS + h).astype(jnp.float32).astype(jnp.bfloat16)
        at = pl.ds((h % in_group) * side, side)
        k.plan_wide[h // in_group, :, at] = jnp.where(same, dot(pick, wide), 0.0).astype(
            jnp.bfloat16
        )
        k.plan_tall[h // in_group, :, at] = jnp.where(same, dot(tall, pick_t), 0.0).astype(
            jnp.bfloat16
        )


def mix_blocks(k, plan_ref, source, source_lane, groups, write):
    blocks, _, _ = source.shape
    width = k.tok.shape[2]
    part = GROUP_LANES // blocks
    lanes = head_lanes(width // HEADS)
    for c in range(BLOCK // part):
        for lane in range(0, 2 * width, GROUP_LANES):
            group = (lane % width) // GROUP_LANES
            if group not in groups:
                continue
            rows = source[:, pl.ds(c * part, part), pl.ds(source_lane + lane, GROUP_LANES)]
            rows = spread_heads(rows.reshape(GROUP_LANES, GROUP_LANES), lanes)
            mixed = dot(plan_ref[group], rows)
            write(c * part, part, lane, mixed.reshape(blocks, part, GROUP_LANES))


def sort_forward(k):
    def write(row, rows, lane, mixed):
        k.sorted[:, pl.ds(row, rows), pl.ds(lane, GROUP_LANES)] = mixed.astype(jnp.bfloat16)

    mix_blocks(k, k.plan_wide, k.mixed, k.tok.shape[2], range(k.plan_wide.shape[0]), write)


def block_parts(k, i, lane):
    width = k.tok.shape[2]
    queries = k.mixed[i, :, pl.ds(lane, GROUP_LANES)]
    keys = jnp.concatenate(
        [
            k.sorted[i, :, pl.ds(lane, GROUP_LANES)],
            k.mixed[i, :, pl.ds(width + lane, GROUP_LANES)],
        ],
        axis=0,
    )
    values = jnp.concatenate(
        [
            k.sorted[i, :, pl.ds(width + lane, GROUP_LANES)],
            k.mixed[i, :, pl.ds(2 * width + lane, GROUP_LANES)],
        ],
        axis=0,
    )
    return (queries, keys, values)


def attend(k):
    width = k.tok.shape[2]
    head_size = width // HEADS
    lanes = head_lanes(head_size)
    some = k.tok.shape[1] // BLOCK
    diagonal = lax.broadcasted_iota(jnp.int32, (BLOCK, 2 * BLOCK), 1) == (
        lax.broadcasted_iota(jnp.int32, (BLOCK, 2 * BLOCK), 0)
    )

    @pl.loop(0, k.mixed.shape[0], unroll=UNROLL)
    def _(i):
        ids = k.seg[i // some, pl.ds(i % some, 1), :]
        of_query = jnp.concatenate([ids] * (len(lanes) // 2), axis=1)
        of_key = jnp.sum(jnp.where(diagonal, ids, 0.0), axis=1, keepdims=True)
        keep = of_key == of_query
        for group in range(width // GROUP_LANES):
            lane = group * GROUP_LANES
            queries, keys, values = block_parts(k, i, lane)
            scores = dot_right_t(keys, spread_heads(queries, lanes, head_size ** (-0.5)))
            sorted_part = scores[:BLOCK]
            own_part = jnp.where(keep, scores[BLOCK:], -1000000000.0)
            top = jnp.maximum(
                jnp.max(sorted_part, axis=0, keepdims=True), jnp.max(own_part, axis=0, keepdims=True)
            )
            raised = jnp.exp(jnp.concatenate([sorted_part, own_part], axis=0) - top)
            weights = raised * (1.0 / row_sum(raised))
            k.weights[i, group] = weights
            mixed = fold_heads(dot_left_t(weights.astype(jnp.bfloat16), values), lanes)
            k.attended[i, :, pl.ds(lane, GROUP_LANES)] = mixed.astype(jnp.bfloat16)


def feed_forward(k):
    chunks, chunk_rows, width = k.tok.shape
    parts = k.w_in.shape[0]
    some = chunk_rows // BLOCK
    units = k.active.shape[3]

    @pl.loop(0, chunks)
    def _(r):
        at = chunk_blocks(r, some)
        projected = dot(k.attended[at].reshape(chunk_rows, width), k.w_out[...]) + k.out_bias[...]
        hidden = k.tok[r].astype(jnp.float32) + projected
        k.hidden[r] = hidden
        unit, _ = norm_parts(hidden)
        normed = (unit * k.gain_two[...] + k.shift_two[...]).astype(jnp.bfloat16)
        k.normed_two[r] = normed
        total = hidden + k.back_bias[...]
        for c in range(parts):
            pre = dot(normed, k.w_in[c].reshape(width, units)) + k.in_bias[c, 0:1, :]
            cdf = 0.5 + 0.5 * lax.erf(pre * 0.5**0.5)
            active = (pre * cdf).astype(jnp.bfloat16)
            slope = cdf + pre * (jnp.exp(pre * pre * -0.5) * 0.3989422804014327)
            k.active[c, at] = active.reshape(some, BLOCK, units)
            k.slope[c, r] = slope.astype(jnp.bfloat16)
            total = total + dot(active, k.w_back[c].reshape(units, width))
        k.stage[r] = total.astype(jnp.bfloat16)
        k.grad_normed[r] = jnp.zeros((chunk_rows, width), jnp.float32)


def feed_back(k, c):
    chunks, chunk_rows, width = k.tok.shape
    units = k.active.shape[3]
    w_in = k.w_in.at[c]
    w_back = k.w_back.at[c]

    def rows(r, in_bias_sum):
        grad = dot_right_t(k.cot[r], w_back[...].reshape(units, width))
        grad = grad * k.slope[c, r].astype(jnp.float32)
        low = grad.astype(jnp.bfloat16)
        k.slope[c, r] = low
        k.grad_normed[r] += dot_right_t(low, w_in[...].reshape(width, units))
        return in_bias_sum + row_sum(grad)

    total = jnp.zeros((1, units), jnp.float32)
    total = lax.fori_loop(0, chunks, rows, total, unroll=UNROLL)
    k.sums[pl.ds(8 + c, 1), :] = total
    grads = k.slope[c].reshape(-1, units)
    k.ff_in[c] = as_pack(dot_left_t(whole_rows(k.normed_two), grads), k.ff_in.shape[1:])
    active = k.active[c].reshape(-1, units)
    k.ff_back[c] = as_pack(dot_left_t(active, whole_rows(k.cot)), k.ff_back.shape[1:])


def second_norm_back(k):
    chunks, chunk_rows, width = k.tok.shape
    some = chunk_rows // BLOCK

    def rows(r, sums):
        out_grad = k.cot[r].astype(jnp.float32)
        grad_normed = k.grad_normed[r]
        unit, inverse = norm_parts(k.hidden[r])
        grad_hidden = out_grad + norm_grad(grad_normed, unit, inverse, k.gain_two[...])
        k.hidden[r] = grad_hidden
        low = grad_hidden.astype(jnp.bfloat16)
        k.normed_two[r] = low
        grad_attended = dot_right_t(low, k.w_out[...]).astype(jnp.bfloat16)
        k.grad_attended[chunk_blocks(r, some)] = grad_attended.reshape(some, BLOCK, width)
        terms = (grad_normed * unit, grad_normed, out_grad, grad_hidden)
        return tuple(total + row_sum(term) for total, term in zip(sums, terms))

    zero = jnp.zeros((1, width), jnp.float32)
    sums = lax.fori_loop(0, chunks, rows, (zero,) * 4, unroll=UNROLL)
    for at, total in enumerate(sums):
        k.sums[at : at + 1, :] = total


def out_weights(k):
    grad = dot_left_t(whole_rows(k.attended), whole_rows(k.normed_two))
    for half in range(2):
        put_matrix(k.output, half, grad[:, half * GROUP_LANES : (half + 1) * GROUP_LANES])


def whole_rows(ref):
    return ref[...].reshape(-1, ref.shape[-1])


def as_pack(array, shape):
    return array.astype(jnp.bfloat16).reshape(shape)


def norm_grad(grad_out, unit, inverse, gain):
    scaled = grad_out * gain
    first = jnp.mean(scaled, axis=-1, keepdims=True)
    second = jnp.mean(scaled * unit, axis=-1, keepdims=True)
    return inverse * (scaled - first - unit * second)


def put_matrix(pack, at, matrix):
    shape = pack.shape[:4] + pack.shape[5:]
    pack[:, :, :, :, at] = as_pack(matrix, shape)


def attend_back(k, group, first, last):
    width = k.tok.shape[2]
    head_size = width // HEADS
    lanes = head_lanes(head_size)
    scale = head_size ** (-0.5)

    @pl.loop(first, last, unroll=UNROLL)
    def _(i):
        lane = group * GROUP_LANES
        queries, keys, values = block_parts(k, i, lane)
        queries = spread_heads(queries, lanes, scale)
        grad_out = spread_heads(k.grad_attended[i, :, pl.ds(lane, GROUP_LANES)], lanes)
        weights = k.weights[i, group]
        grad_weights = dot_right_t(values, grad_out)
        grad_values = dot(weights.astype(jnp.bfloat16), grad_out)
        inner = row_sum(grad_weights * weights)
        grad_scores = (weights * (grad_weights - inner)).astype(jnp.bfloat16)
        grad_queries = fold_heads(dot_left_t(grad_scores, keys), lanes) * scale
        grad_keys = dot(grad_scores, queries)
        place = pl.ds(lane, GROUP_LANES)
        k.mixed[i, :, place] = grad_queries.astype(jnp.bfloat16)
        k.sorted[i, :, place] = grad_keys[:BLOCK].astype(jnp.bfloat16)
        k.sorted[i, :, pl.ds(width + lane, GROUP_LANES)] = grad_values[:BLOCK].astype(
            jnp.bfloat16
        )
        k.weights[i, group] = jnp.concatenate([grad_keys[BLOCK:], grad_values[BLOCK:]], axis=0)


def mix_back(k, group):
    width = k.tok.shape[2]

    def write(row, rows, lane, mixed):
        half = lane // width
        own = k.weights[:, group, pl.ds(half * BLOCK + row, rows), :]
        k.active[half, :, pl.ds(row, rows), pl.ds(lane % width, GROUP_LANES)] = (
            own + mixed
        ).astype(jnp.bfloat16)

    mix_blocks(k, k.plan_tall, k.sorted, 0, (group,), write)


def plan_grad(k, group):
    width = k.tok.shape[2]
    blocks = k.mixed.shape[0]
    side = GROUP_LANES
    part = side // blocks
    lanes = head_lanes(width // HEADS)
    in_group = len(lanes)

    same = (
        lax.broadcasted_iota(jnp.int32, (side, side), 0) % part
        == lax.broadcasted_iota(jnp.int32, (side, side), 1) % part
    )
    fold_columns = (
        lax.broadcasted_iota(jnp.int32, (side, blocks), 0) // part
        == lax.broadcasted_iota(jnp.int32, (side, blocks), 1)
    ).astype(jnp.float32)
    total = jnp.zeros((in_group * side, side), jnp.float32)
    for c in range(BLOCK // part):
        at = pl.ds(c * part, part)
        lane = group * side
        grads, rows = (
            [
                ref[:, at, pl.ds(offset + lane, side)].reshape(side, side)
                for offset in (start_lane, start_lane + width)
            ]
            for ref, start_lane in ((k.sorted, 0), (k.mixed, width))
        )
        grads = jnp.concatenate([spread_heads(grad, lanes) for grad in grads], axis=1)
        total = total + dot_right_t(grads, jnp.concatenate(rows, axis=1))
    for h in range(in_group):
        picked = jnp.where(same, total[h * side : (h + 1) * side], 0.0)
        picked = jnp.sum(picked.reshape(blocks, part, side), axis=1)
        k.grad_plan[:, group * in_group + h, :] = dot(picked, fold_columns, precision=HIGH)


def plan_back(k):
    width = k.tok.shape[2]
    head_size = width // HEADS
    blocks = k.mixed.shape[0]
    grad = k.grad_plan[...] * jnp.exp(k.log_plans[2 * ITERS - 1])

    def sweep(t, grad):
        for half, axis in ((1, 0), (0, 2)):
            share = jnp.exp(k.log_plans[2 * (ITERS - 1 - t) + half])
            grad = grad - share * jnp.sum(grad, axis=axis, keepdims=True)
        return grad

    grad = lax.fori_loop(0, ITERS, sweep, grad)
    grad = jnp.where(k.allowed[...] > 0.5, grad / TEMPER, 0.0) * head_size ** (-0.5)
    grad = grad.reshape(blocks * HEADS, blocks)
    sort_q = k.sort_q[...]
    sort_k = k.sort_k[...]
    shape = (blocks, HEADS, width)
    mine = lax.broadcasted_iota(jnp.int32, shape, 1) == (
        lax.broadcasted_iota(jnp.int32, shape, 2) // head_size
    )
    grad_sq = dot(grad, sort_k, precision=HIGH).reshape(shape)
    grad_sq = jnp.sum(jnp.where(mine, grad_sq, 0.0), axis=1)
    grad_sk = dot_left_t(grad, head_rows(sort_q, head_size), HIGH)
    k.factors[k.place + (0,)] = grad_sq.astype(jnp.bfloat16)
    k.factors[k.place + (1,)] = grad_sk.astype(jnp.bfloat16)
    grad_summary = dot_right_t(grad_sq, k.sort_query[...].astype(jnp.float32), HIGH)
    grad_summary += dot_right_t(grad_sk, k.sort_key[...].astype(jnp.float32), HIGH)
    some = k.means.shape[1]
    k.means[...] = (grad_summary / BLOCK).reshape(blocks // some, some, width)


def first_weights(k, group, pack):
    rows = whole_rows(k.normed_low)
    lanes = pl.ds(group * GROUP_LANES, GROUP_LANES)
    grads = (k.mixed[:, :, lanes], k.active[0, :, :, lanes], k.active[1, :, :, lanes])
    for at, grad in enumerate(grads):
        put_matrix(pack, at, dot_left_t(rows, grad.reshape(-1, GROUP_LANES)))


def first_norm_back(k, order, between):
    chunks, chunk_rows, width = k.tok.shape
    some = chunk_rows // BLOCK
    sums = (jnp.zeros((1, width), jnp.float32),) * 2
    for t in range(chunks):
        r = order(t)
        at = chunk_blocks(r, some)
        grads = (k.mixed[at, :, pl.ds(0, width)], k.active[0, at], k.active[1, at])
        grad_mixed = jnp.concatenate([grad.reshape(chunk_rows, width) for grad in grads], axis=1)
        spread = jnp.broadcast_to(k.means[r][:, None, :], (some, BLOCK, width))
        grad_normed = dot_right_t(grad_mixed, k.w_qkv[...]) + spread.reshape(chunk_rows, width)
        unit, inverse = norm_parts(k.tok[r].astype(jnp.float32))
        grad = k.hidden[r] + norm_grad(grad_normed, unit, inverse, k.gain_one[...])
        k.stage[r] = grad.astype(jnp.bfloat16)
        terms = (grad_normed * unit, grad_normed)
        sums = tuple(total + row_sum(term) for total, term in zip(sums, terms))
        between[t]()
    for at, total in enumerate(sums, 4):
        k.sums[at : at + 1, :] = total


def flip(index, bit):
    return index + bit - 2 * bit * ((index // bit) % 2)


def flip_both(index, step):
    low, high = index % 2, index // 2
    low_step, high_step = step % 2, step // 2
    return (low + low_step - 2 * low * low_step) + 2 * (
        high + high_step - 2 * high * high_step
    )


class Links:
    def __init__(self, k):
        self.k = k
        self.used = 0
        self.used_here = 0

    def take(self, count):
        self.used += count
        return self.used - count

    def copy(self, at, source, target, peer):
        return pltpu.make_async_remote_copy(
            src_ref=source,
            dst_ref=target,
            send_sem=self.k.send.at[at],
            recv_sem=self.k.recv.at[at],
            device_id=peer,
            device_id_type=pl.DeviceIdType.MESH,
        )

    def here(self, source, target):
        self.used_here += 1
        return pltpu.make_async_copy(source, target, self.k.local.at[self.used_here - 1])


def start(copies):
    for copy in copies:
        copy.start()


def wait(copies):
    for copy in copies:
        copy.wait()


class Exchange:
    def __init__(self):
        self.under_way = []
        self.steps = []

    def then(self, copies, work=None):
        self.steps.append((copies, work))

    def step(self):
        copies, work = self.steps.pop(0)
        wait(self.under_way)
        if work is not None:
            work()
        start(copies)
        self.under_way = copies

    def finish(self):
        while self.steps:
            self.step()
        wait(self.under_way)


def add_to(pack, place, land):
    @pl.loop(0, pack.shape[0])
    def _(part):
        at = (part,) + place
        pack[at] = pack[at] + land[part]


def sum_of(pieces):
    total = pieces[0].astype(jnp.float32)
    for piece in pieces[1:]:
        total = total + piece.astype(jnp.float32)
    return total.astype(jnp.bfloat16)


def own_parts(links, pack, lands, out, places, across, z):
    (c, to_c), (a, to_a), (b, to_b) = places
    fresh = lambda source, target, to: links.copy(links.take(1), source, target, to)
    parts = pack.shape[0]
    first, second = links.take(parts), links.take(parts)
    core_part = lambda part, t: links.copy(
        first + t, pack.at[part, 1 - c], lands[0].at[part], to_c
    )
    next_part = lambda part, t: links.copy(
        second + t, pack.at[part, c, 1 - a], lands[1].at[part], to_a
    )

    def go_on(part, t):
        core_part(part, t).wait()
        pack[part, c] = pack[part, c] + lands[0][part]
        next_part(part, t).start()

    steps = Exchange()
    steps.under_way = [next_part(flip_both(z, t), t) for t in range(parts)]
    steps.then(
        [fresh(pack.at[:, c, a, 1 - b], lands[2], to_b)], lambda: add_to(pack, (c, a), lands[1])
    )
    low, high = z % 2, z // 2
    to_near, to_middle, _ = across
    steps.then(
        [
            fresh(pack.at[1 - low + 2 * half, c, a, b], lands[3].at[half], to_near)
            for half in range(2)
        ],
        lambda: add_to(pack, (c, a, b), lands[2]),
    )

    def add_near():
        for half in range(2):
            at = (low + 2 * half, c, a, b)
            pack[at] = pack[at] + lands[3][half]

    far_part = pack.at[low + 2 * (1 - high), c, a, b]
    steps.then([fresh(far_part, lands[3].at[2], to_middle)], add_near)

    def total():
        out[0, c, a, b] = sum_of([pack[z, c, a, b], lands[3][2]])

    steps.then([fresh(out.at[:, c, a, b], out.at[:, c, a, b], to_b)], total)
    steps.then([fresh(out.at[:, c, a], out.at[:, c, a], to_a)])
    steps.then([fresh(out.at[:, c], out.at[:, c], to_c)])
    return (steps, lambda part, t: core_part(part, t).start(), go_on)


def all_parts(links, pack, lands, out, place, plane, to_core, across):
    z, core, x, y = place
    fresh = lambda source, target, to: links.copy(links.take(1), source, target, to)
    steps = Exchange()
    steps.then([fresh(pack.at[:, 1 - core], lands[0], to_core)])
    steps.then(
        [
            fresh(pack.at[:, core, at_x, at_y], lands[1].at[t], to)
            for t, (at_x, at_y, to) in enumerate(plane)
        ],
        lambda: add_to(pack, (core,), lands[0]),
    )

    def add_plane():
        @pl.loop(0, pack.shape[0])
        def _(part):
            at = (part, core, x, y)
            pack[at] = sum_of([pack[at]] + [lands[1][t, part] for t in range(len(plane))])

    steps.then(
        [
            fresh(pack.at[peer["mp"], core, x, y], lands[2].at[t], peer)
            for t, peer in enumerate(across)
        ],
        add_plane,
    )

    def total():
        pieces = [lands[2][t] for t in range(len(across))]
        out[place] = sum_of([pack[place]] + pieces)

    spread_out(links, steps, out, place, plane, to_core, across, total)
    return steps


def spread_out(links, steps, array, place, plane, to_core, across, work=None):
    z, core, x, y = place
    fresh = lambda ref, to: links.copy(links.take(1), ref, ref, to)
    steps.then([fresh(array.at[place], peer) for peer in across], work)
    steps.then([fresh(array.at[:, core, x, y], to) for _, _, to in plane])
    steps.then([fresh(array.at[:, core], to_core)])


def layer_kernel(names, *refs):
    k = SimpleNamespace(**dict(zip(names, refs)))
    p = lax.axis_index("dp")
    z = lax.axis_index("mp")
    core, x, y = p % 2, (p // 2) % 2, p // 4
    k.z = z
    k.place = (z, core, x, y)
    to_core, to_x, to_y, to_far = (
        {"dp": other} for other in (flip(p, 1), flip(p, 2), flip(p, 4), flip(flip(p, 2), 4))
    )
    across = [{"mp": flip_both(z, t)} for t in (1, 2, 3)]
    plane = ((1 - x, y, to_x), (x, 1 - y, to_y), (1 - x, 1 - y, to_far))
    parts = k.w_in.shape[0]

    barrier = pltpu.get_barrier_semaphore()
    for peer in [to_core, to_x, to_y, to_far] + across:
        pl.semaphore_signal(barrier, inc=1, device_id=peer, device_id_type=pl.DeviceIdType.MESH)
    links = Links(k)
    fresh = lambda source, target, to: links.copy(links.take(1), source, target, to)
    here = [
        links.here(source, target)
        for source, target in (
            (k.w_qkv_in, k.w_qkv),
            (k.sort_query_in, k.sort_query),
            (k.sort_key_in, k.sort_key),
            (k.w_out_in, k.w_out),
            (k.w_in_in, k.w_in.at[z]),
            (k.w_back_in, k.w_back.at[z]),
        )
    ]
    start(here)
    lay_out_small(k)
    pl.semaphore_wait(barrier, 7)

    def to_sequences(source, target):
        copies = [links.here(source.at[z], target.at[z])]
        copies += [fresh(source.at[peer["mp"]], target.at[z], peer) for peer in across]
        start(copies)
        return copies

    def weight_part(peer):
        m = peer["mp"]
        same = lambda ref, to: fresh(ref, ref, to)
        steps = Exchange()
        steps.then(
            [
                fresh(k.w_in_in.at[core, x, y], k.w_in.at[z, core, x, y], peer),
                fresh(k.w_back_in.at[core, y, x], k.w_back.at[z, core, y, x], peer),
            ]
        )
        steps.then(
            [same(k.w_in.at[m, core, x, y], to_x), same(k.w_back.at[m, core, y, x], to_y)]
        )
        steps.then(
            [same(k.w_in.at[m, core, :, y], to_y), same(k.w_back.at[m, core, :, x], to_x)]
        )
        steps.then([same(k.w_in.at[m, core], to_core), same(k.w_back.at[m, core], to_core)])
        return steps

    near, middle, far = (weight_part(peer) for peer in across)
    near.step()
    middle.step()
    far.step()
    tokens = to_sequences(k.tok_in, k.tok)
    segments = to_sequences(k.seg_stage, k.seg)
    biases = [fresh(k.in_bias_stage, k.in_bias.at[z], peer) for peer in across]
    start(biases)
    k.in_bias[z] = k.in_bias_stage[...]
    k.sums[...] = jnp.zeros_like(k.sums)
    wait(here[:1] + tokens[:1])
    first_norm(k, z)
    near.step()
    for t, steps in ((1, (near, middle, far)), (2, (near, middle, far)), (3, (middle, far))):
        tokens[t].wait()
        first_norm(k, flip_both(z, t))
        if t < 3:
            for each in steps:
                each.step()
    summarize(k)
    summaries = Exchange()
    spread_out(links, summaries, k.summary_all, k.place, plane, to_core, across)
    summaries.step()
    cotangents = to_sequences(k.cot_in, k.cot)
    middle.step()
    far.step()
    wait(here[1:3])
    sort_plan(k)
    sort_forward(k)
    summaries.step()
    wait(segments)
    attend(k)
    summaries.step()
    wait(here[3:] + biases)
    for each in (near, middle, far):
        each.finish()
    feed_forward(k)

    def to_positions(target):
        copies = [fresh(k.stage.at[peer["mp"]], target.at[z], peer) for peer in across]
        return copies + [links.here(k.stage.at[z], target.at[z])]

    outs = to_positions(k.out_land)

    wait(cotangents)
    start(outs)

    def lands(name, levels):
        return [getattr(k, name + "_land" + str(level)) for level in range(levels)]

    order_x = ((core, to_core), (x, to_x), (y, to_y))
    order_y = ((core, to_core), (y, to_y), (x, to_x))
    ff_in, ff_in_start, ff_in_on = own_parts(
        links, k.ff_in, lands("ff_in", 4), k.ff_in_out, order_x, across, z
    )
    ff_back, ff_back_start, ff_back_on = own_parts(
        links, k.ff_back, lands("ff_back", 4), k.ff_back_out, order_y, across, z
    )
    output, first, second = (
        all_parts(
            links,
            getattr(k, name),
            lands(name, 3),
            getattr(k, name + "_out"),
            k.place,
            plane,
            to_core,
            across,
        )
        for name in ("output", "first", "second")
    )
    factors = Exchange()
    spread_out(links, factors, k.factors, k.place, plane, to_core, across)

    @pl.loop(0, parts)
    def _(t):
        c = flip_both(z, t)
        feed_back(k, c)
        ff_in_start(c, t)
        ff_back_start(c, t)

        @pl.when(t > 0)
        def _():
            before = flip_both(z, t - 1)
            ff_in_on(before, t - 1)
            ff_back_on(before, t - 1)

    second_norm_back(k)
    last = flip_both(z, parts - 1)
    ff_in_on(last, parts - 1)
    ff_back_on(last, parts - 1)
    sums = Exchange()
    lands = k.sums_land

    def add_core():
        k.sums[...] += lands[0]

    def add_plane():
        k.sums[...] = (k.sums[...] + lands[1]) + (lands[2] + lands[3])

    sums.then([fresh(k.sums, lands.at[0], to_core)])
    sums.then([fresh(k.sums, lands.at[1 + t], to) for t, (_, _, to) in enumerate(plane)], add_core)
    sums.then([fresh(k.sums, lands.at[4 + t], peer) for t, peer in enumerate(across)], add_plane)

    def step(*exchanges):
        for each in exchanges:
            each.step()

    blocks = k.mixed.shape[0]
    out_weights(k)
    step(output)
    attend_back(k, 0, 0, blocks // 2)
    step(ff_in, ff_back, output)
    attend_back(k, 0, blocks // 2, blocks)
    mix_back(k, 0)
    first_weights(k, 0, k.first)
    step(first)
    attend_back(k, 1, 0, blocks // 2)
    step(ff_in, ff_back, first)
    attend_back(k, 1, blocks // 2, blocks)
    step(output, ff_in, ff_back)
    mix_back(k, 1)
    first_weights(k, 1, k.second)
    step(second, first)
    plan_grad(k, 0)
    step(output, ff_in, ff_back)
    plan_grad(k, 1)
    step(second, first)
    plan_back(k)
    step(factors, second, output, ff_in, ff_back)
    wait(outs)
    outs = to_positions(k.tokens_land)
    nothing = lambda: None
    first_norm_back(
        k,
        lambda t: flip_both(z, (t + 1) % parts),
        (nothing, lambda: (outs[1].start(), step(first)), nothing, lambda: step(output, ff_in, ff_back)),
    )
    step(sums, second)
    start([outs[0]] + outs[2:])
    step(factors, first, sums, second, factors, sums, second)
    for each in (summaries, output, factors, first, ff_in, ff_back, second, sums):
        each.finish()
    total = (k.sums[...] + lands[4]) + (lands[5] + lands[6])
    lands[0] = total
    k.vectors[...] = total
    k.vectors[6:7, :] = lands[0, pl.ds(8 + z, 1), :]
    wait(outs)
    assert links.used == COPIES and links.used_here == LOCAL_COPIES


def lay_out_small(k):
    sequences, positions = k.seg_in.shape
    k.seg_stage[...] = jnp.zeros_like(k.seg_stage)
    for s in range(sequences):
        ids = k.seg_in[s : s + 1, :].astype(jnp.float32)
        for at in range(positions // BLOCK):
            row = ids[:, at * BLOCK : (at + 1) * BLOCK]
            k.seg_stage[s, at : at + 1, :] = jnp.concatenate([row, row], axis=1)
    k.in_bias_stage[...] = jnp.broadcast_to(k.in_bias_in[...], k.in_bias_stage.shape)


FAR = (
    "tok_in",
    "cot_in",
    "w_qkv_in",
    "w_out_in",
    "sort_query_in",
    "sort_key_in",
    "w_in_in",
    "w_back_in",
)
NEAR = (
    "seg_in",
    "in_bias_in",
    "mask",
    "gain_one",
    "shift_one",
    "out_bias",
    "gain_two",
    "shift_two",
    "back_bias",
)


def buffers_of(parts, chunk_rows, width, units):
    blocks = parts * chunk_rows // BLOCK
    groups = width // GROUP_LANES
    stacked = GROUP_LANES // (width // HEADS) * BLOCK
    rows = (parts, chunk_rows, width)
    in_blocks = (blocks, BLOCK, width)
    small = (blocks, HEADS, blocks)
    plans = (groups, GROUP_LANES, HEADS // groups * GROUP_LANES)
    low, full = jnp.bfloat16, jnp.float32
    ff_in = (1, width // 8, units)
    ff_back = (1, units // 8, width)
    rows_of = width // (8 * parts)
    pieces = dict(
        ff_in=ff_in,
        ff_back=ff_back,
        output=(2, rows_of, GROUP_LANES),
        first=(3, rows_of, GROUP_LANES),
        second=(3, rows_of, GROUP_LANES),
    )
    everywhere = (parts, 2, 2, 2)
    far = dict(out_land=(rows, low), tokens_land=(rows, low))
    near = dict(
        vectors=((16, width), full),
        summary_all=(everywhere + (blocks, width), low),
        factors=(everywhere + (2, blocks, width), low),
    )
    for name, piece in pieces.items():
        whole = 1 if name.startswith("ff") else parts
        near[name + "_out"] = ((whole, 2, 2, 2) + piece, low)
    scratch = dict(
        tok=(rows, low),
        cot=(rows, low),
        seg=((parts, 8, 2 * BLOCK), full),
        seg_stage=((parts, 8, 2 * BLOCK), full),
        in_bias_stage=((8, units), full),
        w_qkv=((width, 3 * width), low),
        w_out=((width, width), low),
        sort_query=((width, width), low),
        sort_key=((width, width), low),
        w_in=((parts, 2, 2, 2, width // 8, units), low),
        w_back=((parts, 2, 2, 2, units // 8, width), low),
        in_bias=((parts, 8, units), full),
        means=((parts, chunk_rows // BLOCK, width), full),
        normed_low=(rows, low),
        mixed=((blocks, BLOCK, 3 * width), low),
        sort_q=((blocks, width), full),
        sort_k=((blocks, width), full),
        allowed=(small, full),
        log_plans=((2 * ITERS,) + small, full),
        grad_plan=(small, full),
        plan_wide=(plans, low),
        plan_tall=(plans, low),
        sorted=((blocks, BLOCK, 2 * width), low),
        weights=((blocks, groups, 2 * BLOCK, stacked), full),
        attended=(in_blocks, low),
        hidden=(rows, full),
        normed_two=(rows, low),
        active=((parts, blocks, BLOCK, units), low),
        slope=((parts, parts, chunk_rows, units), low),
        grad_normed=(rows, full),
        grad_attended=(in_blocks, low),
        stage=(rows, low),
        sums=((16, width), full),
        sums_land=((7, 16, width), full),
    )
    for name, piece in pieces.items():
        scratch[name] = (everywhere + piece, low)
        scratch[name + "_land0"] = ((parts, 2, 2) + piece, low)
    for name in ("ff_in", "ff_back"):
        scratch[name + "_land1"] = ((parts, 2) + pieces[name], low)
        scratch[name + "_land2"] = ((parts,) + pieces[name], low)
        scratch[name + "_land3"] = ((parts - 1,) + pieces[name], low)
    for name in ("output", "first", "second"):
        scratch[name + "_land1"] = ((3, parts) + pieces[name], low)
        scratch[name + "_land2"] = ((parts - 1,) + pieces[name], low)
    return (far, near, scratch)


def layer_call(inputs):
    parts, chunk_rows, width = inputs["tok_in"].shape
    units = inputs["w_in_in"].shape[-1]
    far, near, scratch = buffers_of(parts, chunk_rows, width, units)
    outs = far | near
    in_vmem = pl.BlockSpec(memory_space=pltpu.VMEM)
    anywhere = pl.BlockSpec(memory_space=pl.ANY)
    results = pl.pallas_call(
        partial(layer_kernel, FAR + NEAR + tuple(outs) + tuple(scratch) + ("send", "recv", "local")),
        out_shape=[jax.ShapeDtypeStruct(*entry) for entry in outs.values()],
        in_specs=[anywhere] * len(FAR) + [in_vmem] * len(NEAR),
        out_specs=[anywhere] * len(far) + [in_vmem] * len(near),
        scratch_shapes=[pltpu.VMEM(*entry) for entry in scratch.values()]
        + [
            pltpu.SemaphoreType.DMA((COPIES,)),
            pltpu.SemaphoreType.DMA((COPIES,)),
            pltpu.SemaphoreType.DMA((LOCAL_COPIES,)),
        ],
        compiler_params=pltpu.CompilerParams(
            collective_id=0, has_side_effects=True, vmem_limit_bytes=VMEM_BYTES
        ),
        name="layer",
    )(*[inputs[name] for name in FAR + NEAR])
    return dict(zip(outs, results))


def widen_kernel(
    out, tokens, output, first, second, summary, factors, ff_in, ff_back, vectors, *results
):
    wide = lambda array: array.astype(jnp.float32)
    layer_out, grad_tokens, grad_qkv, grad_w_out, grad_sq, grad_sk, grad_w_in, grad_w_back = results[:8]
    layer_out[...] = wide(out[...])
    grad_tokens[...] = wide(tokens[...])
    lanes = first.shape[-1]
    width = grad_w_out.shape[1]
    half = lambda pack, at: wide(pack[0, :, :, :, at]).reshape(-1, lanes)
    for at in range(2):
        grad_w_out[:, at * lanes : (at + 1) * lanes] = half(output, at)
    for part in range(3):
        for at, (pack, place) in enumerate(((first, part), (second, part))):
            place_at = part * width + at * lanes
            grad_qkv[:, place_at : place_at + lanes] = half(pack, place)
    rows = grad_sq.shape[0]
    columns = pl.ds(pl.multiple_of(pl.program_id(0) * rows, rows), rows)
    left = summary[:, columns]
    for at, result in enumerate((grad_sq, grad_sk)):
        result[...] = dot_left_t(left, factors[:, at].reshape(-1, width))
    grad_w_in[...] = wide(ff_in[...])
    grad_w_back[...] = wide(ff_back[...])
    for at, result in enumerate(results[8:]):
        result[...] = vectors[at : at + 1, :]


def widen_call(results):
    parts, chunk_rows, width = results["out_land"].shape
    units = results["ff_in_out"].shape[-1]
    square = (width, width)
    blocks = results["factors"].shape[-2]
    gathered = (5, 6, 9)
    ins = [
        results["out_land"],
        results["tokens_land"],
        results["output_out"],
        results["first_out"],
        results["second_out"],
        results["summary_all"].reshape(-1, width),
        results["factors"].reshape(-1, 2, blocks, width),
        results["ff_in_out"].reshape(width, units),
        results["ff_back_out"].reshape(units, width),
        results["vectors"],
    ]
    shapes = [ins[0].shape, ins[1].shape, (width, 3 * width), square, square, square]
    shapes += [(width, units), (units, width)] + [(1, width)] * 6 + [(1, units)]

    def part_of(shape):
        if shape[0] < parts:
            return pl.BlockSpec(shape, lambda i: (0,) * len(shape))
        return pl.BlockSpec(
            (shape[0] // parts,) + shape[1:], lambda i: (i,) + (0,) * (len(shape) - 1)
        )

    return pl.pallas_call(
        widen_kernel,
        grid=(parts,),
        out_shape=[jax.ShapeDtypeStruct(shape, jnp.float32) for shape in shapes],
        in_specs=[
            pl.BlockSpec(memory_space=pltpu.VMEM) if at in gathered else part_of(array.shape)
            for at, array in enumerate(ins)
        ],
        out_specs=[part_of(shape) for shape in shapes],
        compiler_params=pltpu.CompilerParams(vmem_limit_bytes=VMEM_BYTES),
        name="widen",
    )(*ins)


def per_sequence(
    tokens,
    segment_ids,
    block_mask,
    gain_one,
    shift_one,
    w_qkv,
    w_out,
    out_bias,
    sort_query,
    sort_key,
    gain_two,
    shift_two,
    input_weight,
    in_bias,
    output_weight,
    back_bias,
    cotangent,
):
    parts, chunk_rows, width = tokens.shape
    units = input_weight.shape[1]
    row = lambda vector: vector.reshape(1, -1)
    results = layer_call(
        dict(
            tok_in=tokens,
            cot_in=cotangent,
            seg_in=segment_ids,
            w_qkv_in=w_qkv,
            w_out_in=w_out,
            sort_query_in=sort_query,
            sort_key_in=sort_key,
            w_in_in=input_weight.reshape(2, 2, 2, width // 8, units),
            w_back_in=output_weight.reshape(2, 2, 2, units // 8, width),
            in_bias_in=row(in_bias.astype(jnp.float32)),
            mask=block_mask,
            gain_one=row(gain_one),
            shift_one=row(shift_one),
            out_bias=row(out_bias),
            gain_two=row(gain_two),
            shift_two=row(shift_two),
            back_bias=row(back_bias),
        )
    )
    wide = widen_call(results)
    flat = [array.reshape(-1) for array in wide[8:]]
    gain_two, shift_two, back_bias, out_bias, gain_one, shift_one, in_bias = flat
    layer_out, grad_tokens, grad_qkv, grad_w_out, grad_sq, grad_sk, grad_w_in, grad_w_back = wide[:8]
    return (
        layer_out,
        grad_tokens,
        gain_one,
        shift_one,
        grad_qkv,
        grad_w_out,
        out_bias,
        grad_sq,
        grad_sk,
        gain_two,
        shift_two,
        grad_w_in,
        in_bias,
        grad_w_back,
        back_bias,
    )


def solution(mesh):
    in_specs = (
        P("dp", "mp", None),
        P("dp", "mp"),
        P("dp", None, None),
        P(),
        P(),
        P(),
        P(),
        P(),
        P(),
        P(),
        P(),
        P(),
        P(None, "mp"),
        P("mp"),
        P("mp", None),
        P(),
        P("dp", "mp", None),
    )
    out_specs = (
        P("dp", "mp", None),
        P("dp", "mp", None),
        P(),
        P(),
        P(),
        P(),
        P(),
        P(),
        P(),
        P(),
        P(),
        P(None, "mp"),
        P("mp"),
        P("mp", None),
        P(),
    )

    def per_shard(tokens, *others):
        sizes = (mesh.shape["dp"], mesh.shape["mp"])
        sequences, positions, width = tokens.shape
        whole = sizes == (8, 4) and sequences == 4
        whole = whole and (positions, width) == (256, 512)
        whole = whole and others[11].shape[1] == width
        return (per_sequence if whole else per_device)(tokens, *others)

    return jax.shard_map(
        per_shard, mesh=mesh, in_specs=in_specs, out_specs=out_specs, check_vma=False
    )
```
